32 devices in a mesh: dp: 8 (over z, y), group: 4 (over x, core).
Axes of the slice: x: 2, y: 2, z: 4, core: 2. Of those that a mesh axis runs over, the one named last changes fastest.
Arguments:
- inputs: bfloat16 [768, 65536], P('group', 'dp'), may hold values from -6 to 6
- labels: int32 [128, 512], P('dp'), may hold values from 0 to 3, never falling along the last dimension, each value on 1 to 256 neighbouring positions
- w_qkv: float32 [4, 192, 576], P('group', 'dp'), may hold values from -0.4375 to 0.4375
- b_qv: float32 [4, 384], P('group'), may hold values from -4 to 4
- w_out: float32 [768, 768], P('dp', 'group'), may hold values from -1.75 to 1.75
- b_out: float32 [768], P('group'), may hold values from -4 to 4
- gain_one: float32 [768], P('group'), may hold values from 0.25 to 1.75
- shift_one: float32 [768], P('group'), may hold values from -4 to 4
- w_up: float32 [4, 192, 768], P('group', 'dp'), may hold values from -0.4375 to 0.4375
- b_up: float32 [4, 768], P('group'), may hold values from -6 to 6
- down_weight: float32 [4, 768, 192], P('group', 'dp'), may hold values from -0.21875 to 0.21875
- down_bias: float32 [4, 192], P('group'), may hold values from -4 to 4
- gain_two: float32 [768], P('group'), may hold values from 0.25 to 1.75
- shift_two: float32 [768], P('group'), may hold values from -4 to 4
- grad_out: bfloat16 [768, 65536], P('group', 'dp'), may hold values from -9 to 9
Outputs:
- result: bfloat16 [768, 65536], P('group', 'dp')
- grad_in: float32 [768, 65536], P('group', 'dp')
- grad_w_qkv: float32 [4, 192, 576], P('group', 'dp')
- grad_b_qv: float32 [4, 384], P('group')
- grad_w_out: float32 [768, 768], P('dp', 'group')
- grad_b_out: float32 [768], P('group')
- grad_gain_one: float32 [768], P('group')
- grad_shift_one: float32 [768], P('group')
- grad_w_up: float32 [4, 192, 768], P('group', 'dp')
- grad_b_up: float32 [4, 768], P('group')
- grad_w_down: float32 [4, 768, 192], P('group', 'dp')
- grad_b_down: float32 [4, 192], P('group')
- grad_gain_two: float32 [768], P('group')
- grad_shift_two: float32 [768], P('group')
The draws below stay inside these ranges and needn't reach their ends.
Inputs may be any that keep to these rules, and one draw needn't show every extreme that they name: `labels`: in each packed row the ids never fall from one position to the next; every document has 1 to half of 512 positions, and some document has exactly half of 512.
All inputs are finite; a program needn't handle non-finite values.
Results may differ from the reference program's by a relative error of at most 0.012.
The reference program's roundings to bfloat16 on the way count: a program that leaves them out, or rounds other values in their place, can miss the bound.
Values may be sent and summed in bfloat16 or wider, within the bound.
A program may use at most 256 MiB of HBM per device.

```python
import math
import jax
import jax.numpy as jnp
import numpy as np
from jax import lax

D = 768
HEADS = 12
CONV_GROUPS = 4
SEQ = 512
HD = 64
GW = 192
GF = 768
HG = 3
ROWS = 128
TOKENS = 65536


def draw_grad_out(key, part):
    key = jax.random.fold_in(key, 7)
    ramp = jnp.arange(TOKENS, dtype=jnp.float32) / (TOKENS - 1)
    base = jnp.clip(jax.random.normal(key, (D, TOKENS), jnp.float32), -6.0, 6.0)
    return (base * (0.5 + ramp)[None, :]).astype(jnp.bfloat16)


def spiked(result, rng, source, target, shards_of, factor):
    owner, partner = [(jnp.arange(result.shape[position]) // (result.shape[position] // shards_of)).reshape([-1 if axis == position else 1 for axis in range(result.ndim)]) for position in (source, target)]
    chosen = jax.random.permutation(rng, shards_of)[partner]
    strong = (owner == chosen) | (owner == (partner + shards_of // 2) % shards_of)
    return jnp.where(strong, factor * result, result)


def level_of(stream_key, shape, cuts, least, top_value):
    factor_of = 1.0
    for axis_at, blocks in cuts:
        draws = jax.random.uniform(jax.random.fold_in(jax.random.fold_in(stream_key, 6), axis_at), (blocks,), jnp.float32, least / len(cuts), top_value / len(cuts))
        factor_of = factor_of * jnp.repeat(jnp.exp(draws), shape[axis_at] // blocks).reshape((-1,) + (1,) * (len(shape) - 1 - axis_at))
    return factor_of


def split_up(amount, total, limit, slope):
    weights = [(1 << 20) // math.isqrt(rank ** slope) + 1 for rank in range(2, amount + 1)]
    surplus, holding = total - limit - (amount - 1), [1] * (amount - 1)
    while surplus > 0:
        free = [i for i in range(amount - 1) if holding[i] < limit]
        pool, left = sum([weights[i] for i in free]), surplus
        for i in free:
            addition = min(limit - holding[i], max(1, left * weights[i] // pool), surplus)
            holding[i] = holding[i] + addition
            surplus = surplus - addition
    return np.array([limit] + holding)


def uneven_parts(rng, count, total, bound, skew):
    if count == 2:
        one = jax.random.randint(rng, (), max(1, total - bound), min(bound, total - 1) + 1)
        return jnp.stack([one, total - one])
    lengths = jnp.asarray(split_up(count, total, bound, skew), jnp.int32)
    twos = (count - 1) // 2
    source_of, sink = lengths[1:1 + 2 * twos:2], lengths[2:2 + 2 * twos:2]
    room = jnp.minimum(source_of - 1, bound - sink)
    moved = jax.random.randint(jax.random.fold_in(rng, 1), (twos,), 0, 1 << 20) % (room + 1)
    lengths = lengths.at[1:1 + 2 * twos:2].set(source_of - moved).at[2:2 + 2 * twos:2].set(sink + moved)
    return lengths[jax.random.permutation(jax.random.fold_in(rng, 2), count)]


def bell_draw(own_key, extent, deviation, most, cuts=(), kind=jnp.bfloat16):
    values = deviation * jax.random.normal(own_key, extent, jnp.float32)
    if cuts:
        values = values * level_of(own_key, extent, cuts, -0.22, 0.18)
    return jnp.clip(values, -most, most).astype(kind)


def bell_draw_with(rng, extent, scale, limit, split, heavy, kind=jnp.bfloat16):
    result = scale * jax.random.normal(rng, extent, jnp.float32)
    if split:
        result = result * level_of(rng, extent, split, -0.22, 0.18)
    return jnp.clip(spiked(result, jax.random.fold_in(rng, 3), *heavy), -limit, limit).astype(kind)


def setup_inputs(seed: int = 0) -> dict:
    streams_of = jax.random.split(jax.random.key(seed), 16)
    return {
        "inputs": bell_draw_with(streams_of[0], (D, TOKENS), 1.0, 6.0, ((0, 4), (1, 8)), (1, 0, 8, 2.0)),
        "labels": jax.vmap(lambda own: jnp.searchsorted(jnp.cumsum(uneven_parts(own, 4, SEQ, SEQ // 2, 0)), jnp.arange(SEQ), side="right"))(jax.random.split(streams_of[1], ROWS)).reshape((ROWS, SEQ)).astype(jnp.int32),
        "w_qkv": bell_draw(streams_of[2], (CONV_GROUPS, GW, 3 * GW), GW ** -0.5, 0.4375, ((0, 4), (1, 8)), jnp.float32),
        "b_qv": bell_draw(streams_of[3], (CONV_GROUPS, 2 * GW), 0.3, 4.0, ((0, 4),), jnp.float32),
        "w_out": bell_draw(streams_of[4], (D, D), (D // 64) ** -0.5, 1.75, ((0, 8), (1, 4)), jnp.float32),
        "b_out": bell_draw(streams_of[5], (D,), 0.3, 4.0, ((0, 4),), jnp.float32),
        "gain_one": jnp.clip(1.0 + 0.15 * jax.random.normal(streams_of[6], (D,), jnp.float32), 0.25, 1.75),
        "shift_one": bell_draw(streams_of[7], (D,), 0.3, 4.0, ((0, 4),), jnp.float32),
        "w_up": bell_draw(streams_of[8], (CONV_GROUPS, GW, GF), GW ** -0.5, 0.4375, ((0, 4), (1, 8)), jnp.float32),
        "b_up": bell_draw(streams_of[9], (CONV_GROUPS, GF), 0.5, 6.0, ((0, 4),), jnp.float32),
        "down_weight": bell_draw(streams_of[10], (CONV_GROUPS, GF, GW), GF ** -0.5, 0.21875, ((0, 4), (1, 8)), jnp.float32),
        "down_bias": bell_draw(streams_of[11], (CONV_GROUPS, GW), 0.3, 4.0, ((0, 4),), jnp.float32),
        "gain_two": jnp.clip(1.0 + 0.15 * jax.random.normal(streams_of[12], (D,), jnp.float32), 0.25, 1.75),
        "shift_two": bell_draw(streams_of[13], (D,), 0.3, 4.0, ((0, 4),), jnp.float32),
        "grad_out": draw_grad_out(jax.random.fold_in(streams_of[15], 71), 0),
    }


eps = 1e-12
precision_highest = lax.Precision.HIGHEST

@jax.custom_vjp
def lowered_copy(v):
    return lax.optimization_barrier(v.astype(jnp.bfloat16)).astype(jnp.float32)

@jax.custom_vjp
def low_back(v):
    return v

def low_keep(v):
    return (lowered_copy(v), None)

def low_pass(kept, grad):
    return (grad,)

def back_keep(v):
    return (v, None)

def back_low(kept, grad):
    return (lowered_copy(grad),)
lowered_copy.defvjp(low_keep, low_pass)
low_back.defvjp(back_keep, back_low)

def smooth_gate(values):
    return jax.nn.gelu(values, approximate=False)

def normalize(residual):
    center = lax.optimization_barrier(jnp.mean(residual, axis=-1, keepdims=True))
    offset = residual - center
    spread = lax.optimization_barrier(jnp.mean(offset * offset, axis=-1, keepdims=True))
    return offset * lax.rsqrt(spread + eps)

def attend(pieces):
    query_rows, key_rows, value_rows, label_rows = pieces
    scores = jnp.einsum('qhd,khd->hqk', query_rows, key_rows, precision=precision_highest) / math.sqrt(HD)
    scores = low_back(scores)
    allowed = label_rows[:, None] == label_rows[None, :]
    scores = jnp.where(allowed[None], scores, -1000000000.0)
    highest = lax.optimization_barrier(jnp.max(scores, axis=-1, keepdims=True))
    exponent = jnp.exp(scores - highest)
    chances = lowered_copy(exponent / lax.optimization_barrier(jnp.sum(exponent, axis=-1, keepdims=True)))
    return jnp.einsum('hqk,khd->qhd', chances, value_rows, precision=precision_highest)

def layer(input_rows, label_rows, w_qkv, b_qv, w_out, b_out, gain_one, shift_one, w_up, b_up, down_weight, down_bias, gain_two, shift_two):
    token_count = input_rows.shape[0]
    row_count = label_rows.shape[0]
    grouped = input_rows.reshape(token_count, CONV_GROUPS, GW)
    key_zero = jnp.zeros((CONV_GROUPS, GW), jnp.float32)
    bias_all = jnp.concatenate([b_qv[:, :GW], key_zero, b_qv[:, GW:]], axis=1)
    mixed_all = jnp.einsum('tgc,gcd->tgd', grouped, lowered_copy(w_qkv), precision=precision_highest) + bias_all
    mixed_all = lowered_copy(low_back(mixed_all))
    shaped = mixed_all.reshape(row_count, SEQ, CONV_GROUPS, 3, HG, HD)
    query_rows = shaped[:, :, :, 0].reshape(row_count, SEQ, HEADS, HD)
    key_rows = shaped[:, :, :, 1].reshape(row_count, SEQ, HEADS, HD)
    value_rows = shaped[:, :, :, 2].reshape(row_count, SEQ, HEADS, HD)
    context = lax.map(jax.checkpoint(attend), (query_rows, key_rows, value_rows, label_rows))
    context = lowered_copy(low_back(context.reshape(token_count, D)))
    attended = low_back(jnp.dot(context, lowered_copy(w_out), precision=precision_highest) + b_out)
    hidden = normalize(input_rows + attended) * gain_one + shift_one
    hidden_low = lowered_copy(hidden).reshape(token_count, CONV_GROUPS, GW)
    pre_act = jnp.einsum('tgc,gcf->tgf', hidden_low, lowered_copy(w_up), precision=precision_highest) + b_up
    active_values = lowered_copy(smooth_gate(low_back(pre_act)))
    branch_output = jnp.einsum('ypz,pze->ype', active_values, lowered_copy(down_weight), precision=precision_highest) + down_bias
    branch_output = low_back(branch_output).reshape(token_count, D)
    return normalize(hidden + branch_output) * gain_two + shift_two

def reference(inputs, labels, w_qkv, b_qv, w_out, b_out, gain_one, shift_one, w_up, b_up, down_weight, down_bias, gain_two, shift_two, grad_out):
    row_count = labels.shape[0]
    block_rows = math.gcd(row_count, 8)
    block_count = row_count // block_rows
    weights = (w_qkv, b_qv, w_out, b_out, gain_one, shift_one, w_up, b_up, down_weight, down_bias, gain_two, shift_two)
    input_blocks = inputs.astype(jnp.float32).T.reshape(block_count, block_rows * SEQ, D)
    label_blocks = labels.reshape(block_count, block_rows, SEQ)
    grad_blocks = grad_out.astype(jnp.float32).T.reshape(block_count, block_rows * SEQ, D)

    def one_block(running, pieces):
        input_rows, label_rows, cotangent = pieces

        def forward(rows_in, *params_in):
            return layer(rows_in, label_rows, *params_in)
        rows_output, pullback = jax.vjp(forward, input_rows, *weights)
        gradients = pullback(cotangent)
        running = tuple((total + extra for total, extra in zip(running, gradients[1:])))
        return (running, (rows_output.astype(jnp.bfloat16), gradients[0]))
    initial = tuple((jnp.zeros_like(weight) for weight in weights))
    summed, (results, input_grads) = lax.scan(one_block, initial, (input_blocks, label_blocks, grad_blocks))
    return (results.reshape(TOKENS, D).T, input_grads.reshape(TOKENS, D).T, summed[0], summed[1], summed[2], summed[3], summed[4], summed[5], summed[6], summed[7], summed[8], summed[9], summed[10], summed[11])
```

```python
import functools
import math

import jax
import jax.numpy as jnp
from jax import lax
from jax.experimental import pallas as pl
from jax.experimental.pallas import tpu as pltpu
from jax.sharding import PartitionSpec as P

HD = 64
HG = 3
LANES = 128
SPLIT = 2
DELAY = 5

eps = 1e-12
f32 = jnp.float32
bf16 = jnp.bfloat16
MESH = pl.DeviceIdType.MESH


def mm(left, right):
    return jnp.dot(left, right, preferred_element_type=f32)


def mm_nt(left, right):
    return lax.dot_general(left, right, (((1,), (1,)), ((), ())), preferred_element_type=f32)


def mm_tn(left, right):
    return lax.dot_general(left, right, (((0,), (0,)), ((), ())), preferred_element_type=f32)


def row_sum(x):
    return jnp.sum(x, axis=0, keepdims=True)


def remote(src, dst, send, recv, device):
    return pltpu.make_async_remote_copy(
        src_ref=src, dst_ref=dst, send_sem=send, recv_sem=recv, device_id=device, device_id_type=MESH
    )


def gather_kernel(dp, groups, *refs):
    shards, fulls, out_rows = refs[:4], refs[4:8], refs[8]
    send, recv, send_rows, recv_rows, local_sem = refs[9:]
    d = lax.axis_index("dp")
    g = lax.axis_index("group")
    per = dp // groups
    for shard, full in zip(shards, fulls):
        full[d] = shard[...].astype(bf16)

    def column_copy(k, which, slot, peer):
        return remote(
            fulls[which].at[slot],
            fulls[which].at[slot],
            send.at[which, k],
            recv.at[which, k],
            {"dp": peer, "group": g},
        )

    def row_copy(k, source_d, source_g, peer, target):
        return remote(
            fulls[1].at[d],
            out_rows.at[lax.rem(source_d, per), source_g],
            send_rows.at[k],
            recv_rows.at[lax.rem(source_d, per), source_g],
            {"dp": peer, "group": target},
        )

    target = d // per
    for which in range(4):

        def start(k, carry):
            column_copy(k, which, d, lax.rem(d + k, dp)).start()
            return carry

        lax.fori_loop(1, dp, start, 0)

    def start_rows(k, carry):
        peer = lax.rem(d + k, dp)

        @pl.when(jnp.logical_or(k != 0, target != g))
        def _():
            row_copy(k, d, g, peer, target).start()

        return carry

    lax.fori_loop(0, dp, start_rows, 0)

    @pl.when(target == g)
    def _():
        copy = pltpu.make_async_copy(fulls[1].at[d], out_rows.at[lax.rem(d, per), g], local_sem)
        copy.start()
        copy.wait()

    for which in range(4):

        def finish(k, carry):
            column_copy(k, which, lax.rem(d - k + dp, dp), lax.rem(d + k, dp)).wait()
            return carry

        lax.fori_loop(1, dp, finish, 0)

    def finish_rows(k, carry):
        @pl.when(jnp.logical_or(k != 0, target != g))
        def _():
            row_copy(k, d, g, lax.rem(d + k, dp), target).wait_send()

        return carry

    lax.fori_loop(0, dp, finish_rows, 0)
    for source in range(groups):

        def arrive(k, carry):
            source_d = g * per + k

            @pl.when(jnp.logical_or(source_d != d, source != g))
            def _():
                row_copy(k, source_d, source, d, g).wait_recv()

            return carry

        lax.fori_loop(0, per, arrive, 0)


def gather_weights(w_qkv, w_out, w_up, down_weight):
    dp = lax.axis_size("dp")
    groups = lax.axis_size("group")
    shards = (w_qkv, w_out, w_up, down_weight)
    full_shapes = tuple(jax.ShapeDtypeStruct((dp, *w.shape), bf16) for w in shards)
    rows_shape = jax.ShapeDtypeStruct((dp // groups, groups, *w_out.shape), bf16)
    vmem = pl.BlockSpec(memory_space=pltpu.VMEM)
    return pl.pallas_call(
        functools.partial(gather_kernel, dp, groups),
        out_shape=(*full_shapes, rows_shape),
        in_specs=[vmem] * 4,
        out_specs=tuple([vmem] * 5),
        scratch_shapes=[
            pltpu.SemaphoreType.DMA((4, dp)),
            pltpu.SemaphoreType.DMA((4, dp)),
            pltpu.SemaphoreType.DMA((dp,)),
            pltpu.SemaphoreType.DMA((dp // groups, groups)),
            pltpu.SemaphoreType.DMA,
        ],
        compiler_params=pltpu.CompilerParams(has_side_effects=True, vmem_limit_bytes=48 << 20),
        name="gather_weights",
    )(*shards)


def scatter_kernel(dp, *refs):
    grads, outs, sums_out = refs[:4], refs[5:9], refs[9]
    sums = refs[4]
    staged, landed = refs[10:14], refs[14:18]
    sums_all, send, recv = refs[18:]
    d = lax.axis_index("dp")
    g = lax.axis_index("group")
    for grad, stage in zip(grads, staged):
        stage[...] = grad[...].astype(bf16)
    total = jnp.sum(sums[...], axis=-1)
    sums_all[d] = total

    def copies(k, slot_from, slot_to, peer):
        device = {"dp": peer, "group": g}
        made = [
            remote(staged[w].at[slot_from], landed[w].at[slot_to], send.at[w, k], recv.at[w, k], device)
            for w in range(4)
        ]
        made.append(
            remote(sums_all.at[slot_to], sums_all.at[slot_to], send.at[4, k], recv.at[4, k], device)
        )
        return made

    def start(k, carry):
        peer = lax.rem(d + k, dp)
        for copy in copies(k, peer, d, peer):
            copy.start()
        return carry

    lax.fori_loop(1, dp, start, 0)
    for w in range(4):
        outs[w][...] = staged[w][d].astype(f32)

    def finish(k, carry):
        source = lax.rem(d - k + dp, dp)
        for copy in copies(k, lax.rem(d + k, dp), source, lax.rem(d + k, dp)):
            copy.wait()
        for w in range(4):
            outs[w][...] += landed[w][source].astype(f32)
        return carry

    lax.fori_loop(1, dp, finish, 0)
    sums_out[...] = jnp.sum(sums_all[...], axis=0)


def scatter_grads(grads, sums):
    dp = lax.axis_size("dp")
    vmem = pl.BlockSpec(memory_space=pltpu.VMEM)
    cut = tuple(g.reshape(dp, g.shape[0] // dp, g.shape[1]) for g in grads)
    sums = sums.reshape(-1, LANES, LANES)
    return pl.pallas_call(
        functools.partial(scatter_kernel, dp),
        out_shape=(
            *(jax.ShapeDtypeStruct(c.shape[1:], f32) for c in cut),
            jax.ShapeDtypeStruct(sums.shape[:2], f32),
        ),
        in_specs=[vmem] * 5,
        out_specs=tuple([vmem] * 5),
        scratch_shapes=[
            *(pltpu.VMEM(c.shape, bf16) for c in cut),
            *(pltpu.VMEM(c.shape, bf16) for c in cut),
            pltpu.VMEM((dp, *sums.shape[:2]), f32),
            pltpu.SemaphoreType.DMA((5, dp)),
            pltpu.SemaphoreType.DMA((5, dp)),
        ],
        compiler_params=pltpu.CompilerParams(has_side_effects=True, vmem_limit_bytes=48 << 20),
        name="scatter_grads",
    )(*cut, sums)


def layer_kernel(
    rows,
    groups,
    place,
    inp,
    gout_in,
    wqkv_t,
    wqkv,
    wout_t,
    wout_rows,
    wup_t,
    wup,
    wdown_t,
    wdown,
    b_qkv,
    b_up,
    cols,
    result,
    grad_in,
    g_qkv,
    g_out,
    g_up,
    g_down,
    sums,
    ctx_all,
    att_all,
    stat_one,
    stat_two,
    sum_one,
    x_ring,
    mix_ring,
    prob_ring,
    mask,
    x_one,
    n_one,
    inv_one,
    hid,
    hid_low,
    pre,
    act,
    slope,
    x_two,
    upstream,
    res,
    rtg,
    br_low,
    pre_low,
    hid_grad,
    rog_ring,
    ctx_grad,
    mix_grad,
    send_blocks,
    recv_blocks,
    send_stats,
    recv_stats,
):
    i = pl.program_id(0)
    steps = pl.num_programs(0)
    g = lax.axis_index("group")
    across = lax.rem(g + 2, groups)
    beside = g + 1 - 2 * lax.rem(g, 2)
    corner = lax.rem(beside + 2, groups)
    local, seq = inp.shape
    half = seq // SPLIT
    channels = local * groups
    parts = seq // LANES
    hidden_units = wup_t.shape[0]
    ring = x_ring.shape[0]
    lanes = [slice(k * LANES, (k + 1) * LANES) for k in range(parts)]
    col = lambda n: cols[n * local : (n + 1) * local, :]
    B_OUT, GAIN1, SHIFT1, B_DOWN, GAIN2, SHIFT2 = range(6)
    S_BOUT, S_GAIN1, S_SHIFT1, S_BDOWN, S_GAIN2, S_SHIFT2 = range(6)

    def accumulate(slot, chunk):
        sums[slot * local : (slot + 1) * local, :] += chunk

    def block_copy(buf, base, kind, r, slot):
        peer = across if kind == 0 else beside
        return remote(
            buf.at[r, slot],
            buf.at[r, slot],
            send_blocks.at[base + kind, r],
            recv_blocks.at[base + kind, r],
            {"group": peer},
        )

    def send_own(buf, base, r):
        block_copy(buf, base, 0, r, g).start()
        block_copy(buf, base, 1, r, g).start()

    def pass_on(buf, base, r):
        block_copy(buf, base, 0, r, across).wait_recv()
        block_copy(buf, base, 2, r, across).start()

    def blocks_ready(buf, base, r):
        block_copy(buf, base, 1, r, beside).wait_recv()
        block_copy(buf, base, 2, r, corner).wait_recv()

    def blocks_sent(buf, base, r):
        block_copy(buf, base, 0, r, g).wait_send()
        block_copy(buf, base, 1, r, g).wait_send()
        block_copy(buf, base, 2, r, across).wait_send()

    def stat_copy(buf, base, offset, r, slot):
        return remote(
            buf.at[r, slot],
            buf.at[r, slot],
            send_stats.at[base + offset - 1, r],
            recv_stats.at[base + offset - 1, r],
            {"group": lax.rem(g + offset, groups)},
        )

    def send_stat(buf, base, r):
        for offset in range(1, groups):
            stat_copy(buf, base, offset, r, g).start()

    def stat_ready(buf, base, r):
        for offset in range(1, groups):
            stat_copy(buf, base, offset, r, lax.rem(g + groups - offset, groups)).wait_recv()

    def stat_sent(buf, base, r):
        for offset in range(1, groups):
            stat_copy(buf, base, offset, r, g).wait_send()

    CTX, ATT = 0, 3
    ONE, TWO, BACK = 0, groups - 1, 2 * (groups - 1)

    @pl.when(i == 0)
    def _():
        barrier = pltpu.get_barrier_semaphore()
        for offset in range(1, groups):
            pl.semaphore_signal(
                barrier, inc=1, device_id={"group": lax.rem(g + offset, groups)}, device_id_type=MESH
            )
        pl.semaphore_wait(barrier, groups - 1)
        for ref in (g_qkv, g_out, g_up, g_down, sums):
            ref[...] = jnp.zeros_like(ref)

    def stage_residual(r):
        blocks_ready(ctx_all, CTX, r)
        attended = mm(wout_t[...], ctx_all[r].reshape(channels, seq))
        xr = x_ring.at[lax.rem(r, ring)]
        for k, s in enumerate(lanes):
            x = xr[:, s].astype(f32) + attended[:, s] + col(B_OUT)
            x_one[:, s] = x
            mean = row_sum(x) * (1.0 / local)
            off = x - mean
            stat_one[r, g, k : k + 1, :] = mean
            stat_one[r, g, parts + k : parts + k + 1, :] = row_sum(off * off)
        send_stat(stat_one, ONE, r)

    def stage_attend(r):
        slot = lax.rem(r, ring)
        rolled = pltpu.roll(inp[...].astype(f32), place[r, 0], 1).astype(bf16)
        x_ring[slot] = rolled
        mixed = mm(wqkv_t[...], rolled)
        for s in lanes:
            mix_ring[slot, :, s] = (mixed[:, s] + b_qkv[...]).astype(bf16)
        first, second = place[r, 2], place[r, 3]
        down = lax.broadcasted_iota(jnp.int32, (half, half), 0)
        along = lax.broadcasted_iota(jnp.int32, (half, half), 1)
        own = lambda at: (at >= first).astype(jnp.int32) + (at >= second).astype(jnp.int32)
        mask[...] = jnp.where(own(down) == own(along), 0.0, -1000000000.0)
        scale = math.log2(math.e) / math.sqrt(HD)
        for h in range(HG):
            heads = slice(h * HD, (h + 1) * HD)
            keys = slice(local + h * HD, local + (h + 1) * HD)
            values = slice(2 * local + h * HD, 2 * local + (h + 1) * HD)
            for b in range(SPLIT):
                toks = slice(b * half, (b + 1) * half)
                scores = mm_tn(mix_ring[slot, keys, toks], mix_ring[slot, heads, toks])
                if b:
                    scores = scores + mask[...]
                highest = jnp.max(scores, axis=0, keepdims=True)
                exponent = jnp.exp2((scores - highest) * scale)
                chances = (exponent * (1.0 / row_sum(exponent))).astype(bf16)
                prob_ring[slot, h * SPLIT + b] = chances
                ctx_all[r, g, heads, toks] = mm(mix_ring[slot, values, toks], chances).astype(bf16)
        send_own(ctx_all, CTX, r)

    def stage_norm_back(r):
        stat_ready(sum_one, BACK, r)
        slot = lax.rem(r, rog_ring.shape[0])
        for k, s in enumerate(lanes):
            first = sum_one[r, 0, k : k + 1, :]
            second = sum_one[r, 0, parts + k : parts + k + 1, :]
            for p in range(1, groups):
                first += sum_one[r, p, k : k + 1, :]
                second += sum_one[r, p, parts + k : parts + k + 1, :]
            first = first * (1.0 / channels)
            second = second * (1.0 / channels)
            scaled = hid_grad[:, s] * col(GAIN1)
            back = inv_one[k : k + 1, :] * (scaled - first - n_one[:, s] * second)
            rog_ring[slot, :, s] = back
            low = back.astype(bf16)
            att_all[r, g, :, s] = low
            accumulate(S_BOUT, low.astype(f32))
        send_own(att_all, ATT, r)
        g_out[...] += mm_nt(ctx_all[r].reshape(channels, seq), att_all[r, g])

    def stage_feed(r):
        stat_ready(stat_one, ONE, r)
        for k, s in enumerate(lanes):
            means = [stat_one[r, p, k : k + 1, :] for p in range(groups)]
            center = sum(means[1:], means[0]) * (1.0 / groups)
            spread = stat_one[r, 0, parts + k : parts + k + 1, :]
            for p in range(1, groups):
                spread += stat_one[r, p, parts + k : parts + k + 1, :]
            for mean in means:
                spread += local * (mean - center) * (mean - center)
            inverse = lax.rsqrt(spread * (1.0 / channels) + eps)
            inv_one[k : k + 1, :] = inverse
            normed = (x_one[:, s] - center) * inverse
            n_one[:, s] = normed
            h = normed * col(GAIN1) + col(SHIFT1)
            hid[:, s] = h
            hid_low[:, s] = h.astype(bf16)
        pre[...] = mm(wup_t[...], hid_low[...])
        for j in range(hidden_units // local):
            units = slice(j * local, (j + 1) * local)
            for s in lanes:
                u = pre[units, s] + b_up[units, :]
                cdf = 0.5 + 0.5 * lax.erf(u * math.sqrt(0.5))
                act[units, s] = (u * cdf).astype(bf16)
                bell = jnp.exp2(u * u * (-0.5 * math.log2(math.e))) * (1.0 / math.sqrt(2.0 * math.pi))
                slope[units, s] = cdf + u * bell
        branch = mm(wdown_t[...], act[...])
        upstream[...] = pltpu.roll(gout_in[...].astype(f32), place[r, 0], 1)
        for k, s in enumerate(lanes):
            x = hid[:, s] + branch[:, s] + col(B_DOWN)
            x_two[:, s] = x
            mean = row_sum(x) * (1.0 / local)
            off = x - mean
            scaled = upstream[:, s] * col(GAIN2)
            tile = (mean, row_sum(off * off), row_sum(scaled), row_sum(scaled * off))
            for n, value in enumerate(tile):
                stat_two[r, g, n * parts + k : n * parts + k + 1, :] = value
        send_stat(stat_two, TWO, r)

    def stage_attend_back(r):
        slot = lax.rem(r, ring)
        blocks_ready(att_all, ATT, r)
        ctx_grad[...] = mm(wout_rows[...], att_all[r].reshape(channels, seq)).astype(bf16)
        factor = 1.0 / math.sqrt(HD)
        for h in range(HG):
            heads = slice(h * HD, (h + 1) * HD)
            keys = slice(local + h * HD, local + (h + 1) * HD)
            values = slice(2 * local + h * HD, 2 * local + (h + 1) * HD)
            for b in range(SPLIT):
                toks = slice(b * half, (b + 1) * half)
                incoming = ctx_grad[heads, toks]
                chances = prob_ring[slot, h * SPLIT + b]
                prob_grad = mm_tn(mix_ring[slot, values, toks], incoming)
                inner = row_sum(incoming.astype(f32) * ctx_all[r, g, heads, toks].astype(f32))
                score_grad = (chances.astype(f32) * (prob_grad - inner)).astype(bf16)
                mix_grad[values, toks] = mm_nt(incoming, chances).astype(bf16)
                mix_grad[heads, toks] = (mm(mix_ring[slot, keys, toks], score_grad) * factor).astype(bf16)
                mix_grad[keys, toks] = (mm_nt(mix_ring[slot, heads, toks], score_grad) * factor).astype(bf16)
        g_qkv[...] += mm_nt(mix_grad[...], x_ring[slot])
        total = mm(wqkv[...], mix_grad[...]) + rog_ring[lax.rem(r, rog_ring.shape[0])]
        grad_in[...] = pltpu.roll(total, place[r, 1], 1)
        base = 6 * local + hidden_units
        for n, start in ((0, 0), (1, 2 * local)):
            chunk = mix_grad[start : start + local, lanes[0]].astype(f32)
            for s in lanes[1:]:
                chunk += mix_grad[start : start + local, s].astype(f32)
            sums[base + n * local : base + (n + 1) * local, :] += chunk

    def stage_feed_back(r):
        stat_ready(stat_two, TWO, r)
        for k, s in enumerate(lanes):
            row = lambda p, n: stat_two[r, p, n * parts + k : n * parts + k + 1, :]
            means = [row(p, 0) for p in range(groups)]
            center = sum(means[1:], means[0]) * (1.0 / groups)
            spread, first, second = row(0, 1), row(0, 2), row(0, 3)
            for p in range(1, groups):
                spread += row(p, 1)
                first += row(p, 2)
                second += row(p, 3)
            for p, mean in enumerate(means):
                spread += local * (mean - center) * (mean - center)
                second += (mean - center) * row(p, 2)
            inverse = lax.rsqrt(spread * (1.0 / channels) + eps)
            first = first * (1.0 / channels)
            second = second * inverse * (1.0 / channels)
            normed = (x_two[:, s] - center) * inverse
            res[:, s] = normed * col(GAIN2) + col(SHIFT2)
            up = upstream[:, s]
            back = inverse * (up * col(GAIN2) - first - normed * second)
            rtg[:, s] = back
            low = back.astype(bf16)
            br_low[:, s] = low
            accumulate(S_GAIN2, up * normed)
            accumulate(S_SHIFT2, up)
            accumulate(S_BDOWN, low.astype(f32))
        result[...] = pltpu.roll(res[...], place[r, 1], 1).astype(bf16)
        pre[...] = mm(wdown[...], br_low[...])
        g_down[...] += mm_nt(act[...], br_low[...])
        base = 6 * local
        for j in range(hidden_units // local):
            units = slice(j * local, (j + 1) * local)
            for s in lanes:
                low = (slope[units, s] * pre[units, s]).astype(bf16)
                pre_low[units, s] = low
                sums[base + j * local : base + (j + 1) * local, :] += low.astype(f32)
        g_up[...] += mm_nt(pre_low[...], hid_low[...])
        change = mm(wup[...], pre_low[...])
        for k, s in enumerate(lanes):
            total = rtg[:, s] + change[:, s]
            hid_grad[:, s] = total
            normed = n_one[:, s]
            scaled = total * col(GAIN1)
            sum_one[r, g, k : k + 1, :] = row_sum(scaled)
            sum_one[r, g, parts + k : parts + k + 1, :] = row_sum(scaled * normed)
            accumulate(S_GAIN1, total * normed)
            accumulate(S_SHIFT1, total)
        send_stat(sum_one, BACK, r)

    def at(delay, stage):
        r = i - delay

        @pl.when(jnp.logical_and(r >= 0, r < rows))
        def _():
            stage(r)

    at(2, stage_residual)
    at(0, stage_attend)
    at(3, stage_norm_back)
    at(2, stage_feed)
    at(DELAY, stage_attend_back)
    at(1, lambda r: pass_on(ctx_all, CTX, r))
    at(4, lambda r: pass_on(att_all, ATT, r))
    at(2, stage_feed_back)

    @pl.when(i == steps - 1)
    def _():
        def drain(r, carry):
            blocks_sent(ctx_all, CTX, r)
            blocks_sent(att_all, ATT, r)
            stat_sent(stat_one, ONE, r)
            stat_sent(stat_two, TWO, r)
            stat_sent(sum_one, BACK, r)
            return carry

        lax.fori_loop(0, rows, drain, 0)


def run_layer(place, inputs, grad_out, mats, b_qkv, b_up, cols):
    groups = lax.axis_size("group")
    local, tok_count = inputs.shape
    rows = place.shape[0]
    seq = tok_count // rows
    half = seq // SPLIT
    parts = seq // LANES
    units = b_up.shape[0]
    last = rows - 1
    ring = DELAY + 1
    vmem = pl.BlockSpec(memory_space=pltpu.VMEM)

    def rows_at(delay):
        return pl.BlockSpec((local, seq), lambda i: (0, jnp.clip(i - delay, 0, last)))

    def whole(shape):
        return pl.BlockSpec(shape, lambda i: (0,) * len(shape))

    acc_shapes = ((3 * local, local), (groups * local, local), (units, local), (units, local))
    sums_shape = (6 * local + units + 2 * local, LANES)
    block = (rows, groups, local, seq)
    return pl.pallas_call(
        functools.partial(layer_kernel, rows, groups),
        grid=(rows + DELAY,),
        out_shape=(
            jax.ShapeDtypeStruct((local, tok_count), bf16),
            jax.ShapeDtypeStruct((local, tok_count), f32),
            *(jax.ShapeDtypeStruct(s, f32) for s in acc_shapes),
            jax.ShapeDtypeStruct(sums_shape, f32),
        ),
        in_specs=[
            pl.BlockSpec(memory_space=pltpu.SMEM),
            rows_at(0),
            rows_at(2),
            *([vmem] * (len(mats) + 3)),
        ],
        out_specs=(
            rows_at(2),
            rows_at(DELAY),
            *(whole(s) for s in acc_shapes),
            whole(sums_shape),
        ),
        scratch_shapes=[
            pltpu.VMEM(block, bf16),
            pltpu.VMEM(block, bf16),
            pltpu.VMEM((rows, groups, 2 * parts, LANES), f32),
            pltpu.VMEM((rows, groups, 4 * parts, LANES), f32),
            pltpu.VMEM((rows, groups, 2 * parts, LANES), f32),
            pltpu.VMEM((ring, local, seq), bf16),
            pltpu.VMEM((ring, 3 * local, seq), bf16),
            pltpu.VMEM((ring, HG * SPLIT, half, half), bf16),
            pltpu.VMEM((half, half), f32),
            pltpu.VMEM((local, seq), f32),
            pltpu.VMEM((local, seq), f32),
            pltpu.VMEM((parts, LANES), f32),
            pltpu.VMEM((local, seq), f32),
            pltpu.VMEM((local, seq), bf16),
            pltpu.VMEM((units, seq), f32),
            pltpu.VMEM((units, seq), bf16),
            pltpu.VMEM((units, seq), f32),
            pltpu.VMEM((local, seq), f32),
            pltpu.VMEM((local, seq), f32),
            pltpu.VMEM((local, seq), f32),
            pltpu.VMEM((local, seq), f32),
            pltpu.VMEM((local, seq), bf16),
            pltpu.VMEM((units, seq), bf16),
            pltpu.VMEM((local, seq), f32),
            pltpu.VMEM((3, local, seq), f32),
            pltpu.VMEM((local, seq), bf16),
            pltpu.VMEM((3 * local, seq), bf16),
            pltpu.SemaphoreType.DMA((6, rows)),
            pltpu.SemaphoreType.DMA((6, rows)),
            pltpu.SemaphoreType.DMA((3 * (groups - 1), rows)),
            pltpu.SemaphoreType.DMA((3 * (groups - 1), rows)),
        ],
        compiler_params=pltpu.CompilerParams(
            collective_id=0, has_side_effects=True, vmem_limit_bytes=60 << 20
        ),
        name="layer",
    )(place, inputs, grad_out, *mats, b_qkv, b_up, cols)


def row_places(labels):
    seq = labels.shape[1]
    half = seq // SPLIT
    counts = [jnp.sum((labels == v).astype(jnp.int32), axis=1) for v in range(4)]
    start = jnp.zeros_like(counts[0])
    first = jnp.zeros_like(start)
    second = jnp.zeros_like(start)
    found = jnp.zeros_like(start)
    begin = jnp.zeros_like(start)
    for v in range(4):
        hit = jnp.where(counts[v] == half, 1 - found, 0)
        start = start + hit * begin
        first = first + hit * counts[(v + 1) % 4]
        second = second + hit * (counts[(v + 1) % 4] + counts[(v + 2) % 4])
        found = found + hit
        begin = begin + counts[v]
    return jnp.stack([(seq - start) % seq, start, first, second], axis=1)


def per_device(
    inputs,
    labels,
    w_qkv,
    b_qv,
    w_out,
    b_out,
    gain_one,
    shift_one,
    w_up,
    b_up,
    down_weight,
    down_bias,
    gain_two,
    shift_two,
    grad_out,
):
    groups = lax.axis_size("group")
    local = inputs.shape[0]
    units = b_up.shape[1]
    channels = local * groups
    gathered = gather_weights(w_qkv[0], w_out, w_up[0], down_weight[0])
    mat_qkv = gathered[0].reshape(local, 3 * local)
    mat_out = gathered[1].reshape(channels, local)
    mat_up = gathered[2].reshape(local, units)
    mat_down = gathered[3].reshape(units, local)
    out_rows = jnp.swapaxes(gathered[4], 1, 2).reshape(local, channels)
    mats = (
        mat_qkv.T,
        mat_qkv,
        mat_out.T,
        out_rows,
        mat_up.T,
        mat_up,
        mat_down.T,
        mat_down,
    )
    wide = lambda v: jnp.broadcast_to(v[:, None], (v.shape[0], LANES))
    key_zero = jnp.zeros((local,), f32)
    qkv_bias = jnp.concatenate([b_qv[0, :local], key_zero, b_qv[0, local:]])
    cols = jnp.concatenate([b_out, gain_one, shift_one, down_bias[0], gain_two, shift_two])
    result, input_grad, qkv_t, out_grad, up_t, down_grad, sums = run_layer(
        row_places(labels), inputs, grad_out, mats, wide(qkv_bias), wide(b_up[0]), wide(cols)
    )
    grads = scatter_grads((qkv_t.T, out_grad, up_t.T, down_grad), sums)
    flat = grads[4].reshape(-1)
    piece = lambda n: flat[n * local : (n + 1) * local]
    base = 6 * local
    return (
        result,
        input_grad,
        grads[0][None],
        flat[base + units :][None],
        grads[1],
        piece(0),
        piece(1),
        piece(2),
        grads[2][None],
        flat[base : base + units][None],
        grads[3][None],
        piece(3)[None],
        piece(4),
        piece(5),
    )


def solution(mesh):
    placed = (
        P("group", "dp"),
        P("dp", None),
        P("group", "dp", None),
        P("group", None),
        P("dp", "group"),
        P("group"),
        P("group"),
        P("group"),
        P("group", "dp", None),
        P("group", None),
        P("group", "dp", None),
        P("group", None),
        P("group"),
        P("group"),
        P("group", "dp"),
    )
    return jax.shard_map(
        per_device,
        mesh=mesh,
        in_specs=placed,
        out_specs=(
            P("group", "dp"),
            P("group", "dp"),
            P("group", "dp", None),
            P("group", None),
            P("dp", "group"),
            P("group"),
            P("group"),
            P("group"),
            P("group", "dp", None),
            P("group", None),
            P("group", "dp", None),
            P("group", None),
            P("group"),
            P("group"),
        ),
        check_vma=False,
    )
```

```python
import functools
import math

import jax
import jax.numpy as jnp
from jax import lax
from jax.experimental import pallas as pl
from jax.experimental.pallas import tpu as pltpu
from jax.sharding import PartitionSpec as P

HD = 64
HG = 3
LANES = 128
SPLIT = 2
DELAY = 7

eps = 1e-12
f32 = jnp.float32
bf16 = jnp.bfloat16
MESH = pl.DeviceIdType.MESH


def mm(left, right):
    return jnp.dot(left, right, preferred_element_type=f32)


def mm_nt(left, right):
    return lax.dot_general(left, right, (((1,), (1,)), ((), ())), preferred_element_type=f32)


def mm_tn(left, right):
    return lax.dot_general(left, right, (((0,), (0,)), ((), ())), preferred_element_type=f32)


def row_sum(x):
    return jnp.sum(x, axis=0, keepdims=True)


def remote(src, dst, send, recv, device):
    return pltpu.make_async_remote_copy(
        src_ref=src, dst_ref=dst, send_sem=send, recv_sem=recv, device_id=device, device_id_type=MESH
    )


def layer_kernel(
    rows,
    groups,
    dp,
    place,
    inp,
    gout_in,
    w_qkv,
    w_out,
    w_up,
    w_down,
    b_qkv,
    b_up,
    cols,
    result,
    grad_in,
    o_qkv,
    o_out,
    o_up,
    o_down,
    o_sums,
    wqkv_t,
    wqkv,
    wout_t,
    wout_rows,
    wup_t,
    wup,
    wdown_t,
    wdown,
    all_qkv,
    all_out,
    all_up,
    all_down,
    out_rows,
    wide_mat,
    tall_mat,
    g_qkv,
    g_out,
    g_up,
    g_down,
    sums,
    land_qkv,
    land_out,
    land_up,
    land_down,
    all_sums,
    ctx_all,
    att_all,
    stat_one,
    stat_two,
    sum_one,
    x_ring,
    mix_ring,
    prob_ring,
    mask,
    x_one,
    n_one,
    inv_one,
    hid,
    hid_low,
    pre,
    act,
    slope,
    x_two,
    upstream,
    rtg,
    br_low,
    pre_low,
    hid_grad,
    rog_ring,
    ctx_grad,
    mix_grad,
    send_blocks,
    recv_blocks,
    send_stats,
    recv_stats,
    send_weights,
    recv_weights,
    send_rows,
    recv_rows,
    send_grads,
    recv_grads,
):
    i = pl.program_id(0)
    steps = pl.num_programs(0)
    g = lax.axis_index("group")
    d = lax.axis_index("dp")
    across = lax.rem(g + 2, groups)
    beside = g + 1 - 2 * lax.rem(g, 2)
    corner = lax.rem(beside + 2, groups)
    local, seq = inp.shape
    half = seq // SPLIT
    channels = local * groups
    parts = seq // LANES
    hidden_units = wup_t.shape[0]
    ring = x_ring.shape[0]
    lanes = [slice(k * LANES, (k + 1) * LANES) for k in range(parts)]
    col = lambda n: cols[n * local : (n + 1) * local, :]
    B_OUT, GAIN1, SHIFT1, B_DOWN, GAIN2, SHIFT2 = range(6)
    S_BOUT, S_GAIN1, S_SHIFT1, S_BDOWN, S_GAIN2, S_SHIFT2 = range(6)

    def accumulate(slot, chunk):
        sums[slot * local : (slot + 1) * local, :] += chunk

    def block_copy(buf, base, kind, r, slot):
        peer = across if kind == 0 else beside
        return remote(
            buf.at[r, slot],
            buf.at[r, slot],
            send_blocks.at[base + kind, r],
            recv_blocks.at[base + kind, r],
            {"group": peer},
        )

    def send_own(buf, base, r):
        block_copy(buf, base, 0, r, g).start()
        block_copy(buf, base, 1, r, g).start()

    def pass_on(buf, base, r):
        block_copy(buf, base, 0, r, across).wait_recv()
        block_copy(buf, base, 2, r, across).start()

    def blocks_ready(buf, base, r):
        block_copy(buf, base, 1, r, beside).wait_recv()
        block_copy(buf, base, 2, r, corner).wait_recv()

    def blocks_sent(buf, base, r):
        block_copy(buf, base, 0, r, g).wait_send()
        block_copy(buf, base, 1, r, g).wait_send()
        block_copy(buf, base, 2, r, across).wait_send()

    def stat_copy(buf, base, offset, r, slot):
        return remote(
            buf.at[r, slot],
            buf.at[r, slot],
            send_stats.at[base + offset - 1, r],
            recv_stats.at[base + offset - 1, r],
            {"group": lax.rem(g + offset, groups)},
        )

    def send_stat(buf, base, r):
        for offset in range(1, groups):
            stat_copy(buf, base, offset, r, g).start()

    def stat_ready(buf, base, r):
        for offset in range(1, groups):
            stat_copy(buf, base, offset, r, lax.rem(g + groups - offset, groups)).wait_recv()

    def stat_sent(buf, base, r):
        for offset in range(1, groups):
            stat_copy(buf, base, offset, r, g).wait_send()

    CTX, ATT = 0, 3
    ONE, TWO, BACK = 0, groups - 1, 2 * (groups - 1)

    shards = (w_qkv, w_out, w_up, w_down)
    fulls = (all_qkv, all_out, all_up, all_down)
    QKV, OUT, UP, DOWN = range(4)

    def weight_copy(which, k, slot):
        full = fulls[which]
        return remote(
            full.at[slot],
            full.at[slot],
            send_weights.at[which, k],
            recv_weights.at[which, k],
            {"dp": lax.rem(d + k, dp)},
        )

    def each_peer(action):
        def body(k, carry):
            action(k)
            return carry

        lax.fori_loop(1, dp, body, 0)

    def weights_ready(which, into):
        each_peer(lambda k: weight_copy(which, k, lax.rem(d - k + dp, dp)).wait_recv())
        full = fulls[which]
        count, width = full.shape[1:]
        for slot in range(dp):
            into[slot * count : (slot + 1) * count, :width] = full[slot].astype(f32)

    per = dp // groups

    def rows_copy(offset, source, target):
        return remote(
            all_out.at[pl.ds(target * per, per)],
            out_rows.at[source],
            send_rows.at[offset - 1],
            recv_rows.at[offset - 1],
            {"group": target},
        )

    @pl.when(i == 0)
    def _():
        barrier = pltpu.get_barrier_semaphore()
        for offset in range(1, groups):
            pl.semaphore_signal(
                barrier, inc=1, device_id={"group": lax.rem(g + offset, groups)}, device_id_type=MESH
            )
        each_peer(
            lambda k: pl.semaphore_signal(
                barrier, inc=1, device_id={"dp": lax.rem(d + k, dp)}, device_id_type=MESH
            )
        )
        for shard, full in zip(shards, fulls):
            full[d] = shard[...].astype(bf16)
        pl.semaphore_wait(barrier, groups - 1 + dp - 1)
        for which in range(4):
            each_peer(lambda k, which=which: weight_copy(which, k, d).start())
        for ref in (g_qkv, g_out, g_up, g_down, sums):
            ref[...] = jnp.zeros_like(ref)
        weights_ready(QKV, wide_mat)
        mat = wide_mat[:, : 3 * local]
        wqkv[...] = mat.astype(bf16)
        wqkv_t[...] = mat.T.astype(bf16)

    @pl.when(i == 2)
    def _():
        weights_ready(OUT, tall_mat)
        for offset in range(1, groups):
            rows_copy(offset, g, lax.rem(g + offset, groups)).start()
        out_rows[g] = all_out[pl.ds(g * per, per)]
        wout_t[...] = tall_mat[...].T.astype(bf16)

    @pl.when(i == 3)
    def _():
        weights_ready(UP, wide_mat)
        mat = wide_mat[...]
        wup[...] = mat.astype(bf16)
        wup_t[...] = mat.T.astype(bf16)
        weights_ready(DOWN, tall_mat)
        mat = tall_mat[...]
        wdown[...] = mat.astype(bf16)
        wdown_t[...] = mat.T.astype(bf16)

    @pl.when(i == DELAY)
    def _():
        for offset in range(1, groups):
            rows_copy(offset, lax.rem(g + groups - offset, groups), g).wait_recv()
        count = local // per
        for p in range(groups):
            for n in range(per):
                wide_mat[n * count : (n + 1) * count, :local] = out_rows[p, n].astype(f32)
            tall_mat[p * local : (p + 1) * local, :] = wide_mat[:, :local].T
        wout_rows[...] = tall_mat[...].T.astype(bf16)

    stages = fulls
    lands = (land_qkv, land_out, land_up, land_down)

    def grad_copy(which, k, slot):
        return remote(
            stages[which].at[lax.rem(d + k, dp)],
            lands[which].at[slot],
            send_grads.at[which, k],
            recv_grads.at[which, k],
            {"dp": lax.rem(d + k, dp)},
        )

    def sums_copy(k, slot):
        return remote(
            all_sums.at[slot],
            all_sums.at[slot],
            send_grads.at[4, k],
            recv_grads.at[4, k],
            {"dp": lax.rem(d + k, dp)},
        )

    def send_grad(which, mat):
        stage = stages[which]
        count = stage.shape[1]
        for slot in range(dp):
            stage[slot] = mat[slot * count : (slot + 1) * count].astype(bf16)
        each_peer(lambda k: grad_copy(which, k, d).start())

    def grad_sum(which, out):
        out[...] = stages[which][d].astype(f32)

        def add(k):
            slot = lax.rem(d - k + dp, dp)
            grad_copy(which, k, slot).wait()
            out[...] += lands[which][slot].astype(f32)

        each_peer(add)

    def stage_residual(r):
        blocks_ready(ctx_all, CTX, r)
        attended = mm(wout_t[...], ctx_all[r].reshape(channels, seq))
        xr = x_ring.at[lax.rem(r, ring)]
        for k, s in enumerate(lanes):
            x = xr[:, s].astype(f32) + attended[:, s] + col(B_OUT)
            x_one[:, s] = x
            mean = row_sum(x) * (1.0 / local)
            off = x - mean
            stat_one[r, g, k : k + 1, :] = mean
            stat_one[r, g, parts + k : parts + k + 1, :] = row_sum(off * off)
        send_stat(stat_one, ONE, r)

    def stage_attend(r):
        slot = lax.rem(r, ring)
        rolled = pltpu.roll(inp[...].astype(f32), place[r, 0], 1).astype(bf16)
        x_ring[slot] = rolled
        mixed = mm(wqkv_t[...], rolled)
        for s in lanes:
            mix_ring[slot, :, s] = (mixed[:, s] + b_qkv[...]).astype(bf16)
        first, second = place[r, 2], place[r, 3]
        down = lax.broadcasted_iota(jnp.int32, (half, half), 0)
        along = lax.broadcasted_iota(jnp.int32, (half, half), 1)
        own = lambda at: (at >= first).astype(jnp.int32) + (at >= second).astype(jnp.int32)
        mask[...] = jnp.where(own(down) == own(along), 0.0, -1000000000.0)
        scale = math.log2(math.e) / math.sqrt(HD)
        for h in range(HG):
            heads = slice(h * HD, (h + 1) * HD)
            keys = slice(local + h * HD, local + (h + 1) * HD)
            values = slice(2 * local + h * HD, 2 * local + (h + 1) * HD)
            for b in range(SPLIT):
                toks = slice(b * half, (b + 1) * half)
                scores = mm_tn(mix_ring[slot, keys, toks], mix_ring[slot, heads, toks])
                if b:
                    scores = scores + mask[...]
                highest = jnp.max(scores, axis=0, keepdims=True)
                exponent = jnp.exp2((scores - highest) * scale)
                chances = (exponent * (1.0 / row_sum(exponent))).astype(bf16)
                prob_ring[slot, h * SPLIT + b] = chances
                ctx_all[r, g, heads, toks] = mm(mix_ring[slot, values, toks], chances).astype(bf16)
        send_own(ctx_all, CTX, r)

    def stage_norm_back(r):
        stat_ready(sum_one, BACK, r)
        slot = lax.rem(r, rog_ring.shape[0])
        two = lax.rem(r, 2)
        for k, s in enumerate(lanes):
            first = sum_one[r, 0, k : k + 1, :]
            second = sum_one[r, 0, parts + k : parts + k + 1, :]
            for p in range(1, groups):
                first += sum_one[r, p, k : k + 1, :]
                second += sum_one[r, p, parts + k : parts + k + 1, :]
            first = first * (1.0 / channels)
            second = second * (1.0 / channels)
            scaled = hid_grad[:, s] * col(GAIN1)
            back = inv_one[two, k : k + 1, :] * (scaled - first - n_one[two, :, s] * second)
            rog_ring[slot, :, s] = back
            low = back.astype(bf16)
            att_all[r, g, :, s] = low
            accumulate(S_BOUT, low.astype(f32))
        send_own(att_all, ATT, r)
        g_out[...] += mm_nt(ctx_all[r].reshape(channels, seq), att_all[r, g])

    def stage_feed(r):
        stat_ready(stat_one, ONE, r)
        two = lax.rem(r, 2)
        for k, s in enumerate(lanes):
            means = [stat_one[r, p, k : k + 1, :] for p in range(groups)]
            center = sum(means[1:], means[0]) * (1.0 / groups)
            spread = stat_one[r, 0, parts + k : parts + k + 1, :]
            for p in range(1, groups):
                spread += stat_one[r, p, parts + k : parts + k + 1, :]
            for mean in means:
                spread += local * (mean - center) * (mean - center)
            inverse = lax.rsqrt(spread * (1.0 / channels) + eps)
            inv_one[two, k : k + 1, :] = inverse
            normed = (x_one[:, s] - center) * inverse
            n_one[two, :, s] = normed
            h = normed * col(GAIN1) + col(SHIFT1)
            hid[:, s] = h
            hid_low[:, s] = h.astype(bf16)
        pre[...] = mm(wup_t[...], hid_low[...])
        for j in range(hidden_units // local):
            units = slice(j * local, (j + 1) * local)
            for s in lanes:
                u = pre[units, s] + b_up[units, :]
                cdf = 0.5 + 0.5 * lax.erf(u * math.sqrt(0.5))
                act[units, s] = (u * cdf).astype(bf16)
                bell = jnp.exp2(u * u * (-0.5 * math.log2(math.e))) * (1.0 / math.sqrt(2.0 * math.pi))
                slope[units, s] = cdf + u * bell
        branch = mm(wdown_t[...], act[...])
        upstream[...] = pltpu.roll(gout_in[...].astype(f32), place[r, 0], 1)
        for k, s in enumerate(lanes):
            x = hid[:, s] + branch[:, s] + col(B_DOWN)
            x_two[:, s] = x
            mean = row_sum(x) * (1.0 / local)
            off = x - mean
            scaled = upstream[:, s] * col(GAIN2)
            tile = (mean, row_sum(off * off), row_sum(scaled), row_sum(scaled * off))
            for n, value in enumerate(tile):
                stat_two[r, g, n * parts + k : n * parts + k + 1, :] = value
        send_stat(stat_two, TWO, r)

    def stage_attend_back(r):
        slot = lax.rem(r, ring)
        blocks_ready(att_all, ATT, r)
        ctx_grad[...] = mm(wout_rows[...], att_all[r].reshape(channels, seq)).astype(bf16)
        factor = 1.0 / math.sqrt(HD)
        for h in range(HG):
            heads = slice(h * HD, (h + 1) * HD)
            keys = slice(local + h * HD, local + (h + 1) * HD)
            values = slice(2 * local + h * HD, 2 * local + (h + 1) * HD)
            for b in range(SPLIT):
                toks = slice(b * half, (b + 1) * half)
                incoming = ctx_grad[heads, toks]
                chances = prob_ring[slot, h * SPLIT + b]
                prob_grad = mm_tn(mix_ring[slot, values, toks], incoming)
                inner = row_sum(incoming.astype(f32) * ctx_all[r, g, heads, toks].astype(f32))
                score_grad = (chances.astype(f32) * (prob_grad - inner)).astype(bf16)
                mix_grad[values, toks] = mm_nt(incoming, chances).astype(bf16)
                mix_grad[heads, toks] = (mm(mix_ring[slot, keys, toks], score_grad) * factor).astype(bf16)
                mix_grad[keys, toks] = (mm_nt(mix_ring[slot, heads, toks], score_grad) * factor).astype(bf16)
        g_qkv[...] += mm_nt(mix_grad[...], x_ring[slot])
        grad_in[...] = mm(wqkv[...], mix_grad[...]) + rog_ring[lax.rem(r, rog_ring.shape[0])]
        base = 6 * local + hidden_units
        for n, start in ((0, 0), (1, 2 * local)):
            chunk = mix_grad[start : start + local, lanes[0]].astype(f32)
            for s in lanes[1:]:
                chunk += mix_grad[start : start + local, s].astype(f32)
            sums[base + n * local : base + (n + 1) * local, :] += chunk

    def stage_feed_back(r):
        stat_ready(stat_two, TWO, r)
        for k, s in enumerate(lanes):
            row = lambda p, n: stat_two[r, p, n * parts + k : n * parts + k + 1, :]
            means = [row(p, 0) for p in range(groups)]
            center = sum(means[1:], means[0]) * (1.0 / groups)
            spread, first, second = row(0, 1), row(0, 2), row(0, 3)
            for p in range(1, groups):
                spread += row(p, 1)
                first += row(p, 2)
                second += row(p, 3)
            for p, mean in enumerate(means):
                spread += local * (mean - center) * (mean - center)
                second += (mean - center) * row(p, 2)
            inverse = lax.rsqrt(spread * (1.0 / channels) + eps)
            first = first * (1.0 / channels)
            second = second * inverse * (1.0 / channels)
            normed = (x_two[:, s] - center) * inverse
            result[:, s] = (normed * col(GAIN2) + col(SHIFT2)).astype(bf16)
            up = upstream[:, s]
            back = inverse * (up * col(GAIN2) - first - normed * second)
            rtg[:, s] = back
            low = back.astype(bf16)
            br_low[:, s] = low
            accumulate(S_GAIN2, up * normed)
            accumulate(S_SHIFT2, up)
            accumulate(S_BDOWN, low.astype(f32))
        pre[...] = mm(wdown[...], br_low[...])
        g_down[...] += mm_nt(act[...], br_low[...])
        base = 6 * local
        for j in range(hidden_units // local):
            units = slice(j * local, (j + 1) * local)
            for s in lanes:
                low = (slope[units, s] * pre[units, s]).astype(bf16)
                pre_low[units, s] = low
                sums[base + j * local : base + (j + 1) * local, :] += low.astype(f32)
        g_up[...] += mm_nt(pre_low[...], hid_low[...])
        change = mm(wup[...], pre_low[...])
        for k, s in enumerate(lanes):
            total = rtg[:, s] + change[:, s]
            hid_grad[:, s] = total
            normed = n_one[lax.rem(r, 2), :, s]
            scaled = total * col(GAIN1)
            sum_one[r, g, k : k + 1, :] = row_sum(scaled)
            sum_one[r, g, parts + k : parts + k + 1, :] = row_sum(scaled * normed)
            accumulate(S_GAIN1, total * normed)
            accumulate(S_SHIFT1, total)
        send_stat(sum_one, BACK, r)

    def at(delay, stage):
        r = i - delay

        @pl.when(jnp.logical_and(r >= 0, r < rows))
        def _():
            stage(r)

    at(5, stage_norm_back)
    at(4, stage_feed_back)
    at(DELAY, stage_attend_back)
    at(3, stage_feed)
    at(2, stage_residual)
    at(0, stage_attend)
    at(1, lambda r: pass_on(ctx_all, CTX, r))
    at(6, lambda r: pass_on(att_all, ATT, r))

    @pl.when(i == rows - 1 + 4)
    def _():
        for which in range(4):
            each_peer(lambda k, which=which: weight_copy(which, k, d).wait_send())
        for offset in range(1, groups):
            rows_copy(offset, g, lax.rem(g + offset, groups)).wait_send()
        send_grad(UP, g_up[...].T)
        send_grad(DOWN, g_down[...])

    @pl.when(i == rows - 1 + 5)
    def _():
        send_grad(OUT, g_out[...])

    @pl.when(i == steps - 1)
    def _():
        send_grad(QKV, g_qkv[...].T)
        mine = all_sums.at[d]
        for n in range(6):
            mine[n : n + 1, :local] = row_sum(sums[n * local : (n + 1) * local, :].T)
        base = 6 * local
        mine[6:7, :] = row_sum(sums[base : base + hidden_units, :].T)
        base += hidden_units
        mine[7:8, : 2 * local] = row_sum(sums[base : base + 2 * local, :].T)
        each_peer(lambda k: sums_copy(k, d).start())
        for which, out in ((UP, o_up), (DOWN, o_down), (OUT, o_out), (QKV, o_qkv)):
            grad_sum(which, out)
        each_peer(lambda k: sums_copy(k, lax.rem(d - k + dp, dp)).wait())
        o_sums[...] = jnp.sum(all_sums[...], axis=0)

        def drain(r, carry):
            blocks_sent(ctx_all, CTX, r)
            blocks_sent(att_all, ATT, r)
            stat_sent(stat_one, ONE, r)
            stat_sent(stat_two, TWO, r)
            stat_sent(sum_one, BACK, r)
            return carry

        lax.fori_loop(0, rows, drain, 0)


def run_layer(place, inputs, grad_out, shards, b_qkv, b_up, cols):
    groups = lax.axis_size("group")
    dp = lax.axis_size("dp")
    local, tok_count = inputs.shape
    rows = place.shape[0]
    channels = groups * local
    seq = tok_count // rows
    half = seq // SPLIT
    parts = seq // LANES
    units = b_up.shape[0]
    last = rows - 1
    ring = DELAY
    vmem = pl.BlockSpec(memory_space=pltpu.VMEM)

    def rows_at(delay):
        return pl.BlockSpec((local, seq), lambda i: (0, jnp.clip(i - delay, 0, last)))

    def whole(shape):
        return pl.BlockSpec(shape, lambda i: (0,) * len(shape))

    acc_shapes = ((3 * local, local), (groups * local, local), (units, local), (units, local))
    sums_shape = (6 * local + units + 2 * local, LANES)
    shard_shapes = tuple(w.shape for w in shards)
    slots = tuple((dp, *s) for s in shard_shapes)
    row_sums = (8, units)
    block = (rows, groups, local, seq)
    return pl.pallas_call(
        functools.partial(layer_kernel, rows, groups, dp),
        grid=(rows + DELAY,),
        out_shape=(
            jax.ShapeDtypeStruct((local, tok_count), bf16),
            jax.ShapeDtypeStruct((local, tok_count), f32),
            *(jax.ShapeDtypeStruct(s, f32) for s in shard_shapes),
            jax.ShapeDtypeStruct(row_sums, f32),
        ),
        in_specs=[
            pl.BlockSpec(memory_space=pltpu.SMEM),
            rows_at(0),
            rows_at(3),
            *([vmem] * (len(shards) + 3)),
        ],
        out_specs=(
            rows_at(4),
            rows_at(DELAY),
            *(whole(s) for s in shard_shapes),
            whole(row_sums),
        ),
        scratch_shapes=[
            pltpu.VMEM((3 * local, local), bf16),
            pltpu.VMEM((local, 3 * local), bf16),
            pltpu.VMEM((local, channels), bf16),
            pltpu.VMEM((local, channels), bf16),
            pltpu.VMEM((units, local), bf16),
            pltpu.VMEM((local, units), bf16),
            pltpu.VMEM((local, units), bf16),
            pltpu.VMEM((units, local), bf16),
            *(pltpu.VMEM(s, bf16) for s in slots),
            pltpu.VMEM((groups, dp // groups, *shard_shapes[1]), bf16),
            pltpu.VMEM((local, units), f32),
            pltpu.VMEM((units, local), f32),
            *(pltpu.VMEM(s, f32) for s in acc_shapes),
            pltpu.VMEM(sums_shape, f32),
            *(pltpu.VMEM(s, bf16) for s in slots),
            pltpu.VMEM((dp, *row_sums), f32),
            pltpu.VMEM(block, bf16),
            pltpu.VMEM(block, bf16),
            pltpu.VMEM((rows, groups, 2 * parts, LANES), f32),
            pltpu.VMEM((rows, groups, 4 * parts, LANES), f32),
            pltpu.VMEM((rows, groups, 2 * parts, LANES), f32),
            pltpu.VMEM((ring, local, seq), bf16),
            pltpu.VMEM((ring, 3 * local, seq), bf16),
            pltpu.VMEM((ring, HG * SPLIT, half, half), bf16),
            pltpu.VMEM((half, half), f32),
            pltpu.VMEM((local, seq), f32),
            pltpu.VMEM((2, local, seq), f32),
            pltpu.VMEM((2, parts, LANES), f32),
            pltpu.VMEM((local, seq), f32),
            pltpu.VMEM((local, seq), bf16),
            pltpu.VMEM((units, seq), f32),
            pltpu.VMEM((units, seq), bf16),
            pltpu.VMEM((units, seq), f32),
            pltpu.VMEM((local, seq), f32),
            pltpu.VMEM((local, seq), f32),
            pltpu.VMEM((local, seq), f32),
            pltpu.VMEM((local, seq), bf16),
            pltpu.VMEM((units, seq), bf16),
            pltpu.VMEM((local, seq), f32),
            pltpu.VMEM((3, local, seq), f32),
            pltpu.VMEM((local, seq), bf16),
            pltpu.VMEM((3 * local, seq), bf16),
            pltpu.SemaphoreType.DMA((6, rows)),
            pltpu.SemaphoreType.DMA((6, rows)),
            pltpu.SemaphoreType.DMA((3 * (groups - 1), rows)),
            pltpu.SemaphoreType.DMA((3 * (groups - 1), rows)),
            pltpu.SemaphoreType.DMA((4, dp)),
            pltpu.SemaphoreType.DMA((4, dp)),
            pltpu.SemaphoreType.DMA((groups - 1,)),
            pltpu.SemaphoreType.DMA((groups - 1,)),
            pltpu.SemaphoreType.DMA((5, dp)),
            pltpu.SemaphoreType.DMA((5, dp)),
        ],
        compiler_params=pltpu.CompilerParams(
            collective_id=0, has_side_effects=True, vmem_limit_bytes=63 << 20
        ),
        name="layer",
    )(place, inputs, grad_out, *shards, b_qkv, b_up, cols)


def prepare_kernel(labels, b_qv, b_up, b_out, gain_one, shift_one, b_down, gain_two, shift_two, place, o_qkv, o_up, o_cols):
    rows, seq = labels.shape
    half = seq // SPLIT
    local = b_out.shape[1]
    ids = labels[...]
    counts = [
        jnp.sum(jnp.where(ids == v, 1.0, 0.0), axis=1, keepdims=True) for v in range(4)
    ]
    start = jnp.zeros_like(counts[0])
    first = jnp.zeros_like(start)
    second = jnp.zeros_like(start)
    found = jnp.zeros_like(start)
    begin = jnp.zeros_like(start)
    for v in range(4):
        hit = jnp.where(counts[v] == half, 1.0 - found, 0.0)
        start = start + hit * begin
        first = first + hit * counts[(v + 1) % 4]
        second = second + hit * (counts[(v + 1) % 4] + counts[(v + 2) % 4])
        found = found + hit
        begin = begin + counts[v]
    turn = jnp.where(start == 0.0, 0.0, seq - start)
    lane = lax.broadcasted_iota(jnp.int32, (rows, LANES), 1)
    table = jnp.zeros((rows, LANES), f32)
    for n, value in enumerate((turn, start, first, second)):
        table = jnp.where(lane == n, value, table)
    place[...] = table.astype(jnp.int32)

    def column(row):
        return jnp.broadcast_to(row, (LANES, row.shape[1])).T

    o_qkv[:local, :] = column(b_qv[:, :local])
    o_qkv[local : 2 * local, :] = jnp.zeros((local, LANES), f32)
    o_qkv[2 * local :, :] = column(b_qv[...])[local:, :]
    o_up[...] = column(b_up[...])
    for n, ref in enumerate((b_out, gain_one, shift_one, b_down, gain_two, shift_two)):
        o_cols[n * local : (n + 1) * local, :] = column(ref[...])


def prepare(labels, b_qv, b_up, *vectors):
    local = vectors[0].shape[-1]
    vmem = pl.BlockSpec(memory_space=pltpu.VMEM)
    return pl.pallas_call(
        prepare_kernel,
        out_shape=(
            jax.ShapeDtypeStruct((labels.shape[0], LANES), jnp.int32),
            jax.ShapeDtypeStruct((3 * local, LANES), f32),
            jax.ShapeDtypeStruct((b_up.shape[1], LANES), f32),
            jax.ShapeDtypeStruct((6 * local, LANES), f32),
        ),
        in_specs=[vmem] * (3 + len(vectors)),
        out_specs=(vmem,) * 4,
        name="prepare",
    )(labels, b_qv, b_up, *(v.reshape(1, local) for v in vectors))


def finish_kernel(place, result, grad_in, qkv, out, up, down, sums, *outs):
    i = pl.program_id(0)
    outs[0][...] = pltpu.roll(result[...].astype(f32), place[i, 1], 1).astype(bf16)
    outs[1][...] = pltpu.roll(grad_in[...], place[i, 1], 1)

    @pl.when(i == 0)
    def _():
        local = result.shape[0]
        for target, source in zip(outs[2:6], (qkv, out, up, down)):
            target[...] = source[...]
        for n in range(6):
            outs[6 + n][...] = sums[n : n + 1, :local]
        outs[12][...] = sums[6:7, :]
        outs[13][...] = sums[7:8, : 2 * local]


def finish(place, result, grad_in, *small):
    local, tok_count = result.shape
    rows = place.shape[0]
    seq = tok_count // rows
    units = small[4].shape[1]
    block = pl.BlockSpec((local, seq), lambda i: (0, i))
    vmem = pl.BlockSpec(memory_space=pltpu.VMEM)
    shapes = (*(s.shape for s in small[:4]), *((1, local),) * 6, (1, units), (1, 2 * local))
    return pl.pallas_call(
        finish_kernel,
        grid=(rows,),
        out_shape=(
            jax.ShapeDtypeStruct(result.shape, bf16),
            jax.ShapeDtypeStruct(grad_in.shape, f32),
            *(jax.ShapeDtypeStruct(s, f32) for s in shapes),
        ),
        in_specs=[pl.BlockSpec(memory_space=pltpu.SMEM), block, block, *[vmem] * 5],
        out_specs=(block, block, *(vmem,) * len(shapes)),
        name="finish",
    )(place, result, grad_in, *small)


def per_device(
    inputs,
    labels,
    w_qkv,
    b_qv,
    w_out,
    b_out,
    gain_one,
    shift_one,
    w_up,
    b_up,
    down_weight,
    down_bias,
    gain_two,
    shift_two,
    grad_out,
):
    place, qkv_col, up_col, cols = prepare(
        labels, b_qv, b_up, b_out, gain_one, shift_one, down_bias, gain_two, shift_two
    )
    shards = (w_qkv[0], w_out, w_up[0], down_weight[0])
    raw = run_layer(place, inputs, grad_out, shards, qkv_col, up_col, cols)
    result, input_grad, qkv, out, up, down, *sums = finish(place, *raw)
    flat = [s.reshape(-1) for s in sums]
    return (
        result,
        input_grad,
        qkv[None],
        sums[7],
        out,
        flat[0],
        flat[1],
        flat[2],
        up[None],
        sums[6],
        down[None],
        sums[3],
        flat[4],
        flat[5],
    )


def solution(mesh):
    placed = (
        P("group", "dp"),
        P("dp", None),
        P("group", "dp", None),
        P("group", None),
        P("dp", "group"),
        P("group"),
        P("group"),
        P("group"),
        P("group", "dp", None),
        P("group", None),
        P("group", "dp", None),
        P("group", None),
        P("group"),
        P("group"),
        P("group", "dp"),
    )
    return jax.shard_map(
        per_device,
        mesh=mesh,
        in_specs=placed,
        out_specs=(
            P("group", "dp"),
            P("group", "dp"),
            P("group", "dp", None),
            P("group", None),
            P("dp", "group"),
            P("group"),
            P("group"),
            P("group"),
            P("group", "dp", None),
            P("group", None),
            P("group", "dp", None),
            P("group", None),
            P("group"),
            P("group"),
        ),
        check_vma=False,
    )
```

```python
import functools
import math

import jax
import jax.numpy as jnp
from jax import lax
from jax.experimental import pallas as pl
from jax.experimental.pallas import tpu as pltpu
from jax.sharding import PartitionSpec as P

HD = 64
HG = 3
LANES = 128
SPLIT = 2
FINISH_ROWS = 4
PASS_CTX, RESIDUAL, FEED, FEED_BACK, NORM_BACK, PASS_ATT, DELAY = 1, 4, 5, 6, 7, 8, 9
CTX_SLOTS, ATT_SLOTS = DELAY + 1, 4

eps = 1e-12
f32 = jnp.float32
bf16 = jnp.bfloat16
MESH = pl.DeviceIdType.MESH


def mm(left, right):
    return jnp.dot(left, right, preferred_element_type=f32)


def mm_nt(left, right):
    return lax.dot_general(left, right, (((1,), (1,)), ((), ())), preferred_element_type=f32)


def mm_tn(left, right):
    return lax.dot_general(left, right, (((0,), (0,)), ((), ())), preferred_element_type=f32)


def packed_rows(count, width):
    tail = 0 if width % LANES == 0 else count // (2 - count % 2)
    return -(-(width // LANES * count + tail) // 16) * 16


def pack(into, x):
    count, width = x.shape
    whole = width // LANES
    for k in range(whole):
        into[k * count : (k + 1) * count, :] = x[:, k * LANES : (k + 1) * LANES]
    if width % LANES:
        left = width - whole * LANES
        folds = 2 - count % 2
        part = count // folds
        for n in range(folds):
            into[whole * count : whole * count + part, n * left : (n + 1) * left] = x[
                n * part : (n + 1) * part, whole * LANES :
            ]


def unpack(into, start, count, width, x):
    whole = width // LANES
    for k in range(whole):
        into[start : start + count, k * LANES : (k + 1) * LANES] = x[k * count : (k + 1) * count, :]
    if width % LANES:
        left = width - whole * LANES
        folds = 2 - count % 2
        part = count // folds
        for n in range(folds):
            into[start + n * part : start + (n + 1) * part, whole * LANES : width] = x[
                whole * count : whole * count + part, n * left : (n + 1) * left
            ]


def row_sum(x):
    return jnp.sum(x, axis=0, keepdims=True)


def remote(src, dst, send, recv, device):
    return pltpu.make_async_remote_copy(
        src_ref=src, dst_ref=dst, send_sem=send, recv_sem=recv, device_id=device, device_id_type=MESH
    )


def layer_kernel(
    rows,
    groups,
    dp,
    place,
    inp,
    gout_in,
    w_qkv,
    w_out,
    w_up,
    w_down,
    b_qkv,
    b_up,
    cols,
    result,
    grad_in,
    o_qkv,
    o_out,
    o_up,
    o_down,
    o_sums,
    wqkv_t,
    wqkv,
    wout_t,
    wout_rows,
    wup_t,
    wup,
    wdown_t,
    wdown,
    all_qkv,
    all_out,
    all_up,
    all_down,
    out_rows,
    wide_mat,
    tall_mat,
    g_qkv,
    g_out,
    g_up,
    g_down,
    sums,
    flat,
    land_qkv,
    land_out,
    land_up,
    land_down,
    all_sums,
    ctx_all,
    att_all,
    stats,
    x_ring,
    mix_ring,
    prob_ring,
    mask,
    x_one,
    n_one,
    inv_one,
    hid,
    hid_low,
    pre,
    act,
    slope,
    x_two,
    upstream,
    rtg,
    br_low,
    pre_low,
    hid_grad,
    rog_ring,
    ctx_grad,
    mix_grad,
    send_blocks,
    recv_blocks,
    send_stats,
    recv_stats,
    send_weights,
    recv_weights,
    send_rows,
    recv_rows,
    send_grads,
    recv_grads,
):
    i = pl.program_id(0)
    steps = pl.num_programs(0)
    g = lax.axis_index("group")
    d = lax.axis_index("dp")
    across = lax.rem(g + 2, groups)
    beside = g + 1 - 2 * lax.rem(g, 2)
    corner = lax.rem(beside + 2, groups)
    local, seq = inp.shape
    half = seq // SPLIT
    channels = local * groups
    parts = seq // LANES
    hidden_units = wup_t.shape[0]
    ring = x_ring.shape[0]
    lanes = [slice(k * LANES, (k + 1) * LANES) for k in range(parts)]
    col = lambda n: cols[n * local : (n + 1) * local, :]
    B_OUT, GAIN1, SHIFT1, B_DOWN, GAIN2, SHIFT2 = range(6)
    S_BOUT, S_GAIN1, S_SHIFT1, S_BDOWN, S_GAIN2, S_SHIFT2 = range(6)

    def accumulate(slot, chunk):
        sums[slot * local : (slot + 1) * local, :] += chunk

    def block_copy(buf, base, kind, r, slot):
        peer = across if kind == 0 else beside
        at_row = lax.rem(r, buf.shape[0])
        return remote(
            buf.at[at_row, slot],
            buf.at[at_row, slot],
            send_blocks.at[base + kind, r],
            recv_blocks.at[base + kind, r],
            {"group": peer},
        )

    def send_own(buf, base, r):
        block_copy(buf, base, 0, r, g).start()
        block_copy(buf, base, 1, r, g).start()

    def pass_on(buf, base, r):
        block_copy(buf, base, 0, r, across).wait_recv()
        block_copy(buf, base, 2, r, across).start()

    def blocks_ready(buf, base, r):
        block_copy(buf, base, 1, r, beside).wait_recv()
        block_copy(buf, base, 2, r, corner).wait_recv()

    def blocks_sent(buf, base, r):
        block_copy(buf, base, 0, r, g).wait_send()
        block_copy(buf, base, 1, r, g).wait_send()
        block_copy(buf, base, 2, r, across).wait_send()

    def stat_copy(step, offset, slot):
        return remote(
            stats.at[step, slot],
            stats.at[step, slot],
            send_stats.at[offset - 1, step],
            recv_stats.at[offset - 1, step],
            {"group": lax.rem(g + offset, groups)},
        )

    def stats_send():
        for offset in range(1, groups):
            stat_copy(i, offset, g).start()

    def stats_ready():
        for offset in range(1, groups):
            stat_copy(i - 1, offset, lax.rem(g + groups - offset, groups)).wait_recv()
            stat_copy(i - 1, offset, g).wait_send()

    def put_stat(first, k, value):
        stats[i, g, first + k : first + k + 1, :] = value

    def get_stat(first, k, p):
        return stats[i - 1, p, first + k : first + k + 1, :]

    ONE, TWO, BACK = 0, 2 * parts, 6 * parts
    CTX, ATT = 0, 3

    shards = (w_qkv, w_out, w_up, w_down)
    fulls = (all_qkv, all_out, all_up, all_down)
    QKV, OUT, UP, DOWN = range(4)

    def weight_copy(which, k, slot):
        full = fulls[which]
        return remote(
            full.at[slot],
            full.at[slot],
            send_weights.at[which, k],
            recv_weights.at[which, k],
            {"dp": lax.rem(d + k, dp)},
        )

    def each_peer(action):
        def body(k, carry):
            action(k)
            return carry

        lax.fori_loop(1, dp, body, 0)

    def weights_ready(which, into):
        each_peer(lambda k: weight_copy(which, k, lax.rem(d - k + dp, dp)).wait_recv())
        count, width = shards[which].shape
        for slot in range(dp):
            unpack(into, slot * count, count, width, fulls[which][slot].astype(f32))

    per = dp // groups

    def rows_copy(offset, source, target):
        return remote(
            all_out.at[pl.ds(target * per, per)],
            out_rows.at[source],
            send_rows.at[offset - 1],
            recv_rows.at[offset - 1],
            {"group": target},
        )

    @pl.when(i == 0)
    def _():
        barrier = pltpu.get_barrier_semaphore()
        for offset in range(1, groups):
            pl.semaphore_signal(
                barrier, inc=1, device_id={"group": lax.rem(g + offset, groups)}, device_id_type=MESH
            )
        each_peer(
            lambda k: pl.semaphore_signal(
                barrier, inc=1, device_id={"dp": lax.rem(d + k, dp)}, device_id_type=MESH
            )
        )
        flat[...] = jnp.zeros_like(flat)
        for shard, full in zip(shards, fulls):
            pack(flat, shard[...])
            full[d] = flat[: full.shape[1], :].astype(bf16)
        pl.semaphore_wait(barrier, groups - 1 + dp - 1)
        each_peer(lambda k: weight_copy(QKV, k, d).start())
        for ref in (g_qkv, g_out, g_up, g_down, sums):
            ref[...] = jnp.zeros_like(ref)
        weights_ready(QKV, wide_mat)
        for which in (OUT, UP, DOWN):
            each_peer(lambda k, which=which: weight_copy(which, k, d).start())
        mat = wide_mat[:, : 3 * local]
        wqkv[...] = mat.astype(bf16)
        wqkv_t[...] = mat.T.astype(bf16)

    @pl.when(i == RESIDUAL)
    def _():
        weights_ready(OUT, tall_mat)
        for offset in range(1, groups):
            rows_copy(offset, g, lax.rem(g + offset, groups)).start()
        out_rows[g] = all_out[pl.ds(g * per, per)]
        wout_t[...] = tall_mat[...].T.astype(bf16)

    @pl.when(i == FEED)
    def _():
        weights_ready(UP, wide_mat)
        mat = wide_mat[...]
        wup[...] = mat.astype(bf16)
        wup_t[...] = mat.T.astype(bf16)
        weights_ready(DOWN, tall_mat)
        mat = tall_mat[...]
        wdown[...] = mat.astype(bf16)
        wdown_t[...] = mat.T.astype(bf16)

    @pl.when(i == DELAY)
    def _():
        for offset in range(1, groups):
            rows_copy(offset, lax.rem(g + groups - offset, groups), g).wait_recv()
        count = local // per
        for p in range(groups):
            for n in range(per):
                unpack(wide_mat, n * count, count, local, out_rows[p, n].astype(f32))
            tall_mat[p * local : (p + 1) * local, :] = wide_mat[:, :local].T
        wout_rows[...] = tall_mat[...].T.astype(bf16)

    stages = fulls
    lands = (land_qkv, land_out, land_up, land_down)

    def grad_copy(which, k, slot):
        return remote(
            stages[which].at[lax.rem(d + k, dp)],
            lands[which].at[slot],
            send_grads.at[which, k],
            recv_grads.at[which, k],
            {"dp": lax.rem(d + k, dp)},
        )

    def sums_copy(k, slot):
        return remote(
            all_sums.at[slot],
            all_sums.at[slot],
            send_grads.at[4, k],
            recv_grads.at[4, k],
            {"dp": lax.rem(d + k, dp)},
        )

    def send_grad(which, mat):
        stage = stages[which]
        count = shards[which].shape[0]
        for slot in range(dp):
            pack(flat, mat[slot * count : (slot + 1) * count])
            stage[slot] = flat[: stage.shape[1], :].astype(bf16)
        each_peer(lambda k: grad_copy(which, k, d).start())

    def grad_sum(which, out):
        count = stages[which].shape[1]
        flat[:count, :] = stages[which][d].astype(f32)

        def add(k):
            slot = lax.rem(d - k + dp, dp)
            grad_copy(which, k, slot).wait()
            flat[:count, :] += lands[which][slot].astype(f32)

        each_peer(add)
        unpack(out, 0, *out.shape, flat[...])

    def stage_residual(r):
        blocks_ready(ctx_all, CTX, r)
        attended = mm(wout_t[...], ctx_all[lax.rem(r, CTX_SLOTS)].reshape(channels, seq))
        xr = x_ring.at[lax.rem(r, ring)]
        for k, s in enumerate(lanes):
            x = xr[:, s].astype(f32) + attended[:, s] + col(B_OUT)
            x_one[:, s] = x
            mean = row_sum(x) * (1.0 / local)
            off = x - mean
            put_stat(ONE, k, mean)
            put_stat(ONE + parts, k, row_sum(off * off))
        blocks_sent(ctx_all, CTX, r)

    def stage_attend(r):
        slot = lax.rem(r, ring)
        rolled = pltpu.roll(inp[...].astype(f32), place[r, 0], 1).astype(bf16)
        x_ring[slot] = rolled
        mixed = mm(wqkv_t[...], rolled)
        for s in lanes:
            mix_ring[slot, :, s] = (mixed[:, s] + b_qkv[...]).astype(bf16)
        first, second = place[r, 2], place[r, 3]
        down = lax.broadcasted_iota(jnp.int32, (half, half), 0)
        along = lax.broadcasted_iota(jnp.int32, (half, half), 1)
        own = lambda at: (at >= first).astype(jnp.int32) + (at >= second).astype(jnp.int32)
        mask[...] = jnp.where(own(down) == own(along), 0.0, -1000000000.0)
        scale = math.log2(math.e) / math.sqrt(HD)
        blocks = [(h, b) for h in range(HG) for b in range(SPLIT)]

        def piece(part, n):
            h, b = blocks[n]
            start = part * local + h * HD
            return mix_ring[slot, start : start + HD, b * half : (b + 1) * half]

        def score(n):
            return mm_tn(piece(1, n), piece(0, n))

        def soften(n, scores):
            if blocks[n][1]:
                scores = scores + mask[...]
            highest = jnp.max(scores, axis=0, keepdims=True)
            return jnp.exp2((scores - highest) * scale)

        def norm(n, exponent):
            chances = (exponent * (1.0 / row_sum(exponent))).astype(bf16)
            prob_ring[slot, n] = chances
            return chances

        def blend(n, chances):
            h, b = blocks[n]
            ctx_all[lax.rem(r, CTX_SLOTS), g, h * HD : (h + 1) * HD, b * half : (b + 1) * half] = mm(
                piece(2, n), chances
            ).astype(bf16)

        held = {}
        for step in range(len(blocks) + 3):
            n = step - 0
            if 0 <= n < len(blocks):
                held[0, n] = score(n)
            n = step - 1
            if 0 <= n < len(blocks):
                held[1, n] = soften(n, held.pop((0, n)))
            n = step - 2
            if 0 <= n < len(blocks):
                held[2, n] = norm(n, held.pop((1, n)))
            n = step - 3
            if 0 <= n < len(blocks):
                blend(n, held.pop((2, n)))
        send_own(ctx_all, CTX, r)

    def stage_norm_back(r):
        slot = lax.rem(r, rog_ring.shape[0])
        two = lax.rem(r, 2)
        for k, s in enumerate(lanes):
            first = get_stat(BACK, k, 0)
            second = get_stat(BACK + parts, k, 0)
            for p in range(1, groups):
                first += get_stat(BACK, k, p)
                second += get_stat(BACK + parts, k, p)
            first = first * (1.0 / channels)
            second = second * (1.0 / channels)
            scaled = hid_grad[:, s] * col(GAIN1)
            back = inv_one[two, k : k + 1, :] * (scaled - first - n_one[two, :, s] * second)
            rog_ring[slot, :, s] = back
            low = back.astype(bf16)
            att_all[lax.rem(r, ATT_SLOTS), g, :, s] = low
            accumulate(S_BOUT, low.astype(f32))
        send_own(att_all, ATT, r)
        contexts = ctx_all[lax.rem(r, CTX_SLOTS)].reshape(channels, seq)
        g_out[...] += mm_nt(contexts, att_all[lax.rem(r, ATT_SLOTS), g])

    def stage_feed(r):
        two = lax.rem(r, 2)
        for k, s in enumerate(lanes):
            means = [get_stat(ONE, k, p) for p in range(groups)]
            center = sum(means[1:], means[0]) * (1.0 / groups)
            spread = get_stat(ONE + parts, k, 0)
            for p in range(1, groups):
                spread += get_stat(ONE + parts, k, p)
            for mean in means:
                spread += local * (mean - center) * (mean - center)
            inverse = lax.rsqrt(spread * (1.0 / channels) + eps)
            inv_one[two, k : k + 1, :] = inverse
            normed = (x_one[:, s] - center) * inverse
            n_one[two, :, s] = normed
            h = normed * col(GAIN1) + col(SHIFT1)
            hid[:, s] = h
            hid_low[:, s] = h.astype(bf16)
        pre[...] = mm(wup_t[...], hid_low[...])
        for j in range(hidden_units // local):
            units = slice(j * local, (j + 1) * local)
            for s in lanes:
                u = pre[units, s] + b_up[units, :]
                cdf = 0.5 + 0.5 * lax.erf(u * math.sqrt(0.5))
                act[units, s] = (u * cdf).astype(bf16)
                bell = jnp.exp2(u * u * (-0.5 * math.log2(math.e))) * (1.0 / math.sqrt(2.0 * math.pi))
                slope[units, s] = cdf + u * bell
        branch = mm(wdown_t[...], act[...])
        upstream[...] = pltpu.roll(gout_in[...].astype(f32), place[r, 0], 1)
        for k, s in enumerate(lanes):
            x = hid[:, s] + branch[:, s] + col(B_DOWN)
            x_two[:, s] = x
            mean = row_sum(x) * (1.0 / local)
            off = x - mean
            scaled = upstream[:, s] * col(GAIN2)
            tile = (mean, row_sum(off * off), row_sum(scaled), row_sum(scaled * off))
            for n, value in enumerate(tile):
                put_stat(TWO + n * parts, k, value)

    def stage_attend_back(r):
        slot = lax.rem(r, ring)
        blocks_ready(att_all, ATT, r)
        ctx_grad[...] = mm(
            wout_rows[...], att_all[lax.rem(r, ATT_SLOTS)].reshape(channels, seq)
        ).astype(bf16)
        factor = 1.0 / math.sqrt(HD)
        blocks = [(h, b) for h in range(HG) for b in range(SPLIT)]

        def at_block(part, n):
            h, b = blocks[n]
            start = part * local + h * HD
            return slice(start, start + HD), slice(b * half, (b + 1) * half)

        def piece(part, n):
            return mix_ring[slot, *at_block(part, n)]

        def spread(n):
            incoming = ctx_grad[at_block(0, n)]
            mix_grad[at_block(2, n)] = mm_nt(incoming, prob_ring[slot, n]).astype(bf16)

        def open_up(n):
            return mm_tn(piece(2, n), ctx_grad[at_block(0, n)])

        def center(n, prob_grad):
            at_n = at_block(0, n)
            inner = row_sum(ctx_grad[at_n].astype(f32) * ctx_all[lax.rem(r, CTX_SLOTS), g, *at_n].astype(f32))
            return (prob_ring[slot, n].astype(f32) * (prob_grad - inner)).astype(bf16)

        def queries(n, score_grad):
            mix_grad[at_block(0, n)] = (mm(piece(1, n), score_grad) * factor).astype(bf16)

        def keys(n, score_grad):
            mix_grad[at_block(1, n)] = (mm_nt(piece(0, n), score_grad) * factor).astype(bf16)

        held = {}
        for step in range(len(blocks) + 2):
            n = step - 0
            if 0 <= n < len(blocks):
                held[0, n] = open_up(n)
            n = step - 0
            if 0 <= n < len(blocks):
                spread(n)
            n = step - 1
            if 0 <= n < len(blocks):
                held[1, n] = center(n, held.pop((0, n)))
            n = step - 2
            if 0 <= n < len(blocks):
                queries(n, held[1, n])
            n = step - 2
            if 0 <= n < len(blocks):
                keys(n, held.pop((1, n)))
        g_qkv[...] += mm_nt(mix_grad[...], x_ring[slot])
        blocks_sent(att_all, ATT, r)
        grad_in[...] = mm(wqkv[...], mix_grad[...]) + rog_ring[lax.rem(r, rog_ring.shape[0])]
        base = 6 * local + hidden_units
        for n, start in ((0, 0), (1, 2 * local)):
            chunk = mix_grad[start : start + local, lanes[0]].astype(f32)
            for s in lanes[1:]:
                chunk += mix_grad[start : start + local, s].astype(f32)
            sums[base + n * local : base + (n + 1) * local, :] += chunk

    def stage_feed_back(r):
        for k, s in enumerate(lanes):
            row = lambda p, n: get_stat(TWO + n * parts, k, p)
            means = [row(p, 0) for p in range(groups)]
            center = sum(means[1:], means[0]) * (1.0 / groups)
            spread, first, second = row(0, 1), row(0, 2), row(0, 3)
            for p in range(1, groups):
                spread += row(p, 1)
                first += row(p, 2)
                second += row(p, 3)
            for p, mean in enumerate(means):
                spread += local * (mean - center) * (mean - center)
                second += (mean - center) * row(p, 2)
            inverse = lax.rsqrt(spread * (1.0 / channels) + eps)
            first = first * (1.0 / channels)
            second = second * inverse * (1.0 / channels)
            normed = (x_two[:, s] - center) * inverse
            result[:, s] = (normed * col(GAIN2) + col(SHIFT2)).astype(bf16)
            up = upstream[:, s]
            back = inverse * (up * col(GAIN2) - first - normed * second)
            rtg[:, s] = back
            low = back.astype(bf16)
            br_low[:, s] = low
            accumulate(S_GAIN2, up * normed)
            accumulate(S_SHIFT2, up)
            accumulate(S_BDOWN, low.astype(f32))
        pre[...] = mm(wdown[...], br_low[...])
        g_down[...] += mm_nt(act[...], br_low[...])
        base = 6 * local
        for j in range(hidden_units // local):
            units = slice(j * local, (j + 1) * local)
            for s in lanes:
                low = (slope[units, s] * pre[units, s]).astype(bf16)
                pre_low[units, s] = low
                sums[base + j * local : base + (j + 1) * local, :] += low.astype(f32)
        g_up[...] += mm_nt(pre_low[...], hid_low[...])
        change = mm(wup[...], pre_low[...])
        for k, s in enumerate(lanes):
            total = rtg[:, s] + change[:, s]
            hid_grad[:, s] = total
            normed = n_one[lax.rem(r, 2), :, s]
            scaled = total * col(GAIN1)
            put_stat(BACK, k, row_sum(scaled))
            put_stat(BACK + parts, k, row_sum(scaled * normed))
            accumulate(S_GAIN1, total * normed)
            accumulate(S_SHIFT1, total)

    def at(delay, stage):
        r = i - delay

        @pl.when(jnp.logical_and(r >= 0, r < rows))
        def _():
            stage(r)

    @pl.when(jnp.logical_and(i > RESIDUAL, i <= rows + FEED_BACK))
    def _():
        stats_ready()

    at(NORM_BACK, stage_norm_back)
    at(FEED_BACK, stage_feed_back)
    at(FEED, stage_feed)
    at(RESIDUAL, stage_residual)

    @pl.when(jnp.logical_and(i >= RESIDUAL, i < rows + FEED_BACK))
    def _():
        stats_send()

    at(DELAY, stage_attend_back)
    at(0, stage_attend)
    at(PASS_CTX, lambda r: pass_on(ctx_all, CTX, r))
    at(PASS_ATT, lambda r: pass_on(att_all, ATT, r))

    @pl.when(i == rows - 1 + FEED_BACK)
    def _():
        for which in range(4):
            each_peer(lambda k, which=which: weight_copy(which, k, d).wait_send())
        for offset in range(1, groups):
            rows_copy(offset, g, lax.rem(g + offset, groups)).wait_send()
        send_grad(UP, g_up[...].T)
        send_grad(DOWN, g_down[...])

    @pl.when(i == rows - 1 + NORM_BACK)
    def _():
        send_grad(OUT, g_out[...])

    @pl.when(i == steps - 1)
    def _():
        send_grad(QKV, g_qkv[...].T)
        mine = all_sums.at[d]
        for n in range(6):
            mine[n : n + 1, :local] = row_sum(sums[n * local : (n + 1) * local, :].T)
        base = 6 * local
        mine[6:7, :] = row_sum(sums[base : base + hidden_units, :].T)
        base += hidden_units
        mine[7:8, : 2 * local] = row_sum(sums[base : base + 2 * local, :].T)
        each_peer(lambda k: sums_copy(k, d).start())
        for which, out in ((UP, o_up), (DOWN, o_down), (OUT, o_out), (QKV, o_qkv)):
            grad_sum(which, out)
        each_peer(lambda k: sums_copy(k, lax.rem(d - k + dp, dp)).wait())
        o_sums[...] = jnp.sum(all_sums[...], axis=0)


def run_layer(place, inputs, grad_out, shards, b_qkv, b_up, cols):
    groups = lax.axis_size("group")
    dp = lax.axis_size("dp")
    local, tok_count = inputs.shape
    rows = place.shape[0]
    channels = groups * local
    seq = tok_count // rows
    half = seq // SPLIT
    parts = seq // LANES
    units = b_up.shape[0]
    last = rows - 1
    ring = DELAY
    vmem = pl.BlockSpec(memory_space=pltpu.VMEM)

    def rows_at(delay):
        return pl.BlockSpec((local, seq), lambda i: (0, jnp.clip(i - delay, 0, last)))

    def whole(shape):
        return pl.BlockSpec(shape, lambda i: (0,) * len(shape))

    acc_shapes = ((3 * local, local), (groups * local, local), (units, local), (units, local))
    sums_shape = (6 * local + units + 2 * local, LANES)
    shard_shapes = tuple(w.shape for w in shards)
    slots = tuple((dp, packed_rows(*s), LANES) for s in shard_shapes)
    row_sums = (8, units)
    block = (groups, local, seq)
    return pl.pallas_call(
        functools.partial(layer_kernel, rows, groups, dp),
        grid=(rows + DELAY,),
        out_shape=(
            jax.ShapeDtypeStruct((local, tok_count), bf16),
            jax.ShapeDtypeStruct((local, tok_count), f32),
            *(jax.ShapeDtypeStruct(s, f32) for s in shard_shapes),
            jax.ShapeDtypeStruct(row_sums, f32),
        ),
        in_specs=[
            pl.BlockSpec(memory_space=pltpu.SMEM),
            rows_at(0),
            rows_at(FEED),
            *([vmem] * (len(shards) + 3)),
        ],
        out_specs=(
            rows_at(FEED_BACK),
            rows_at(DELAY),
            *(whole(s) for s in shard_shapes),
            whole(row_sums),
        ),
        scratch_shapes=[
            pltpu.VMEM((3 * local, local), bf16),
            pltpu.VMEM((local, 3 * local), bf16),
            pltpu.VMEM((local, channels), bf16),
            pltpu.VMEM((local, channels), bf16),
            pltpu.VMEM((units, local), bf16),
            pltpu.VMEM((local, units), bf16),
            pltpu.VMEM((local, units), bf16),
            pltpu.VMEM((units, local), bf16),
            *(pltpu.VMEM(s, bf16) for s in slots),
            pltpu.VMEM((groups, dp // groups, *slots[1][1:]), bf16),
            pltpu.VMEM((local, units), f32),
            pltpu.VMEM((units, local), f32),
            *(pltpu.VMEM(s, f32) for s in acc_shapes),
            pltpu.VMEM(sums_shape, f32),
            pltpu.VMEM((max(s[1] for s in slots), LANES), f32),
            *(pltpu.VMEM(s, bf16) for s in slots),
            pltpu.VMEM((dp, *row_sums), f32),
            pltpu.VMEM((CTX_SLOTS, *block), bf16),
            pltpu.VMEM((ATT_SLOTS, *block), bf16),
            pltpu.VMEM((rows + DELAY, groups, 8 * parts, LANES), f32),
            pltpu.VMEM((ring, local, seq), bf16),
            pltpu.VMEM((ring, 3 * local, seq), bf16),
            pltpu.VMEM((ring, HG * SPLIT, half, half), bf16),
            pltpu.VMEM((half, half), f32),
            pltpu.VMEM((local, seq), f32),
            pltpu.VMEM((2, local, seq), f32),
            pltpu.VMEM((2, parts, LANES), f32),
            pltpu.VMEM((local, seq), f32),
            pltpu.VMEM((local, seq), bf16),
            pltpu.VMEM((units, seq), f32),
            pltpu.VMEM((units, seq), bf16),
            pltpu.VMEM((units, seq), f32),
            pltpu.VMEM((local, seq), f32),
            pltpu.VMEM((local, seq), f32),
            pltpu.VMEM((local, seq), f32),
            pltpu.VMEM((local, seq), bf16),
            pltpu.VMEM((units, seq), bf16),
            pltpu.VMEM((local, seq), f32),
            pltpu.VMEM((3, local, seq), f32),
            pltpu.VMEM((local, seq), bf16),
            pltpu.VMEM((3 * local, seq), bf16),
            pltpu.SemaphoreType.DMA((6, rows)),
            pltpu.SemaphoreType.DMA((6, rows)),
            pltpu.SemaphoreType.DMA((groups - 1, rows + DELAY)),
            pltpu.SemaphoreType.DMA((groups - 1, rows + DELAY)),
            pltpu.SemaphoreType.DMA((4, dp)),
            pltpu.SemaphoreType.DMA((4, dp)),
            pltpu.SemaphoreType.DMA((groups - 1,)),
            pltpu.SemaphoreType.DMA((groups - 1,)),
            pltpu.SemaphoreType.DMA((5, dp)),
            pltpu.SemaphoreType.DMA((5, dp)),
        ],
        compiler_params=pltpu.CompilerParams(
            collective_id=0, has_side_effects=True, vmem_limit_bytes=63 << 20
        ),
        name="layer",
    )(place, inputs, grad_out, *shards, b_qkv, b_up, cols)


def prepare_kernel(labels, b_qv, b_up, b_out, gain_one, shift_one, b_down, gain_two, shift_two, place, o_qkv, o_up, o_cols):
    rows, seq = labels.shape
    half = seq // SPLIT
    local = b_out.shape[1]
    ids = labels[...]
    counts = [
        jnp.sum(jnp.where(ids == v, 1.0, 0.0), axis=1, keepdims=True) for v in range(4)
    ]
    start = jnp.zeros_like(counts[0])
    first = jnp.zeros_like(start)
    second = jnp.zeros_like(start)
    found = jnp.zeros_like(start)
    begin = jnp.zeros_like(start)
    for v in range(4):
        hit = jnp.where(counts[v] == half, 1.0 - found, 0.0)
        start = start + hit * begin
        first = first + hit * counts[(v + 1) % 4]
        second = second + hit * (counts[(v + 1) % 4] + counts[(v + 2) % 4])
        found = found + hit
        begin = begin + counts[v]
    turn = jnp.where(start == 0.0, 0.0, seq - start)
    lane = lax.broadcasted_iota(jnp.int32, (rows, LANES), 1)
    table = jnp.zeros((rows, LANES), f32)
    for n, value in enumerate((turn, start, first, second)):
        table = jnp.where(lane == n, value, table)
    place[...] = table.astype(jnp.int32)

    def column(row):
        return jnp.broadcast_to(row, (LANES, row.shape[1])).T

    o_qkv[:local, :] = column(b_qv[:, :local])
    o_qkv[local : 2 * local, :] = jnp.zeros((local, LANES), f32)
    o_qkv[2 * local :, :] = column(b_qv[...])[local:, :]
    o_up[...] = column(b_up[...])
    for n, ref in enumerate((b_out, gain_one, shift_one, b_down, gain_two, shift_two)):
        o_cols[n * local : (n + 1) * local, :] = column(ref[...])


def prepare(labels, b_qv, b_up, *vectors):
    local = vectors[0].shape[-1]
    vmem = pl.BlockSpec(memory_space=pltpu.VMEM)
    return pl.pallas_call(
        prepare_kernel,
        out_shape=(
            jax.ShapeDtypeStruct((labels.shape[0], LANES), jnp.int32),
            jax.ShapeDtypeStruct((3 * local, LANES), f32),
            jax.ShapeDtypeStruct((b_up.shape[1], LANES), f32),
            jax.ShapeDtypeStruct((6 * local, LANES), f32),
        ),
        in_specs=[vmem] * (3 + len(vectors)),
        out_specs=(vmem,) * 4,
        name="prepare",
    )(labels, b_qv, b_up, *(v.reshape(1, local) for v in vectors))


def finish_kernel(many, seq, place, result, grad_in, qkv, out, up, down, sums, *outs):
    i = pl.program_id(0)
    for n in range(many):
        toks = slice(n * seq, (n + 1) * seq)
        turn = place[i * many + n, 1]
        outs[0][:, toks] = pltpu.roll(result[:, toks].astype(f32), turn, 1).astype(bf16)
        outs[1][:, toks] = pltpu.roll(grad_in[:, toks], turn, 1)

    @pl.when(i == 0)
    def _():
        local = result.shape[0]
        for target, source in zip(outs[2:6], (qkv, out, up, down)):
            target[...] = source[...]
        for n in range(6):
            outs[6 + n][...] = sums[n : n + 1, :local]
        outs[12][...] = sums[6:7, :]
        outs[13][...] = sums[7:8, : 2 * local]


def finish(place, result, grad_in, *small):
    local, tok_count = result.shape
    rows = place.shape[0]
    seq = tok_count // rows
    units = small[4].shape[1]
    many = math.gcd(rows, FINISH_ROWS)
    block = pl.BlockSpec((local, many * seq), lambda i: (0, i))
    vmem = pl.BlockSpec(memory_space=pltpu.VMEM)
    shapes = (*(s.shape for s in small[:4]), *((1, local),) * 6, (1, units), (1, 2 * local))
    return pl.pallas_call(
        functools.partial(finish_kernel, many, seq),
        grid=(rows // many,),
        out_shape=(
            jax.ShapeDtypeStruct(result.shape, bf16),
            jax.ShapeDtypeStruct(grad_in.shape, f32),
            *(jax.ShapeDtypeStruct(s, f32) for s in shapes),
        ),
        in_specs=[pl.BlockSpec(memory_space=pltpu.SMEM), block, block, *[vmem] * 5],
        out_specs=(block, block, *(vmem,) * len(shapes)),
        compiler_params=pltpu.CompilerParams(vmem_limit_bytes=48 << 20),
        name="finish",
    )(place, result, grad_in, *small)


def per_device(
    inputs,
    labels,
    w_qkv,
    b_qv,
    w_out,
    b_out,
    gain_one,
    shift_one,
    w_up,
    b_up,
    down_weight,
    down_bias,
    gain_two,
    shift_two,
    grad_out,
):
    place, qkv_col, up_col, cols = prepare(
        labels, b_qv, b_up, b_out, gain_one, shift_one, down_bias, gain_two, shift_two
    )
    shards = (w_qkv[0], w_out, w_up[0], down_weight[0])
    raw = run_layer(place, inputs, grad_out, shards, qkv_col, up_col, cols)
    result, input_grad, qkv, out, up, down, *sums = finish(place, *raw)
    flat = [s.reshape(-1) for s in sums]
    return (
        result,
        input_grad,
        qkv[None],
        sums[7],
        out,
        flat[0],
        flat[1],
        flat[2],
        up[None],
        sums[6],
        down[None],
        sums[3],
        flat[4],
        flat[5],
    )


def solution(mesh):
    placed = (
        P("group", "dp"),
        P("dp", None),
        P("group", "dp", None),
        P("group", None),
        P("dp", "group"),
        P("group"),
        P("group"),
        P("group"),
        P("group", "dp", None),
        P("group", None),
        P("group", "dp", None),
        P("group", None),
        P("group"),
        P("group"),
        P("group", "dp"),
    )
    return jax.shard_map(
        per_device,
        mesh=mesh,
        in_specs=placed,
        out_specs=(
            P("group", "dp"),
            P("group", "dp"),
            P("group", "dp", None),
            P("group", None),
            P("dp", "group"),
            P("group"),
            P("group"),
            P("group"),
            P("group", "dp", None),
            P("group", None),
            P("group", "dp", None),
            P("group", None),
            P("group"),
            P("group"),
        ),
        check_vma=False,
    )
```

```python
import functools
import math

import jax
import jax.numpy as jnp
from jax import lax
from jax.experimental import pallas as pl
from jax.experimental.pallas import tpu as pltpu
from jax.sharding import PartitionSpec as P

HD = 64
HG = 3
LANES = 128
SPLIT = 2
FINISH_ROWS = 4
PASS_CTX, RESIDUAL, FEED, FEED_BACK, NORM_BACK, PASS_ATT, DELAY = 1, 3, 4, 5, 7, 8, 9
CTX_SLOTS, ATT_SLOTS = DELAY + 1, 5
GRAD_LAG = NORM_BACK - FEED_BACK

eps = 1e-12
f32 = jnp.float32
bf16 = jnp.bfloat16
MESH = pl.DeviceIdType.MESH


def mm(left, right):
    return jnp.dot(left, right, preferred_element_type=f32)


def mm_nt(left, right):
    return lax.dot_general(left, right, (((1,), (1,)), ((), ())), preferred_element_type=f32)


def mm_tn(left, right):
    return lax.dot_general(left, right, (((0,), (0,)), ((), ())), preferred_element_type=f32)


def packed_rows(count, width):
    tail = 0 if width % LANES == 0 else count // (2 - count % 2)
    return -(-(width // LANES * count + tail) // 16) * 16


def pack(into, x):
    count, width = x.shape
    whole = width // LANES
    for k in range(whole):
        into[k * count : (k + 1) * count, :] = x[:, k * LANES : (k + 1) * LANES]
    if width % LANES:
        left = width - whole * LANES
        folds = 2 - count % 2
        part = count // folds
        for n in range(folds):
            into[whole * count : whole * count + part, n * left : (n + 1) * left] = x[
                n * part : (n + 1) * part, whole * LANES :
            ]


def unpack(into, start, count, width, x):
    whole = width // LANES
    for k in range(whole):
        into[start : start + count, k * LANES : (k + 1) * LANES] = x[k * count : (k + 1) * count, :]
    if width % LANES:
        left = width - whole * LANES
        folds = 2 - count % 2
        part = count // folds
        for n in range(folds):
            into[start + n * part : start + (n + 1) * part, whole * LANES : width] = x[
                whole * count : whole * count + part, n * left : (n + 1) * left
            ]


def row_sum(x):
    return jnp.sum(x, axis=0, keepdims=True)


def remote(src, dst, send, recv, device):
    return pltpu.make_async_remote_copy(
        src_ref=src, dst_ref=dst, send_sem=send, recv_sem=recv, device_id=device, device_id_type=MESH
    )


def layer_kernel(
    rows,
    groups,
    dp,
    place,
    inp,
    gout_in,
    w_qkv,
    w_out,
    w_up,
    w_down,
    b_qkv,
    b_up,
    cols,
    result,
    grad_in,
    o_qkv,
    o_out,
    o_up,
    o_down,
    o_sums,
    wqkv_t,
    wqkv,
    wout_t,
    wout_rows,
    wup_t,
    wup,
    wdown_t,
    wdown,
    all_qkv,
    all_out,
    all_up,
    all_down,
    out_rows,
    wide_mat,
    tall_mat,
    g_qkv,
    g_out,
    g_up,
    g_down,
    sums,
    flat,
    land_qkv,
    land_out,
    land_up,
    land_down,
    all_sums,
    ctx_all,
    att_all,
    stats,
    x_ring,
    mix_ring,
    prob_ring,
    mask,
    x_one,
    n_one,
    inv_one,
    hid,
    hid_low,
    pre,
    act,
    slope,
    x_two,
    upstream,
    rtg,
    br_low,
    pre_low,
    hid_grad,
    rog_ring,
    ctx_grad,
    mix_grad,
    send_blocks,
    recv_blocks,
    send_stats,
    recv_stats,
    send_weights,
    recv_weights,
    send_rows,
    recv_rows,
    send_grads,
    recv_grads,
):
    i = pl.program_id(0)
    steps = pl.num_programs(0)
    g = lax.axis_index("group")
    d = lax.axis_index("dp")
    across = lax.rem(g + 2, groups)
    beside = g + 1 - 2 * lax.rem(g, 2)
    corner = lax.rem(beside + 2, groups)
    local, seq = inp.shape
    half = seq // SPLIT
    channels = local * groups
    parts = seq // LANES
    hidden_units = wup_t.shape[0]
    ring = x_ring.shape[0]
    lanes = [slice(k * LANES, (k + 1) * LANES) for k in range(parts)]
    col = lambda n: cols[n * local : (n + 1) * local, :]
    B_OUT, GAIN1, SHIFT1, B_DOWN, GAIN2, SHIFT2 = range(6)
    S_BOUT, S_GAIN1, S_SHIFT1, S_BDOWN, S_GAIN2, S_SHIFT2 = range(6)

    def accumulate(slot, chunk):
        sums[slot * local : (slot + 1) * local, :] += chunk

    def block_copy(buf, base, kind, r, slot):
        peer = across if kind == 0 else beside
        at_row = lax.rem(r, buf.shape[0])
        return remote(
            buf.at[at_row, slot],
            buf.at[at_row, slot],
            send_blocks.at[base + kind, r],
            recv_blocks.at[base + kind, r],
            {"group": peer},
        )

    def send_own(buf, base, r):
        block_copy(buf, base, 0, r, g).start()
        block_copy(buf, base, 1, r, g).start()

    def pass_on(buf, base, r):
        block_copy(buf, base, 0, r, across).wait_recv()
        block_copy(buf, base, 2, r, across).start()

    def blocks_ready(buf, base, r):
        block_copy(buf, base, 1, r, beside).wait_recv()
        block_copy(buf, base, 2, r, corner).wait_recv()

    def blocks_sent(buf, base, r):
        block_copy(buf, base, 0, r, g).wait_send()
        block_copy(buf, base, 1, r, g).wait_send()
        block_copy(buf, base, 2, r, across).wait_send()

    def stat_copy(step, offset, slot):
        return remote(
            stats.at[step, slot],
            stats.at[step, slot],
            send_stats.at[offset - 1, step],
            recv_stats.at[offset - 1, step],
            {"group": lax.rem(g + offset, groups)},
        )

    def stats_send():
        for offset in range(1, groups):
            stat_copy(i, offset, g).start()

    def stats_ready():
        for offset in range(1, groups):
            stat_copy(i - 1, offset, lax.rem(g + groups - offset, groups)).wait_recv()
            stat_copy(i - 1, offset, g).wait_send()

    def put_stat(first, k, value):
        stats[i, g, first + k : first + k + 1, :] = value

    def get_stat(first, k, p, ago=1):
        return stats[i - ago, p, first + k : first + k + 1, :]

    ONE, TWO, BACK = 0, 2 * parts, 6 * parts
    CTX, ATT = 0, 3

    shards = (w_qkv, w_out, w_up, w_down)
    fulls = (all_qkv, all_out, all_up, all_down)
    QKV, OUT, UP, DOWN = range(4)

    def weight_copy(which, k, slot):
        full = fulls[which]
        return remote(
            full.at[slot],
            full.at[slot],
            send_weights.at[which, k],
            recv_weights.at[which, k],
            {"dp": lax.rem(d + k, dp)},
        )

    def each_peer(action):
        def body(k, carry):
            action(k)
            return carry

        lax.fori_loop(1, dp, body, 0)

    def weights_ready(which, into):
        each_peer(lambda k: weight_copy(which, k, lax.rem(d - k + dp, dp)).wait_recv())
        count, width = shards[which].shape
        for slot in range(dp):
            unpack(into, slot * count, count, width, fulls[which][slot].astype(f32))

    per = dp // groups

    def rows_copy(offset, source, target):
        return remote(
            all_out.at[pl.ds(target * per, per)],
            out_rows.at[source],
            send_rows.at[offset - 1],
            recv_rows.at[offset - 1],
            {"group": target},
        )

    @pl.when(i == 0)
    def _():
        barrier = pltpu.get_barrier_semaphore()
        for offset in range(1, groups):
            pl.semaphore_signal(
                barrier, inc=1, device_id={"group": lax.rem(g + offset, groups)}, device_id_type=MESH
            )
        each_peer(
            lambda k: pl.semaphore_signal(
                barrier, inc=1, device_id={"dp": lax.rem(d + k, dp)}, device_id_type=MESH
            )
        )
        flat[...] = jnp.zeros_like(flat)
        for shard, full in zip(shards, fulls):
            pack(flat, shard[...])
            full[d] = flat[: full.shape[1], :].astype(bf16)
        pl.semaphore_wait(barrier, groups - 1 + dp - 1)
        each_peer(lambda k: weight_copy(QKV, k, d).start())
        for ref in (g_qkv, g_out, g_up, g_down, sums):
            ref[...] = jnp.zeros_like(ref)
        weights_ready(QKV, wide_mat)
        for which in (OUT, UP, DOWN):
            each_peer(lambda k, which=which: weight_copy(which, k, d).start())
        mat = wide_mat[:, : 3 * local]
        wqkv[...] = mat.astype(bf16)
        wqkv_t[...] = mat.T.astype(bf16)

    @pl.when(i == RESIDUAL)
    def _():
        weights_ready(OUT, tall_mat)
        for offset in range(1, groups):
            rows_copy(offset, g, lax.rem(g + offset, groups)).start()
        out_rows[g] = all_out[pl.ds(g * per, per)]
        wout_t[...] = tall_mat[...].T.astype(bf16)

    @pl.when(i == FEED)
    def _():
        weights_ready(UP, wide_mat)
        mat = wide_mat[...]
        wup[...] = mat.astype(bf16)
        wup_t[...] = mat.T.astype(bf16)
        weights_ready(DOWN, tall_mat)
        mat = tall_mat[...]
        wdown[...] = mat.astype(bf16)
        wdown_t[...] = mat.T.astype(bf16)

    @pl.when(i == DELAY)
    def _():
        for offset in range(1, groups):
            rows_copy(offset, lax.rem(g + groups - offset, groups), g).wait_recv()
        count = local // per
        for p in range(groups):
            for n in range(per):
                unpack(wide_mat, n * count, count, local, out_rows[p, n].astype(f32))
            tall_mat[p * local : (p + 1) * local, :] = wide_mat[:, :local].T
        wout_rows[...] = tall_mat[...].T.astype(bf16)

    stages = fulls
    lands = (land_qkv, land_out, land_up, land_down)

    def grad_copy(which, k, slot):
        return remote(
            stages[which].at[lax.rem(d + k, dp)],
            lands[which].at[slot],
            send_grads.at[which, k],
            recv_grads.at[which, k],
            {"dp": lax.rem(d + k, dp)},
        )

    def sums_copy(k, slot):
        return remote(
            all_sums.at[slot],
            all_sums.at[slot],
            send_grads.at[4, k],
            recv_grads.at[4, k],
            {"dp": lax.rem(d + k, dp)},
        )

    def send_grad(which, mat):
        stage = stages[which]
        count = shards[which].shape[0]
        for slot in range(dp):
            pack(flat, mat[slot * count : (slot + 1) * count])
            stage[slot] = flat[: stage.shape[1], :].astype(bf16)
        each_peer(lambda k: grad_copy(which, k, d).start())

    def grad_sum(which, out):
        count = stages[which].shape[1]
        flat[:count, :] = stages[which][d].astype(f32)

        def add(k):
            slot = lax.rem(d - k + dp, dp)
            grad_copy(which, k, slot).wait()
            flat[:count, :] += lands[which][slot].astype(f32)

        each_peer(add)
        unpack(out, 0, *out.shape, flat[...])

    def stage_residual(r):
        blocks_ready(ctx_all, CTX, r)
        attended = mm(wout_t[...], ctx_all[lax.rem(r, CTX_SLOTS)].reshape(channels, seq))
        xr = x_ring.at[lax.rem(r, ring)]
        for k, s in enumerate(lanes):
            x = xr[:, s].astype(f32) + attended[:, s] + col(B_OUT)
            x_one[:, s] = x
            mean = row_sum(x) * (1.0 / local)
            off = x - mean
            put_stat(ONE, k, mean)
            put_stat(ONE + parts, k, row_sum(off * off))
        blocks_sent(ctx_all, CTX, r)

    def stage_attend(r):
        slot = lax.rem(r, ring)
        rolled = pltpu.roll(inp[...].astype(f32), place[r, 0], 1).astype(bf16)
        x_ring[slot] = rolled
        mixed = mm(wqkv_t[...], rolled)
        for s in lanes:
            mix_ring[slot, :, s] = (mixed[:, s] + b_qkv[...]).astype(bf16)
        first, second = place[r, 2], place[r, 3]
        down = lax.broadcasted_iota(jnp.int32, (half, half), 0)
        along = lax.broadcasted_iota(jnp.int32, (half, half), 1)
        own = lambda at: (at >= first).astype(jnp.int32) + (at >= second).astype(jnp.int32)
        mask[...] = jnp.where(own(down) == own(along), 0.0, -1000000000.0)
        scale = math.log2(math.e) / math.sqrt(HD)
        blocks = [(h, b) for h in range(HG) for b in range(SPLIT)]

        def piece(part, n):
            h, b = blocks[n]
            start = part * local + h * HD
            return mix_ring[slot, start : start + HD, b * half : (b + 1) * half]

        def score(n):
            return mm_tn(piece(1, n), piece(0, n))

        def soften(n, scores):
            if blocks[n][1]:
                scores = scores + mask[...]
            highest = jnp.max(scores, axis=0, keepdims=True)
            return jnp.exp2((scores - highest) * scale)

        def norm(n, exponent):
            chances = (exponent * (1.0 / row_sum(exponent))).astype(bf16)
            prob_ring[slot, n] = chances
            return chances

        def blend(n, chances):
            h, b = blocks[n]
            ctx_all[lax.rem(r, CTX_SLOTS), g, h * HD : (h + 1) * HD, b * half : (b + 1) * half] = mm(
                piece(2, n), chances
            ).astype(bf16)

        held = {}
        for step in range(len(blocks) + 3):
            n = step - 0
            if 0 <= n < len(blocks):
                held[0, n] = score(n)
            n = step - 1
            if 0 <= n < len(blocks):
                held[1, n] = soften(n, held.pop((0, n)))
            n = step - 2
            if 0 <= n < len(blocks):
                held[2, n] = norm(n, held.pop((1, n)))
            n = step - 3
            if 0 <= n < len(blocks):
                blend(n, held.pop((2, n)))
        send_own(ctx_all, CTX, r)

    def stage_norm_back(r):
        slot = lax.rem(r, rog_ring.shape[0])
        kept = lax.rem(r, (NORM_BACK - FEED + 1))
        for k, s in enumerate(lanes):
            first = get_stat(BACK, k, 0, GRAD_LAG)
            second = get_stat(BACK + parts, k, 0, GRAD_LAG)
            for p in range(1, groups):
                first += get_stat(BACK, k, p, GRAD_LAG)
                second += get_stat(BACK + parts, k, p, GRAD_LAG)
            first = first * (1.0 / channels)
            second = second * (1.0 / channels)
            scaled = hid_grad[lax.rem(r, (GRAD_LAG + 1)), :, s] * col(GAIN1)
            back = inv_one[kept, k : k + 1, :] * (scaled - first - n_one[kept, :, s] * second)
            rog_ring[slot, :, s] = back
            low = back.astype(bf16)
            att_all[lax.rem(r, ATT_SLOTS), g, :, s] = low
            accumulate(S_BOUT, low.astype(f32))
        send_own(att_all, ATT, r)
        contexts = ctx_all[lax.rem(r, CTX_SLOTS)].reshape(channels, seq)
        g_out[...] += mm_nt(contexts, att_all[lax.rem(r, ATT_SLOTS), g])

    def stage_feed(r):
        kept = lax.rem(r, (NORM_BACK - FEED + 1))
        for k, s in enumerate(lanes):
            means = [get_stat(ONE, k, p) for p in range(groups)]
            center = sum(means[1:], means[0]) * (1.0 / groups)
            spread = get_stat(ONE + parts, k, 0)
            for p in range(1, groups):
                spread += get_stat(ONE + parts, k, p)
            for mean in means:
                spread += local * (mean - center) * (mean - center)
            inverse = lax.rsqrt(spread * (1.0 / channels) + eps)
            inv_one[kept, k : k + 1, :] = inverse
            normed = (x_one[:, s] - center) * inverse
            n_one[kept, :, s] = normed
            h = normed * col(GAIN1) + col(SHIFT1)
            hid[:, s] = h
            hid_low[:, s] = h.astype(bf16)
        pre[...] = mm(wup_t[...], hid_low[...])
        for j in range(hidden_units // local):
            units = slice(j * local, (j + 1) * local)
            for s in lanes:
                u = pre[units, s] + b_up[units, :]
                cdf = 0.5 + 0.5 * lax.erf(u * math.sqrt(0.5))
                act[units, s] = (u * cdf).astype(bf16)
                bell = jnp.exp2(u * u * (-0.5 * math.log2(math.e))) * (1.0 / math.sqrt(2.0 * math.pi))
                slope[units, s] = cdf + u * bell
        branch = mm(wdown_t[...], act[...])
        upstream[...] = pltpu.roll(gout_in[...].astype(f32), place[r, 0], 1)
        for k, s in enumerate(lanes):
            x = hid[:, s] + branch[:, s] + col(B_DOWN)
            x_two[:, s] = x
            mean = row_sum(x) * (1.0 / local)
            off = x - mean
            scaled = upstream[:, s] * col(GAIN2)
            tile = (mean, row_sum(off * off), row_sum(scaled), row_sum(scaled * off))
            for n, value in enumerate(tile):
                put_stat(TWO + n * parts, k, value)

    def stage_attend_back(r):
        slot = lax.rem(r, ring)
        blocks_ready(att_all, ATT, r)
        ctx_grad[...] = mm(
            wout_rows[...], att_all[lax.rem(r, ATT_SLOTS)].reshape(channels, seq)
        ).astype(bf16)
        factor = 1.0 / math.sqrt(HD)
        blocks = [(h, b) for h in range(HG) for b in range(SPLIT)]

        def at_block(part, n):
            h, b = blocks[n]
            start = part * local + h * HD
            return slice(start, start + HD), slice(b * half, (b + 1) * half)

        def piece(part, n):
            return mix_ring[slot, *at_block(part, n)]

        def spread(n):
            incoming = ctx_grad[at_block(0, n)]
            mix_grad[at_block(2, n)] = mm_nt(incoming, prob_ring[slot, n]).astype(bf16)

        def open_up(n):
            return mm_tn(piece(2, n), ctx_grad[at_block(0, n)])

        def center(n, prob_grad):
            at_n = at_block(0, n)
            inner = row_sum(ctx_grad[at_n].astype(f32) * ctx_all[lax.rem(r, CTX_SLOTS), g, *at_n].astype(f32))
            return (prob_ring[slot, n].astype(f32) * (prob_grad - inner)).astype(bf16)

        def queries(n, score_grad):
            mix_grad[at_block(0, n)] = (mm(piece(1, n), score_grad) * factor).astype(bf16)

        def keys(n, score_grad):
            mix_grad[at_block(1, n)] = (mm_nt(piece(0, n), score_grad) * factor).astype(bf16)

        held = {}
        for step in range(len(blocks) + 2):
            n = step - 0
            if 0 <= n < len(blocks):
                held[0, n] = open_up(n)
            n = step - 0
            if 0 <= n < len(blocks):
                spread(n)
            n = step - 1
            if 0 <= n < len(blocks):
                held[1, n] = center(n, held.pop((0, n)))
            n = step - 2
            if 0 <= n < len(blocks):
                queries(n, held[1, n])
            n = step - 2
            if 0 <= n < len(blocks):
                keys(n, held.pop((1, n)))
        g_qkv[...] += mm_nt(mix_grad[...], x_ring[slot])
        blocks_sent(att_all, ATT, r)
        grad_in[...] = mm(wqkv[...], mix_grad[...]) + rog_ring[lax.rem(r, rog_ring.shape[0])]
        base = 6 * local + hidden_units
        for n, start in ((0, 0), (1, 2 * local)):
            chunk = mix_grad[start : start + local, lanes[0]].astype(f32)
            for s in lanes[1:]:
                chunk += mix_grad[start : start + local, s].astype(f32)
            sums[base + n * local : base + (n + 1) * local, :] += chunk

    def stage_feed_back(r):
        for k, s in enumerate(lanes):
            row = lambda p, n: get_stat(TWO + n * parts, k, p)
            means = [row(p, 0) for p in range(groups)]
            center = sum(means[1:], means[0]) * (1.0 / groups)
            spread, first, second = row(0, 1), row(0, 2), row(0, 3)
            for p in range(1, groups):
                spread += row(p, 1)
                first += row(p, 2)
                second += row(p, 3)
            for p, mean in enumerate(means):
                spread += local * (mean - center) * (mean - center)
                second += (mean - center) * row(p, 2)
            inverse = lax.rsqrt(spread * (1.0 / channels) + eps)
            first = first * (1.0 / channels)
            second = second * inverse * (1.0 / channels)
            normed = (x_two[:, s] - center) * inverse
            result[:, s] = (normed * col(GAIN2) + col(SHIFT2)).astype(bf16)
            up = upstream[:, s]
            back = inverse * (up * col(GAIN2) - first - normed * second)
            rtg[:, s] = back
            low = back.astype(bf16)
            br_low[:, s] = low
            accumulate(S_GAIN2, up * normed)
            accumulate(S_SHIFT2, up)
            accumulate(S_BDOWN, low.astype(f32))
        pre[...] = mm(wdown[...], br_low[...])
        g_down[...] += mm_nt(act[...], br_low[...])
        base = 6 * local
        for j in range(hidden_units // local):
            units = slice(j * local, (j + 1) * local)
            for s in lanes:
                low = (slope[units, s] * pre[units, s]).astype(bf16)
                pre_low[units, s] = low
                sums[base + j * local : base + (j + 1) * local, :] += low.astype(f32)
        g_up[...] += mm_nt(pre_low[...], hid_low[...])
        change = mm(wup[...], pre_low[...])
        for k, s in enumerate(lanes):
            total = rtg[:, s] + change[:, s]
            hid_grad[lax.rem(r, (GRAD_LAG + 1)), :, s] = total
            normed = n_one[lax.rem(r, (NORM_BACK - FEED + 1)), :, s]
            scaled = total * col(GAIN1)
            put_stat(BACK, k, row_sum(scaled))
            put_stat(BACK + parts, k, row_sum(scaled * normed))
            accumulate(S_GAIN1, total * normed)
            accumulate(S_SHIFT1, total)

    def at(delay, stage):
        r = i - delay

        @pl.when(jnp.logical_and(r >= 0, r < rows))
        def _():
            stage(r)

    @pl.when(jnp.logical_and(i > RESIDUAL, i < rows + NORM_BACK))
    def _():
        stats_ready()

    at(FEED_BACK, stage_feed_back)
    at(FEED, stage_feed)
    at(RESIDUAL, stage_residual)

    @pl.when(jnp.logical_and(i >= RESIDUAL, i < rows + NORM_BACK - 1))
    def _():
        stats_send()

    at(0, stage_attend)
    at(NORM_BACK, stage_norm_back)
    at(PASS_CTX, lambda r: pass_on(ctx_all, CTX, r))
    at(DELAY, stage_attend_back)
    at(PASS_ATT, lambda r: pass_on(att_all, ATT, r))

    @pl.when(i == rows - 1 + FEED_BACK)
    def _():
        for which in range(4):
            each_peer(lambda k, which=which: weight_copy(which, k, d).wait_send())
        for offset in range(1, groups):
            rows_copy(offset, g, lax.rem(g + offset, groups)).wait_send()
        send_grad(UP, g_up[...].T)
        send_grad(DOWN, g_down[...])

    @pl.when(i == rows - 1 + NORM_BACK)
    def _():
        send_grad(OUT, g_out[...])

    @pl.when(i == steps - 1)
    def _():
        send_grad(QKV, g_qkv[...].T)
        mine = all_sums.at[d]
        for n in range(6):
            mine[n : n + 1, :local] = row_sum(sums[n * local : (n + 1) * local, :].T)
        base = 6 * local
        mine[6:7, :] = row_sum(sums[base : base + hidden_units, :].T)
        base += hidden_units
        mine[7:8, : 2 * local] = row_sum(sums[base : base + 2 * local, :].T)
        each_peer(lambda k: sums_copy(k, d).start())
        for which, out in ((UP, o_up), (DOWN, o_down), (OUT, o_out), (QKV, o_qkv)):
            grad_sum(which, out)
        each_peer(lambda k: sums_copy(k, lax.rem(d - k + dp, dp)).wait())
        o_sums[...] = jnp.sum(all_sums[...], axis=0)


def run_layer(place, inputs, grad_out, shards, b_qkv, b_up, cols):
    groups = lax.axis_size("group")
    dp = lax.axis_size("dp")
    local, tok_count = inputs.shape
    rows = place.shape[0]
    channels = groups * local
    seq = tok_count // rows
    half = seq // SPLIT
    parts = seq // LANES
    units = b_up.shape[0]
    last = rows - 1
    ring = DELAY + 1
    vmem = pl.BlockSpec(memory_space=pltpu.VMEM)

    def rows_at(delay):
        return pl.BlockSpec((local, seq), lambda i: (0, jnp.clip(i - delay, 0, last)))

    def whole(shape):
        return pl.BlockSpec(shape, lambda i: (0,) * len(shape))

    acc_shapes = ((3 * local, local), (groups * local, local), (units, local), (units, local))
    sums_shape = (6 * local + units + 2 * local, LANES)
    shard_shapes = tuple(w.shape for w in shards)
    slots = tuple((dp, packed_rows(*s), LANES) for s in shard_shapes)
    row_sums = (8, units)
    block = (groups, local, seq)
    return pl.pallas_call(
        functools.partial(layer_kernel, rows, groups, dp),
        grid=(rows + DELAY,),
        out_shape=(
            jax.ShapeDtypeStruct((local, tok_count), bf16),
            jax.ShapeDtypeStruct((local, tok_count), f32),
            *(jax.ShapeDtypeStruct(s, f32) for s in shard_shapes),
            jax.ShapeDtypeStruct(row_sums, f32),
        ),
        in_specs=[
            pl.BlockSpec(memory_space=pltpu.SMEM),
            rows_at(0),
            rows_at(FEED),
            *([vmem] * (len(shards) + 3)),
        ],
        out_specs=(
            rows_at(FEED_BACK),
            rows_at(DELAY),
            *(whole(s) for s in shard_shapes),
            whole(row_sums),
        ),
        scratch_shapes=[
            pltpu.VMEM((3 * local, local), bf16),
            pltpu.VMEM((local, 3 * local), bf16),
            pltpu.VMEM((local, channels), bf16),
            pltpu.VMEM((local, channels), bf16),
            pltpu.VMEM((units, local), bf16),
            pltpu.VMEM((local, units), bf16),
            pltpu.VMEM((local, units), bf16),
            pltpu.VMEM((units, local), bf16),
            *(pltpu.VMEM(s, bf16) for s in slots),
            pltpu.VMEM((groups, dp // groups, *slots[1][1:]), bf16),
            pltpu.VMEM((local, units), f32),
            pltpu.VMEM((units, local), f32),
            *(pltpu.VMEM(s, f32) for s in acc_shapes),
            pltpu.VMEM(sums_shape, f32),
            pltpu.VMEM((max(s[1] for s in slots), LANES), f32),
            *(pltpu.VMEM(s, bf16) for s in slots),
            pltpu.VMEM((dp, *row_sums), f32),
            pltpu.VMEM((CTX_SLOTS, *block), bf16),
            pltpu.VMEM((ATT_SLOTS, *block), bf16),
            pltpu.VMEM((rows + DELAY, groups, 8 * parts, LANES), f32),
            pltpu.VMEM((ring, local, seq), bf16),
            pltpu.VMEM((ring, 3 * local, seq), bf16),
            pltpu.VMEM((ring, HG * SPLIT, half, half), bf16),
            pltpu.VMEM((half, half), f32),
            pltpu.VMEM((local, seq), f32),
            pltpu.VMEM(((NORM_BACK - FEED + 1), local, seq), f32),
            pltpu.VMEM(((NORM_BACK - FEED + 1), parts, LANES), f32),
            pltpu.VMEM((local, seq), f32),
            pltpu.VMEM((local, seq), bf16),
            pltpu.VMEM((units, seq), f32),
            pltpu.VMEM((units, seq), bf16),
            pltpu.VMEM((units, seq), f32),
            pltpu.VMEM((local, seq), f32),
            pltpu.VMEM((local, seq), f32),
            pltpu.VMEM((local, seq), f32),
            pltpu.VMEM((local, seq), bf16),
            pltpu.VMEM((units, seq), bf16),
            pltpu.VMEM(((GRAD_LAG + 1), local, seq), f32),
            pltpu.VMEM((3, local, seq), f32),
            pltpu.VMEM((local, seq), bf16),
            pltpu.VMEM((3 * local, seq), bf16),
            pltpu.SemaphoreType.DMA((6, rows)),
            pltpu.SemaphoreType.DMA((6, rows)),
            pltpu.SemaphoreType.DMA((groups - 1, rows + DELAY)),
            pltpu.SemaphoreType.DMA((groups - 1, rows + DELAY)),
            pltpu.SemaphoreType.DMA((4, dp)),
            pltpu.SemaphoreType.DMA((4, dp)),
            pltpu.SemaphoreType.DMA((groups - 1,)),
            pltpu.SemaphoreType.DMA((groups - 1,)),
            pltpu.SemaphoreType.DMA((5, dp)),
            pltpu.SemaphoreType.DMA((5, dp)),
        ],
        compiler_params=pltpu.CompilerParams(
            collective_id=0, has_side_effects=True, vmem_limit_bytes=63 << 20
        ),
        name="layer",
    )(place, inputs, grad_out, *shards, b_qkv, b_up, cols)


def prepare_kernel(labels, b_qv, b_up, b_out, gain_one, shift_one, b_down, gain_two, shift_two, place, o_qkv, o_up, o_cols):
    rows, seq = labels.shape
    half = seq // SPLIT
    local = b_out.shape[1]
    ids = labels[...]
    counts = [
        jnp.sum(jnp.where(ids == v, 1.0, 0.0), axis=1, keepdims=True) for v in range(4)
    ]
    start = jnp.zeros_like(counts[0])
    first = jnp.zeros_like(start)
    second = jnp.zeros_like(start)
    found = jnp.zeros_like(start)
    begin = jnp.zeros_like(start)
    for v in range(4):
        hit = jnp.where(counts[v] == half, 1.0 - found, 0.0)
        start = start + hit * begin
        first = first + hit * counts[(v + 1) % 4]
        second = second + hit * (counts[(v + 1) % 4] + counts[(v + 2) % 4])
        found = found + hit
        begin = begin + counts[v]
    turn = jnp.where(start == 0.0, 0.0, seq - start)
    lane = lax.broadcasted_iota(jnp.int32, (rows, LANES), 1)
    table = jnp.zeros((rows, LANES), f32)
    for n, value in enumerate((turn, start, first, second)):
        table = jnp.where(lane == n, value, table)
    place[...] = table.astype(jnp.int32)

    def column(row):
        return jnp.broadcast_to(row, (LANES, row.shape[1])).T

    o_qkv[:local, :] = column(b_qv[:, :local])
    o_qkv[local : 2 * local, :] = jnp.zeros((local, LANES), f32)
    o_qkv[2 * local :, :] = column(b_qv[...])[local:, :]
    o_up[...] = column(b_up[...])
    for n, ref in enumerate((b_out, gain_one, shift_one, b_down, gain_two, shift_two)):
        o_cols[n * local : (n + 1) * local, :] = column(ref[...])


def prepare(labels, b_qv, b_up, *vectors):
    local = vectors[0].shape[-1]
    vmem = pl.BlockSpec(memory_space=pltpu.VMEM)
    return pl.pallas_call(
        prepare_kernel,
        out_shape=(
            jax.ShapeDtypeStruct((labels.shape[0], LANES), jnp.int32),
            jax.ShapeDtypeStruct((3 * local, LANES), f32),
            jax.ShapeDtypeStruct((b_up.shape[1], LANES), f32),
            jax.ShapeDtypeStruct((6 * local, LANES), f32),
        ),
        in_specs=[vmem] * (3 + len(vectors)),
        out_specs=(vmem,) * 4,
        name="prepare",
    )(labels, b_qv, b_up, *(v.reshape(1, local) for v in vectors))


def finish_kernel(many, seq, place, result, grad_in, qkv, out, up, down, sums, *outs):
    i = pl.program_id(0)
    for n in range(many):
        toks = slice(n * seq, (n + 1) * seq)
        turn = place[i * many + n, 1]
        outs[0][:, toks] = pltpu.roll(result[:, toks].astype(f32), turn, 1).astype(bf16)
        outs[1][:, toks] = pltpu.roll(grad_in[:, toks], turn, 1)

    @pl.when(i == 0)
    def _():
        local = result.shape[0]
        for target, source in zip(outs[2:6], (qkv, out, up, down)):
            target[...] = source[...]
        for n in range(6):
            outs[6 + n][...] = sums[n : n + 1, :local]
        outs[12][...] = sums[6:7, :]
        outs[13][...] = sums[7:8, : 2 * local]


def finish(place, result, grad_in, *small):
    local, tok_count = result.shape
    rows = place.shape[0]
    seq = tok_count // rows
    units = small[4].shape[1]
    many = math.gcd(rows, FINISH_ROWS)
    block = pl.BlockSpec((local, many * seq), lambda i: (0, i))
    vmem = pl.BlockSpec(memory_space=pltpu.VMEM)
    shapes = (*(s.shape for s in small[:4]), *((1, local),) * 6, (1, units), (1, 2 * local))
    return pl.pallas_call(
        functools.partial(finish_kernel, many, seq),
        grid=(rows // many,),
        out_shape=(
            jax.ShapeDtypeStruct(result.shape, bf16),
            jax.ShapeDtypeStruct(grad_in.shape, f32),
            *(jax.ShapeDtypeStruct(s, f32) for s in shapes),
        ),
        in_specs=[pl.BlockSpec(memory_space=pltpu.SMEM), block, block, *[vmem] * 5],
        out_specs=(block, block, *(vmem,) * len(shapes)),
        compiler_params=pltpu.CompilerParams(vmem_limit_bytes=48 << 20),
        name="finish",
    )(place, result, grad_in, *small)


def per_device(
    inputs,
    labels,
    w_qkv,
    b_qv,
    w_out,
    b_out,
    gain_one,
    shift_one,
    w_up,
    b_up,
    down_weight,
    down_bias,
    gain_two,
    shift_two,
    grad_out,
):
    place, qkv_col, up_col, cols = prepare(
        labels, b_qv, b_up, b_out, gain_one, shift_one, down_bias, gain_two, shift_two
    )
    shards = (w_qkv[0], w_out, w_up[0], down_weight[0])
    raw = run_layer(place, inputs, grad_out, shards, qkv_col, up_col, cols)
    result, input_grad, qkv, out, up, down, *sums = finish(place, *raw)
    flat = [s.reshape(-1) for s in sums]
    return (
        result,
        input_grad,
        qkv[None],
        sums[7],
        out,
        flat[0],
        flat[1],
        flat[2],
        up[None],
        sums[6],
        down[None],
        sums[3],
        flat[4],
        flat[5],
    )


def solution(mesh):
    placed = (
        P("group", "dp"),
        P("dp", None),
        P("group", "dp", None),
        P("group", None),
        P("dp", "group"),
        P("group"),
        P("group"),
        P("group"),
        P("group", "dp", None),
        P("group", None),
        P("group", "dp", None),
        P("group", None),
        P("group"),
        P("group"),
        P("group", "dp"),
    )
    return jax.shard_map(
        per_device,
        mesh=mesh,
        in_specs=placed,
        out_specs=(
            P("group", "dp"),
            P("group", "dp"),
            P("group", "dp", None),
            P("group", None),
            P("dp", "group"),
            P("group"),
            P("group"),
            P("group"),
            P("group", "dp", None),
            P("group", None),
            P("group", "dp", None),
            P("group", None),
            P("group"),
            P("group"),
        ),
        check_vma=False,
    )
```

```python
import functools
import math

import jax
import jax.numpy as jnp
from jax import lax
from jax.experimental import pallas as pl
from jax.experimental.pallas import tpu as pltpu
from jax.sharding import PartitionSpec as P

HD = 64
HG = 3
LANES = 128
SPLIT = 2
FINISH_ROWS = 4
PASS_CTX, RESIDUAL, FEED, FEED_BACK, NORM_BACK, PASS_ATT, DELAY = 1, 3, 4, 5, 7, 8, 9
CTX_SLOTS, ATT_SLOTS, SEMS = DELAY + 1, 5, 5
GRAD_LAG = NORM_BACK - FEED_BACK

eps = 1e-12
f32 = jnp.float32
bf16 = jnp.bfloat16
MESH = pl.DeviceIdType.MESH


def mm(left, right):
    return jnp.dot(left, right, preferred_element_type=f32)


def mm_nt(left, right):
    return lax.dot_general(left, right, (((1,), (1,)), ((), ())), preferred_element_type=f32)


def mm_tn(left, right):
    return lax.dot_general(left, right, (((0,), (0,)), ((), ())), preferred_element_type=f32)


def packed_rows(count, width):
    tail = 0 if width % LANES == 0 else count // (2 - count % 2)
    return -(-(width // LANES * count + tail) // 16) * 16


def pack(into, x):
    count, width = x.shape
    whole = width // LANES
    for k in range(whole):
        into[k * count : (k + 1) * count, :] = x[:, k * LANES : (k + 1) * LANES]
    if width % LANES:
        left = width - whole * LANES
        folds = 2 - count % 2
        part = count // folds
        for n in range(folds):
            into[whole * count : whole * count + part, n * left : (n + 1) * left] = x[
                n * part : (n + 1) * part, whole * LANES :
            ]


def unpack(into, start, count, width, x):
    whole = width // LANES
    for k in range(whole):
        into[start : start + count, k * LANES : (k + 1) * LANES] = x[k * count : (k + 1) * count, :]
    if width % LANES:
        left = width - whole * LANES
        folds = 2 - count % 2
        part = count // folds
        for n in range(folds):
            into[start + n * part : start + (n + 1) * part, whole * LANES : width] = x[
                whole * count : whole * count + part, n * left : (n + 1) * left
            ]


def row_sum(x):
    return jnp.sum(x, axis=0, keepdims=True)


def remote(src, dst, send, recv, device):
    return pltpu.make_async_remote_copy(
        src_ref=src, dst_ref=dst, send_sem=send, recv_sem=recv, device_id=device, device_id_type=MESH
    )


def layer_kernel(
    rows,
    groups,
    dp,
    labels,
    inp,
    gout_in,
    w_qkv,
    w_out,
    w_up,
    w_down,
    in_qv,
    in_up,
    in_out,
    in_gain_one,
    in_shift_one,
    in_down,
    in_gain_two,
    in_shift_two,
    result,
    grad_in,
    o_qkv,
    o_out,
    o_up,
    o_down,
    o_sums,
    o_place,
    place,
    b_qkv,
    b_up,
    cols,
    inp_rows,
    gout_rows,
    res_ring,
    gin_ring,
    wqkv_t,
    wqkv,
    wout_t,
    wout_rows,
    wup_t,
    wup,
    wdown_t,
    wdown,
    all_qkv,
    all_out,
    all_up,
    all_down,
    out_rows,
    wide_mat,
    tall_mat,
    g_qkv,
    g_out,
    g_up,
    g_down,
    sums,
    flat,
    land_qkv,
    land_out,
    land_up,
    land_down,
    all_sums,
    ctx_all,
    att_all,
    stats,
    x_ring,
    mix_ring,
    prob_ring,
    mask,
    x_one,
    n_one,
    inv_one,
    hid,
    hid_low,
    pre,
    act,
    slope,
    x_two,
    upstream,
    rtg,
    br_low,
    pre_low,
    hid_grad,
    rog_ring,
    ctx_grad,
    mix_grad,
    send_blocks,
    recv_blocks,
    send_stats,
    recv_stats,
    send_weights,
    recv_weights,
    send_rows,
    recv_rows,
    send_grads,
    recv_grads,
    fetch,
    store,
    place_sem,
):
    steps = rows + DELAY
    local = w_out.shape[1]
    seq = inp.shape[1] // rows

    def inp_copy(r):
        toks = pl.ds(pl.multiple_of(r * seq, seq), seq)
        return pltpu.make_async_copy(inp.at[:, toks], inp_rows.at[r], fetch.at[0, r])

    def gout_copy(r):
        toks = pl.ds(pl.multiple_of(r * seq, seq), seq)
        return pltpu.make_async_copy(gout_in.at[:, toks], gout_rows.at[r], fetch.at[1, r])

    def result_copy(r):
        toks = pl.ds(pl.multiple_of(r * seq, seq), seq)
        slot = lax.rem(r, 2)
        return pltpu.make_async_copy(res_ring.at[slot], result.at[:, toks], store.at[0, slot])

    def grad_in_copy(r):
        toks = pl.ds(pl.multiple_of(r * seq, seq), seq)
        slot = lax.rem(r, 2)
        return pltpu.make_async_copy(gin_ring.at[slot], grad_in.at[:, toks], store.at[1, slot])

    def find_places():
        ids = labels[...]
        counts = [
            jnp.sum(jnp.where(ids == v, 1.0, 0.0), axis=1, keepdims=True) for v in range(4)
        ]
        start = jnp.zeros_like(counts[0])
        first = jnp.zeros_like(start)
        second = jnp.zeros_like(start)
        found = jnp.zeros_like(start)
        begin = jnp.zeros_like(start)
        for v in range(4):
            hit = jnp.where(counts[v] == seq // SPLIT, 1.0 - found, 0.0)
            start = start + hit * begin
            first = first + hit * counts[(v + 1) % 4]
            second = second + hit * (counts[(v + 1) % 4] + counts[(v + 2) % 4])
            found = found + hit
            begin = begin + counts[v]
        turn = jnp.where(start == 0.0, 0.0, seq - start)
        lane = lax.broadcasted_iota(jnp.int32, (rows, LANES), 1)
        table = jnp.zeros((rows, LANES), f32)
        for n, value in enumerate((turn, start, first, second)):
            table = jnp.where(lane == n, value, table)
        o_place[...] = table.astype(jnp.int32)
        copy = pltpu.make_async_copy(o_place, place, place_sem)
        copy.start()
        copy.wait()

    def spread_vectors():
        def column(row):
            return jnp.broadcast_to(row, (LANES, row.shape[1])).T

        qv = column(in_qv[...])
        b_qkv[:local, :] = qv[:local]
        b_qkv[local : 2 * local, :] = jnp.zeros((local, LANES), f32)
        b_qkv[2 * local :, :] = qv[local:]
        b_up[...] = column(in_up[...])
        vectors = (in_out, in_gain_one, in_shift_one, in_down, in_gain_two, in_shift_two)
        for n, ref in enumerate(vectors):
            cols[n * local : (n + 1) * local, :] = column(ref[...])

    def step(i, carry):
        g = lax.axis_index("group")
        d = lax.axis_index("dp")
        across = lax.rem(g + 2, groups)
        beside = g + 1 - 2 * lax.rem(g, 2)
        corner = lax.rem(beside + 2, groups)
        half = seq // SPLIT
        channels = local * groups
        parts = seq // LANES
        hidden_units = wup_t.shape[0]
        ring = x_ring.shape[0]
        lanes = [slice(k * LANES, (k + 1) * LANES) for k in range(parts)]
        col = lambda n: cols[n * local : (n + 1) * local, :]
        B_OUT, GAIN1, SHIFT1, B_DOWN, GAIN2, SHIFT2 = range(6)
        S_BOUT, S_GAIN1, S_SHIFT1, S_BDOWN, S_GAIN2, S_SHIFT2 = range(6)

        def accumulate(slot, chunk):
            sums[slot * local : (slot + 1) * local, :] += chunk

        def block_copy(buf, base, kind, r, slot):
            peer = across if kind == 0 else beside
            at_row = lax.rem(r, buf.shape[0])
            return remote(
                buf.at[at_row, slot],
                buf.at[at_row, slot],
                send_blocks.at[base + kind, lax.rem(r, SEMS)],
                recv_blocks.at[base + kind, lax.rem(r, SEMS)],
                {"group": peer},
            )

        def send_own(buf, base, r):
            block_copy(buf, base, 0, r, g).start()
            block_copy(buf, base, 1, r, g).start()

        def pass_on(buf, base, r):
            block_copy(buf, base, 0, r, across).wait_recv()
            block_copy(buf, base, 2, r, across).start()

        def blocks_ready(buf, base, r):
            block_copy(buf, base, 1, r, beside).wait_recv()
            block_copy(buf, base, 2, r, corner).wait_recv()

        def blocks_sent(buf, base, r):
            block_copy(buf, base, 0, r, g).wait_send()
            block_copy(buf, base, 1, r, g).wait_send()
            block_copy(buf, base, 2, r, across).wait_send()

        def stat_copy(step, offset, slot):
            return remote(
                stats.at[step, slot],
                stats.at[step, slot],
                send_stats.at[offset - 1, lax.rem(step, SEMS)],
                recv_stats.at[offset - 1, lax.rem(step, SEMS)],
                {"group": lax.rem(g + offset, groups)},
            )

        def stats_send():
            for offset in range(1, groups):
                stat_copy(i, offset, g).start()

        def stats_ready():
            for offset in range(1, groups):
                stat_copy(i - 1, offset, lax.rem(g + groups - offset, groups)).wait_recv()
                stat_copy(i - 1, offset, g).wait_send()

        def put_stat(first, k, value):
            stats[i, g, first + k : first + k + 1, :] = value

        def get_stat(first, k, p, ago=1):
            return stats[i - ago, p, first + k : first + k + 1, :]

        ONE, TWO, BACK = 0, 2 * parts, 6 * parts
        CTX, ATT = 0, 3

        shards = (w_qkv, w_out, w_up, w_down)
        fulls = (all_qkv, all_out, all_up, all_down)
        QKV, OUT, UP, DOWN = range(4)

        def weight_copy(which, k, slot):
            full = fulls[which]
            return remote(
                full.at[slot],
                full.at[slot],
                send_weights.at[which, k],
                recv_weights.at[which, k],
                {"dp": lax.rem(d + k, dp)},
            )

        def each_peer(action):
            def body(k, carry):
                action(k)
                return carry

            lax.fori_loop(1, dp, body, 0)

        def weights_ready(which, into):
            each_peer(lambda k: weight_copy(which, k, lax.rem(d - k + dp, dp)).wait_recv())
            count, width = shards[which].shape
            for slot in range(dp):
                unpack(into, slot * count, count, width, fulls[which][slot].astype(f32))

        per = dp // groups

        def rows_copy(offset, source, target):
            return remote(
                all_out.at[pl.ds(target * per, per)],
                out_rows.at[source],
                send_rows.at[offset - 1],
                recv_rows.at[offset - 1],
                {"group": target},
            )

        @pl.when(i == 0)
        def _():
            barrier = pltpu.get_barrier_semaphore()
            for offset in range(1, groups):
                pl.semaphore_signal(
                    barrier, inc=1, device_id={"group": lax.rem(g + offset, groups)}, device_id_type=MESH
                )
            each_peer(
                lambda k: pl.semaphore_signal(
                    barrier, inc=1, device_id={"dp": lax.rem(d + k, dp)}, device_id_type=MESH
                )
            )
            flat[...] = jnp.zeros_like(flat)

            def pack_shard(which):
                pack(flat, shards[which][...])
                fulls[which][d] = flat[: fulls[which].shape[1], :].astype(bf16)

            pack_shard(QKV)
            pl.semaphore_wait(barrier, groups - 1 + dp - 1)
            each_peer(lambda k: weight_copy(QKV, k, d).start())
            for which in (OUT, UP, DOWN):
                pack_shard(which)

            def fetch_row(r, carry):
                inp_copy(r).start()
                gout_copy(r).start()
                return carry

            lax.fori_loop(0, rows, fetch_row, 0)
            find_places()
            spread_vectors()
            for ref in (g_qkv, g_out, g_up, g_down, sums):
                ref[...] = jnp.zeros_like(ref)
            weights_ready(QKV, wide_mat)
            for which in (OUT, UP, DOWN):
                each_peer(lambda k, which=which: weight_copy(which, k, d).start())
            mat = wide_mat[:, : 3 * local]
            wqkv[...] = mat.astype(bf16)
            wqkv_t[...] = mat.T.astype(bf16)

        @pl.when(i == RESIDUAL)
        def _():
            weights_ready(OUT, tall_mat)
            for offset in range(1, groups):
                rows_copy(offset, g, lax.rem(g + offset, groups)).start()
            out_rows[g] = all_out[pl.ds(g * per, per)]
            wout_t[...] = tall_mat[...].T.astype(bf16)

        @pl.when(i == FEED)
        def _():
            weights_ready(UP, wide_mat)
            mat = wide_mat[...]
            wup[...] = mat.astype(bf16)
            wup_t[...] = mat.T.astype(bf16)
            weights_ready(DOWN, tall_mat)
            mat = tall_mat[...]
            wdown[...] = mat.astype(bf16)
            wdown_t[...] = mat.T.astype(bf16)

        @pl.when(i == DELAY)
        def _():
            for offset in range(1, groups):
                rows_copy(offset, lax.rem(g + groups - offset, groups), g).wait_recv()
            count = local // per
            for p in range(groups):
                for n in range(per):
                    unpack(wide_mat, n * count, count, local, out_rows[p, n].astype(f32))
                tall_mat[p * local : (p + 1) * local, :] = wide_mat[:, :local].T
            wout_rows[...] = tall_mat[...].T.astype(bf16)

        stages = fulls
        lands = (land_qkv, land_out, land_up, land_down)

        def grad_copy(which, k, slot):
            return remote(
                stages[which].at[lax.rem(d + k, dp)],
                lands[which].at[slot],
                send_grads.at[which, k],
                recv_grads.at[which, k],
                {"dp": lax.rem(d + k, dp)},
            )

        def sums_copy(k, slot):
            return remote(
                all_sums.at[slot],
                all_sums.at[slot],
                send_grads.at[4, k],
                recv_grads.at[4, k],
                {"dp": lax.rem(d + k, dp)},
            )

        def send_grad(which, mat):
            stage = stages[which]
            count = shards[which].shape[0]
            for slot in range(dp):
                pack(flat, mat[slot * count : (slot + 1) * count])
                stage[slot] = flat[: stage.shape[1], :].astype(bf16)
            each_peer(lambda k: grad_copy(which, k, d).start())

        def grad_sum(which, out):
            count = stages[which].shape[1]
            flat[:count, :] = stages[which][d].astype(f32)

            def add(k):
                slot = lax.rem(d - k + dp, dp)
                grad_copy(which, k, slot).wait()
                flat[:count, :] += lands[which][slot].astype(f32)

            each_peer(add)
            unpack(out, 0, *out.shape, flat[...])

        def stage_residual(r):
            blocks_ready(ctx_all, CTX, r)
            attended = mm(wout_t[...], ctx_all[lax.rem(r, CTX_SLOTS)].reshape(channels, seq))
            xr = x_ring.at[lax.rem(r, ring)]
            for k, s in enumerate(lanes):
                x = xr[:, s].astype(f32) + attended[:, s] + col(B_OUT)
                x_one[:, s] = x
                mean = row_sum(x) * (1.0 / local)
                off = x - mean
                put_stat(ONE, k, mean)
                put_stat(ONE + parts, k, row_sum(off * off))
            blocks_sent(ctx_all, CTX, r)

        def stage_attend(r):
            slot = lax.rem(r, ring)
            inp_copy(r).wait()
            rolled = pltpu.roll(inp_rows[r].astype(f32), place[r, 0], 1).astype(bf16)
            x_ring[slot] = rolled
            mixed = mm(wqkv_t[...], rolled)
            for s in lanes:
                mix_ring[slot, :, s] = (mixed[:, s] + b_qkv[...]).astype(bf16)
            first, second = place[r, 2], place[r, 3]
            down = lax.broadcasted_iota(jnp.int32, (half, half), 0)
            along = lax.broadcasted_iota(jnp.int32, (half, half), 1)
            own = lambda at: (at >= first).astype(jnp.int32) + (at >= second).astype(jnp.int32)
            mask[...] = jnp.where(own(down) == own(along), 0.0, -1000000000.0)
            scale = math.log2(math.e) / math.sqrt(HD)
            blocks = [(h, b) for h in range(HG) for b in range(SPLIT)]

            def piece(part, n):
                h, b = blocks[n]
                start = part * local + h * HD
                return mix_ring[slot, start : start + HD, b * half : (b + 1) * half]

            def score(n):
                return mm_tn(piece(1, n), piece(0, n))

            def soften(n, scores):
                if blocks[n][1]:
                    scores = scores + mask[...]
                highest = jnp.max(scores, axis=0, keepdims=True)
                return jnp.exp2((scores - highest) * scale)

            def norm(n, exponent):
                chances = (exponent * (1.0 / row_sum(exponent))).astype(bf16)
                prob_ring[slot, n] = chances
                return chances

            def blend(n, chances):
                h, b = blocks[n]
                ctx_all[lax.rem(r, CTX_SLOTS), g, h * HD : (h + 1) * HD, b * half : (b + 1) * half] = mm(
                    piece(2, n), chances
                ).astype(bf16)

            held = {}
            for step in range(len(blocks) + 3):
                n = step - 0
                if 0 <= n < len(blocks):
                    held[0, n] = score(n)
                n = step - 1
                if 0 <= n < len(blocks):
                    held[1, n] = soften(n, held.pop((0, n)))
                n = step - 2
                if 0 <= n < len(blocks):
                    held[2, n] = norm(n, held.pop((1, n)))
                n = step - 3
                if 0 <= n < len(blocks):
                    blend(n, held.pop((2, n)))
            send_own(ctx_all, CTX, r)

        def stage_norm_back(r):
            slot = lax.rem(r, rog_ring.shape[0])
            kept = lax.rem(r, (NORM_BACK - FEED + 1))
            for k, s in enumerate(lanes):
                first = get_stat(BACK, k, 0, GRAD_LAG)
                second = get_stat(BACK + parts, k, 0, GRAD_LAG)
                for p in range(1, groups):
                    first += get_stat(BACK, k, p, GRAD_LAG)
                    second += get_stat(BACK + parts, k, p, GRAD_LAG)
                first = first * (1.0 / channels)
                second = second * (1.0 / channels)
                scaled = hid_grad[lax.rem(r, (GRAD_LAG + 1)), :, s] * col(GAIN1)
                back = inv_one[kept, k : k + 1, :] * (scaled - first - n_one[kept, :, s] * second)
                rog_ring[slot, :, s] = back
                low = back.astype(bf16)
                att_all[lax.rem(r, ATT_SLOTS), g, :, s] = low
                accumulate(S_BOUT, low.astype(f32))
            send_own(att_all, ATT, r)
            contexts = ctx_all[lax.rem(r, CTX_SLOTS)].reshape(channels, seq)
            g_out[...] += mm_nt(contexts, att_all[lax.rem(r, ATT_SLOTS), g])

        def stage_feed(r):
            kept = lax.rem(r, (NORM_BACK - FEED + 1))
            for k, s in enumerate(lanes):
                means = [get_stat(ONE, k, p) for p in range(groups)]
                center = sum(means[1:], means[0]) * (1.0 / groups)
                spread = get_stat(ONE + parts, k, 0)
                for p in range(1, groups):
                    spread += get_stat(ONE + parts, k, p)
                for mean in means:
                    spread += local * (mean - center) * (mean - center)
                inverse = lax.rsqrt(spread * (1.0 / channels) + eps)
                inv_one[kept, k : k + 1, :] = inverse
                normed = (x_one[:, s] - center) * inverse
                n_one[kept, :, s] = normed
                h = normed * col(GAIN1) + col(SHIFT1)
                hid[:, s] = h
                hid_low[:, s] = h.astype(bf16)
            pre[...] = mm(wup_t[...], hid_low[...])
            for j in range(hidden_units // local):
                units = slice(j * local, (j + 1) * local)
                for s in lanes:
                    u = pre[units, s] + b_up[units, :]
                    cdf = 0.5 + 0.5 * lax.erf(u * math.sqrt(0.5))
                    act[units, s] = (u * cdf).astype(bf16)
                    bell = jnp.exp2(u * u * (-0.5 * math.log2(math.e))) * (1.0 / math.sqrt(2.0 * math.pi))
                    slope[units, s] = cdf + u * bell
            branch = mm(wdown_t[...], act[...])
            gout_copy(r).wait()
            upstream[...] = pltpu.roll(gout_rows[r].astype(f32), place[r, 0], 1)
            for k, s in enumerate(lanes):
                x = hid[:, s] + branch[:, s] + col(B_DOWN)
                x_two[:, s] = x
                mean = row_sum(x) * (1.0 / local)
                off = x - mean
                scaled = upstream[:, s] * col(GAIN2)
                tile = (mean, row_sum(off * off), row_sum(scaled), row_sum(scaled * off))
                for n, value in enumerate(tile):
                    put_stat(TWO + n * parts, k, value)

        def stage_attend_back(r):
            slot = lax.rem(r, ring)
            blocks_ready(att_all, ATT, r)
            ctx_grad[...] = mm(
                wout_rows[...], att_all[lax.rem(r, ATT_SLOTS)].reshape(channels, seq)
            ).astype(bf16)
            factor = 1.0 / math.sqrt(HD)
            blocks = [(h, b) for h in range(HG) for b in range(SPLIT)]

            def at_block(part, n):
                h, b = blocks[n]
                start = part * local + h * HD
                return slice(start, start + HD), slice(b * half, (b + 1) * half)

            def piece(part, n):
                return mix_ring[slot, *at_block(part, n)]

            def spread(n):
                incoming = ctx_grad[at_block(0, n)]
                mix_grad[at_block(2, n)] = mm_nt(incoming, prob_ring[slot, n]).astype(bf16)

            def open_up(n):
                return mm_tn(piece(2, n), ctx_grad[at_block(0, n)])

            def center(n, prob_grad):
                at_n = at_block(0, n)
                inner = row_sum(ctx_grad[at_n].astype(f32) * ctx_all[lax.rem(r, CTX_SLOTS), g, *at_n].astype(f32))
                return (prob_ring[slot, n].astype(f32) * (prob_grad - inner)).astype(bf16)

            def queries(n, score_grad):
                mix_grad[at_block(0, n)] = (mm(piece(1, n), score_grad) * factor).astype(bf16)

            def keys(n, score_grad):
                mix_grad[at_block(1, n)] = (mm_nt(piece(0, n), score_grad) * factor).astype(bf16)

            held = {}
            for step in range(len(blocks) + 2):
                n = step - 0
                if 0 <= n < len(blocks):
                    held[0, n] = open_up(n)
                n = step - 0
                if 0 <= n < len(blocks):
                    spread(n)
                n = step - 1
                if 0 <= n < len(blocks):
                    held[1, n] = center(n, held.pop((0, n)))
                n = step - 2
                if 0 <= n < len(blocks):
                    queries(n, held[1, n])
                n = step - 2
                if 0 <= n < len(blocks):
                    keys(n, held.pop((1, n)))
            g_qkv[...] += mm_nt(mix_grad[...], x_ring[slot])
            blocks_sent(att_all, ATT, r)

            @pl.when(r >= 2)
            def _():
                grad_in_copy(r - 2).wait()

            total = mm(wqkv[...], mix_grad[...]) + rog_ring[lax.rem(r, rog_ring.shape[0])]
            gin_ring[lax.rem(r, 2)] = total
            grad_in_copy(r).start()
            base = 6 * local + hidden_units
            for n, start in ((0, 0), (1, 2 * local)):
                chunk = mix_grad[start : start + local, lanes[0]].astype(f32)
                for s in lanes[1:]:
                    chunk += mix_grad[start : start + local, s].astype(f32)
                sums[base + n * local : base + (n + 1) * local, :] += chunk

        def stage_feed_back(r):
            @pl.when(r >= 2)
            def _():
                result_copy(r - 2).wait()

            for k, s in enumerate(lanes):
                row = lambda p, n: get_stat(TWO + n * parts, k, p)
                means = [row(p, 0) for p in range(groups)]
                center = sum(means[1:], means[0]) * (1.0 / groups)
                spread, first, second = row(0, 1), row(0, 2), row(0, 3)
                for p in range(1, groups):
                    spread += row(p, 1)
                    first += row(p, 2)
                    second += row(p, 3)
                for p, mean in enumerate(means):
                    spread += local * (mean - center) * (mean - center)
                    second += (mean - center) * row(p, 2)
                inverse = lax.rsqrt(spread * (1.0 / channels) + eps)
                first = first * (1.0 / channels)
                second = second * inverse * (1.0 / channels)
                normed = (x_two[:, s] - center) * inverse
                res_ring[lax.rem(r, 2), :, s] = (normed * col(GAIN2) + col(SHIFT2)).astype(bf16)
                up = upstream[:, s]
                back = inverse * (up * col(GAIN2) - first - normed * second)
                rtg[:, s] = back
                low = back.astype(bf16)
                br_low[:, s] = low
                accumulate(S_GAIN2, up * normed)
                accumulate(S_SHIFT2, up)
                accumulate(S_BDOWN, low.astype(f32))
            result_copy(r).start()
            pre[...] = mm(wdown[...], br_low[...])
            g_down[...] += mm_nt(act[...], br_low[...])
            base = 6 * local
            for j in range(hidden_units // local):
                units = slice(j * local, (j + 1) * local)
                for s in lanes:
                    low = (slope[units, s] * pre[units, s]).astype(bf16)
                    pre_low[units, s] = low
                    sums[base + j * local : base + (j + 1) * local, :] += low.astype(f32)
            g_up[...] += mm_nt(pre_low[...], hid_low[...])
            change = mm(wup[...], pre_low[...])
            for k, s in enumerate(lanes):
                total = rtg[:, s] + change[:, s]
                hid_grad[lax.rem(r, (GRAD_LAG + 1)), :, s] = total
                normed = n_one[lax.rem(r, (NORM_BACK - FEED + 1)), :, s]
                scaled = total * col(GAIN1)
                put_stat(BACK, k, row_sum(scaled))
                put_stat(BACK + parts, k, row_sum(scaled * normed))
                accumulate(S_GAIN1, total * normed)
                accumulate(S_SHIFT1, total)

        def at(delay, stage):
            r = i - delay

            @pl.when(jnp.logical_and(r >= 0, r < rows))
            def _():
                stage(r)

        @pl.when(jnp.logical_and(i > RESIDUAL, i < rows + NORM_BACK))
        def _():
            stats_ready()

        at(FEED_BACK, stage_feed_back)
        at(FEED, stage_feed)
        at(RESIDUAL, stage_residual)

        @pl.when(jnp.logical_and(i >= RESIDUAL, i < rows + NORM_BACK - 1))
        def _():
            stats_send()

        at(0, stage_attend)
        at(NORM_BACK, stage_norm_back)

        @pl.when(i == rows - 1 + FEED_BACK)
        def _():
            for which in range(4):
                each_peer(lambda k, which=which: weight_copy(which, k, d).wait_send())
            for offset in range(1, groups):
                rows_copy(offset, g, lax.rem(g + offset, groups)).wait_send()
            send_grad(UP, g_up[...].T)
            send_grad(DOWN, g_down[...])

        @pl.when(i == rows - 1 + NORM_BACK)
        def _():
            send_grad(OUT, g_out[...])
            mine = all_sums.at[d]
            for n in range(6):
                mine[n : n + 1, :local] = row_sum(sums[n * local : (n + 1) * local, :].T)
            base = 6 * local
            mine[6:7, :] = row_sum(sums[base : base + hidden_units, :].T)

        at(PASS_CTX, lambda r: pass_on(ctx_all, CTX, r))
        at(DELAY, stage_attend_back)
        at(PASS_ATT, lambda r: pass_on(att_all, ATT, r))

        @pl.when(i == steps - 1)
        def _():
            send_grad(QKV, g_qkv[...].T)
            mine = all_sums.at[d]
            base = 6 * local + hidden_units
            mine[7:8, : 2 * local] = row_sum(sums[base : base + 2 * local, :].T)
            each_peer(lambda k: sums_copy(k, d).start())
            for which, out in ((UP, o_up), (DOWN, o_down), (OUT, o_out), (QKV, o_qkv)):
                grad_sum(which, out)
            each_peer(lambda k: sums_copy(k, lax.rem(d - k + dp, dp)).wait())
            o_sums[...] = jnp.sum(all_sums[...], axis=0)
        return carry

    lax.fori_loop(0, steps, step, 0)
    for r in (rows - 2, rows - 1):
        result_copy(r).wait()
        grad_in_copy(r).wait()


def run_layer(labels, inputs, grad_out, shards, b_qv, b_up, *vectors):
    groups = lax.axis_size("group")
    dp = lax.axis_size("dp")
    local, tok_count = inputs.shape
    rows, seq = labels.shape
    channels = groups * local
    half = seq // SPLIT
    parts = seq // LANES
    units = b_up.shape[1]
    ring = DELAY + 1
    vmem = pl.BlockSpec(memory_space=pltpu.VMEM)
    anywhere = pl.BlockSpec(memory_space=pl.ANY)
    acc_shapes = ((3 * local, local), (groups * local, local), (units, local), (units, local))
    sums_shape = (6 * local + units + 2 * local, LANES)
    shard_shapes = tuple(w.shape for w in shards)
    slots = tuple((dp, packed_rows(*s), LANES) for s in shard_shapes)
    row_sums = (8, units)
    block = (groups, local, seq)
    return pl.pallas_call(
        functools.partial(layer_kernel, rows, groups, dp),
        out_shape=(
            jax.ShapeDtypeStruct((local, tok_count), bf16),
            jax.ShapeDtypeStruct((local, tok_count), f32),
            *(jax.ShapeDtypeStruct(s, f32) for s in shard_shapes),
            jax.ShapeDtypeStruct(row_sums, f32),
            jax.ShapeDtypeStruct((rows, LANES), jnp.int32),
        ),
        in_specs=[vmem, anywhere, anywhere, *([vmem] * (len(shards) + 2 + len(vectors)))],
        out_specs=(anywhere, anywhere, *([vmem] * (len(shards) + 2))),
        scratch_shapes=[
            pltpu.SMEM((rows, LANES), jnp.int32),
            pltpu.VMEM((3 * local, LANES), f32),
            pltpu.VMEM((units, LANES), f32),
            pltpu.VMEM((6 * local, LANES), f32),
            pltpu.VMEM((rows, local, seq), bf16),
            pltpu.VMEM((rows, local, seq), bf16),
            pltpu.VMEM((2, local, seq), bf16),
            pltpu.VMEM((2, local, seq), f32),
            pltpu.VMEM((3 * local, local), bf16),
            pltpu.VMEM((local, 3 * local), bf16),
            pltpu.VMEM((local, channels), bf16),
            pltpu.VMEM((local, channels), bf16),
            pltpu.VMEM((units, local), bf16),
            pltpu.VMEM((local, units), bf16),
            pltpu.VMEM((local, units), bf16),
            pltpu.VMEM((units, local), bf16),
            *(pltpu.VMEM(s, bf16) for s in slots),
            pltpu.VMEM((groups, dp // groups, *slots[1][1:]), bf16),
            pltpu.VMEM((local, units), f32),
            pltpu.VMEM((units, local), f32),
            *(pltpu.VMEM(s, f32) for s in acc_shapes),
            pltpu.VMEM(sums_shape, f32),
            pltpu.VMEM((max(s[1] for s in slots), LANES), f32),
            *(pltpu.VMEM(s, bf16) for s in slots),
            pltpu.VMEM((dp, *row_sums), f32),
            pltpu.VMEM((CTX_SLOTS, *block), bf16),
            pltpu.VMEM((ATT_SLOTS, *block), bf16),
            pltpu.VMEM((rows + DELAY, groups, 8 * parts, LANES), f32),
            pltpu.VMEM((ring, local, seq), bf16),
            pltpu.VMEM((ring, 3 * local, seq), bf16),
            pltpu.VMEM((ring, HG * SPLIT, half, half), bf16),
            pltpu.VMEM((half, half), f32),
            pltpu.VMEM((local, seq), f32),
            pltpu.VMEM(((NORM_BACK - FEED + 1), local, seq), f32),
            pltpu.VMEM(((NORM_BACK - FEED + 1), parts, LANES), f32),
            pltpu.VMEM((local, seq), f32),
            pltpu.VMEM((local, seq), bf16),
            pltpu.VMEM((units, seq), f32),
            pltpu.VMEM((units, seq), bf16),
            pltpu.VMEM((units, seq), f32),
            pltpu.VMEM((local, seq), f32),
            pltpu.VMEM((local, seq), f32),
            pltpu.VMEM((local, seq), f32),
            pltpu.VMEM((local, seq), bf16),
            pltpu.VMEM((units, seq), bf16),
            pltpu.VMEM(((GRAD_LAG + 1), local, seq), f32),
            pltpu.VMEM((3, local, seq), f32),
            pltpu.VMEM((local, seq), bf16),
            pltpu.VMEM((3 * local, seq), bf16),
            pltpu.SemaphoreType.DMA((6, SEMS)),
            pltpu.SemaphoreType.DMA((6, SEMS)),
            pltpu.SemaphoreType.DMA((groups - 1, SEMS)),
            pltpu.SemaphoreType.DMA((groups - 1, SEMS)),
            pltpu.SemaphoreType.DMA((4, dp)),
            pltpu.SemaphoreType.DMA((4, dp)),
            pltpu.SemaphoreType.DMA((groups - 1,)),
            pltpu.SemaphoreType.DMA((groups - 1,)),
            pltpu.SemaphoreType.DMA((5, dp)),
            pltpu.SemaphoreType.DMA((5, dp)),
            pltpu.SemaphoreType.DMA((2, rows)),
            pltpu.SemaphoreType.DMA((2, 2)),
            pltpu.SemaphoreType.DMA,
        ],
        compiler_params=pltpu.CompilerParams(
            collective_id=0, has_side_effects=True, vmem_limit_bytes=63 << 20
        ),
        name="layer",
    )(labels, inputs, grad_out, *shards, b_qv, b_up, *(v.reshape(1, local) for v in vectors))


def finish_kernel(many, seq, result, grad_in, qkv, out, up, down, sums, place, *outs):
    i = pl.program_id(0)
    for n in range(many):
        toks = slice(n * seq, (n + 1) * seq)
        turn = place[i * many + n, 1]
        outs[0][:, toks] = pltpu.roll(result[:, toks].astype(f32), turn, 1).astype(bf16)
        outs[1][:, toks] = pltpu.roll(grad_in[:, toks], turn, 1)

    @pl.when(i == 0)
    def _():
        local = result.shape[0]
        for target, source in zip(outs[2:6], (qkv, out, up, down)):
            target[...] = source[...]
        for n in range(6):
            outs[6 + n][...] = sums[n : n + 1, :local]
        outs[12][...] = sums[6:7, :]
        outs[13][...] = sums[7:8, : 2 * local]


def finish(result, grad_in, *small):
    local, tok_count = result.shape
    rows = small[5].shape[0]
    seq = tok_count // rows
    units = small[4].shape[1]
    many = math.gcd(rows, FINISH_ROWS)
    block = pl.BlockSpec((local, many * seq), lambda i: (0, i))
    vmem = pl.BlockSpec(memory_space=pltpu.VMEM)
    shapes = (*(s.shape for s in small[:4]), *((1, local),) * 6, (1, units), (1, 2 * local))
    return pl.pallas_call(
        functools.partial(finish_kernel, many, seq),
        grid=(rows // many,),
        out_shape=(
            jax.ShapeDtypeStruct(result.shape, bf16),
            jax.ShapeDtypeStruct(grad_in.shape, f32),
            *(jax.ShapeDtypeStruct(s, f32) for s in shapes),
        ),
        in_specs=[block, block, *[vmem] * 5, pl.BlockSpec(memory_space=pltpu.SMEM)],
        out_specs=(block, block, *(vmem,) * len(shapes)),
        compiler_params=pltpu.CompilerParams(vmem_limit_bytes=60 << 20),
        name="finish",
    )(result, grad_in, *small)


def per_device(
    inputs,
    labels,
    w_qkv,
    b_qv,
    w_out,
    b_out,
    gain_one,
    shift_one,
    w_up,
    b_up,
    down_weight,
    down_bias,
    gain_two,
    shift_two,
    grad_out,
):
    shards = (w_qkv[0], w_out, w_up[0], down_weight[0])
    vectors = (b_out, gain_one, shift_one, down_bias, gain_two, shift_two)
    raw = run_layer(labels, inputs, grad_out, shards, b_qv, b_up, *vectors)
    result, input_grad, qkv, out, up, down, *sums = finish(*raw)
    flat = [s.reshape(-1) for s in sums]
    return (
        result,
        input_grad,
        qkv[None],
        sums[7],
        out,
        flat[0],
        flat[1],
        flat[2],
        up[None],
        sums[6],
        down[None],
        sums[3],
        flat[4],
        flat[5],
    )


def solution(mesh):
    placed = (
        P("group", "dp"),
        P("dp", None),
        P("group", "dp", None),
        P("group", None),
        P("dp", "group"),
        P("group"),
        P("group"),
        P("group"),
        P("group", "dp", None),
        P("group", None),
        P("group", "dp", None),
        P("group", None),
        P("group"),
        P("group"),
        P("group", "dp"),
    )
    return jax.shard_map(
        per_device,
        mesh=mesh,
        in_specs=placed,
        out_specs=(
            P("group", "dp"),
            P("group", "dp"),
            P("group", "dp", None),
            P("group", None),
            P("dp", "group"),
            P("group"),
            P("group"),
            P("group"),
            P("group", "dp", None),
            P("group", None),
            P("group", "dp", None),
            P("group", None),
            P("group"),
            P("group"),
        ),
        check_vma=False,
    )
```

```python
import functools
import math

import jax
import jax.numpy as jnp
from jax import lax
from jax.experimental import pallas as pl
from jax.experimental.pallas import tpu as pltpu
from jax.sharding import PartitionSpec as P

HD = 64
HG = 3
LANES = 128
SPLIT = 2
FINISH_ROWS = 8
PASS_CTX, RESIDUAL, FEED, FEED_BACK, NORM_BACK, PASS_ATT, DELAY = 1, 3, 4, 5, 7, 8, 9
CTX_SLOTS, ATT_SLOTS, SEMS = DELAY + 1, 5, 5
FLATS = 4
GRAD_LAG = NORM_BACK - FEED_BACK

eps = 1e-12
f32 = jnp.float32
bf16 = jnp.bfloat16
MESH = pl.DeviceIdType.MESH


def mm(left, right):
    return jnp.dot(left, right, preferred_element_type=f32)


def mm_nt(left, right):
    return lax.dot_general(left, right, (((1,), (1,)), ((), ())), preferred_element_type=f32)


def mm_tn(left, right):
    return lax.dot_general(left, right, (((0,), (0,)), ((), ())), preferred_element_type=f32)


def packed_rows(count, width):
    tail = 0 if width % LANES == 0 else count // (2 - count % 2)
    return -(-(width // LANES * count + tail) // 16) * 16


def pack(into, x):
    count, width = x.shape
    whole = width // LANES
    for k in range(whole):
        into[k * count : (k + 1) * count, :] = x[:, k * LANES : (k + 1) * LANES]
    if width % LANES:
        left = width - whole * LANES
        folds = 2 - count % 2
        part = count // folds
        for n in range(folds):
            into[whole * count : whole * count + part, n * left : (n + 1) * left] = x[
                n * part : (n + 1) * part, whole * LANES :
            ]


def unpack(into, start, count, width, x):
    whole = width // LANES
    for k in range(whole):
        into[start : start + count, k * LANES : (k + 1) * LANES] = x[k * count : (k + 1) * count, :]
    if width % LANES:
        left = width - whole * LANES
        folds = 2 - count % 2
        part = count // folds
        for n in range(folds):
            into[start + n * part : start + (n + 1) * part, whole * LANES : width] = x[
                whole * count : whole * count + part, n * left : (n + 1) * left
            ]


def row_sum(x):
    return jnp.sum(x, axis=0, keepdims=True)


def remote(src, dst, send, recv, device):
    return pltpu.make_async_remote_copy(
        src_ref=src, dst_ref=dst, send_sem=send, recv_sem=recv, device_id=device, device_id_type=MESH
    )


def layer_kernel(
    rows,
    groups,
    dp,
    labels,
    inp,
    gout_in,
    w_qkv,
    w_out,
    w_up,
    w_down,
    in_qv,
    in_up,
    in_out,
    in_gain_one,
    in_shift_one,
    in_down,
    in_gain_two,
    in_shift_two,
    result,
    grad_in,
    o_qkv,
    o_out,
    o_up,
    o_down,
    o_sums,
    o_place,
    place,
    b_qkv,
    b_up,
    cols,
    inp_rows,
    gout_rows,
    res_ring,
    gin_ring,
    wqkv_t,
    wqkv,
    wout_t,
    wout_rows,
    wup_t,
    wup,
    wdown_t,
    wdown,
    all_qkv,
    all_out,
    all_up,
    all_down,
    out_rows,
    wide_mat,
    tall_mat,
    g_qkv,
    g_out,
    g_up,
    g_down,
    sums,
    flats,
    land_qkv,
    land_out,
    land_up,
    land_down,
    all_sums,
    ctx_all,
    att_all,
    stats,
    x_ring,
    mix_ring,
    prob_ring,
    mask,
    x_one,
    n_one,
    inv_one,
    hid,
    hid_low,
    pre,
    act,
    slope,
    x_two,
    upstream,
    rtg,
    br_low,
    pre_low,
    hid_grad,
    rog_ring,
    ctx_grad,
    mix_grad,
    send_blocks,
    recv_blocks,
    send_stats,
    recv_stats,
    send_weights,
    recv_weights,
    send_rows,
    recv_rows,
    send_grads,
    recv_grads,
    fetch,
    store,
    place_sem,
):
    steps = rows + DELAY
    local = w_out.shape[1]
    seq = inp.shape[1] // rows

    def inp_copy(r):
        toks = pl.ds(pl.multiple_of(r * seq, seq), seq)
        return pltpu.make_async_copy(inp.at[:, toks], inp_rows.at[r], fetch.at[0, r])

    def gout_copy(r):
        toks = pl.ds(pl.multiple_of(r * seq, seq), seq)
        return pltpu.make_async_copy(gout_in.at[:, toks], gout_rows.at[r], fetch.at[1, r])

    def result_copy(r):
        slot = lax.rem(r, 2)
        return pltpu.make_async_copy(res_ring.at[slot], result.at[r], store.at[0, slot])

    def grad_in_copy(r):
        slot = lax.rem(r, 2)
        return pltpu.make_async_copy(gin_ring.at[slot], grad_in.at[r], store.at[1, slot])

    def find_places():
        ids = labels[...]
        counts = [
            jnp.sum(jnp.where(ids == v, 1.0, 0.0), axis=1, keepdims=True) for v in range(4)
        ]
        start = jnp.zeros_like(counts[0])
        first = jnp.zeros_like(start)
        second = jnp.zeros_like(start)
        found = jnp.zeros_like(start)
        begin = jnp.zeros_like(start)
        for v in range(4):
            hit = jnp.where(counts[v] == seq // SPLIT, 1.0 - found, 0.0)
            start = start + hit * begin
            first = first + hit * counts[(v + 1) % 4]
            second = second + hit * (counts[(v + 1) % 4] + counts[(v + 2) % 4])
            found = found + hit
            begin = begin + counts[v]
        turn = jnp.where(start == 0.0, 0.0, seq - start)
        lane = lax.broadcasted_iota(jnp.int32, (rows, LANES), 1)
        table = jnp.zeros((rows, LANES), f32)
        for n, value in enumerate((turn, start, first, second)):
            table = jnp.where(lane == n, value, table)
        o_place[...] = table.astype(jnp.int32)
        copy = pltpu.make_async_copy(o_place, place, place_sem)
        copy.start()
        copy.wait()

    def spread_vectors():
        def column(row):
            return jnp.broadcast_to(row, (LANES, row.shape[1])).T

        qv = column(in_qv[...])
        b_qkv[:local, :] = qv[:local]
        b_qkv[local : 2 * local, :] = jnp.zeros((local, LANES), f32)
        b_qkv[2 * local :, :] = qv[local:]
        b_up[...] = column(in_up[...])
        vectors = (in_out, in_gain_one, in_shift_one, in_down, in_gain_two, in_shift_two)
        for n, ref in enumerate(vectors):
            cols[n * local : (n + 1) * local, :] = column(ref[...])

    def step(i, carry):
        g = lax.axis_index("group")
        d = lax.axis_index("dp")
        across = lax.rem(g + 2, groups)
        beside = g + 1 - 2 * lax.rem(g, 2)
        corner = lax.rem(beside + 2, groups)
        half = seq // SPLIT
        channels = local * groups
        parts = seq // LANES
        hidden_units = wup_t.shape[0]
        ring = x_ring.shape[0]
        lanes = [slice(k * LANES, (k + 1) * LANES) for k in range(parts)]
        col = lambda n: cols[n * local : (n + 1) * local, :]
        B_OUT, GAIN1, SHIFT1, B_DOWN, GAIN2, SHIFT2 = range(6)
        S_BOUT, S_GAIN1, S_SHIFT1, S_BDOWN, S_GAIN2, S_SHIFT2 = range(6)

        def accumulate(slot, chunk):
            sums[slot * local : (slot + 1) * local, :] += chunk

        def block_copy(buf, base, kind, r, slot):
            peer = across if kind == 0 else beside
            at_row = lax.rem(r, buf.shape[0])
            return remote(
                buf.at[at_row, slot],
                buf.at[at_row, slot],
                send_blocks.at[base + kind, lax.rem(r, SEMS)],
                recv_blocks.at[base + kind, lax.rem(r, SEMS)],
                {"group": peer},
            )

        def send_own(buf, base, r):
            block_copy(buf, base, 0, r, g).start()
            block_copy(buf, base, 1, r, g).start()

        def pass_on(buf, base, r):
            block_copy(buf, base, 0, r, across).wait_recv()
            block_copy(buf, base, 2, r, across).start()

        def blocks_ready(buf, base, r):
            block_copy(buf, base, 1, r, beside).wait_recv()
            block_copy(buf, base, 2, r, corner).wait_recv()

        def blocks_sent(buf, base, r):
            block_copy(buf, base, 0, r, g).wait_send()
            block_copy(buf, base, 1, r, g).wait_send()
            block_copy(buf, base, 2, r, across).wait_send()

        def stat_copy(step, offset, slot):
            return remote(
                stats.at[step, slot],
                stats.at[step, slot],
                send_stats.at[offset - 1, lax.rem(step, SEMS)],
                recv_stats.at[offset - 1, lax.rem(step, SEMS)],
                {"group": lax.rem(g + offset, groups)},
            )

        def stats_send():
            for offset in range(1, groups):
                stat_copy(i, offset, g).start()

        def stats_ready():
            for offset in range(1, groups):
                stat_copy(i - 1, offset, lax.rem(g + groups - offset, groups)).wait_recv()
                stat_copy(i - 1, offset, g).wait_send()

        def put_stat(first, k, value):
            stats[i, g, first + k : first + k + 1, :] = value

        def get_stat(first, k, p, ago=1):
            return stats[i - ago, p, first + k : first + k + 1, :]

        ONE, TWO, BACK = 0, 2 * parts, 6 * parts
        CTX, ATT = 0, 3

        shards = (w_qkv, w_out, w_up, w_down)
        fulls = (all_qkv, all_out, all_up, all_down)
        QKV, OUT, UP, DOWN = range(4)

        def weight_copy(which, k, slot):
            full = fulls[which]
            return remote(
                full.at[slot],
                full.at[slot],
                send_weights.at[which, k],
                recv_weights.at[which, k],
                {"dp": lax.rem(d + k, dp)},
            )

        def each_peer(action):
            def body(k, carry):
                action(k)
                return carry

            lax.fori_loop(1, dp, body, 0)

        def weights_ready(which, into):
            each_peer(lambda k: weight_copy(which, k, lax.rem(d - k + dp, dp)).wait_recv())
            count, width = shards[which].shape
            for slot in range(dp):
                unpack(into, slot * count, count, width, fulls[which][slot].astype(f32))

        per = dp // groups

        def rows_copy(offset, source, target):
            return remote(
                all_out.at[pl.ds(target * per, per)],
                out_rows.at[source],
                send_rows.at[offset - 1],
                recv_rows.at[offset - 1],
                {"group": target},
            )

        @pl.when(i == 0)
        def _():
            barrier = pltpu.get_barrier_semaphore()
            for offset in range(1, groups):
                pl.semaphore_signal(
                    barrier, inc=1, device_id={"group": lax.rem(g + offset, groups)}, device_id_type=MESH
                )
            each_peer(
                lambda k: pl.semaphore_signal(
                    barrier, inc=1, device_id={"dp": lax.rem(d + k, dp)}, device_id_type=MESH
                )
            )
            flats[...] = jnp.zeros_like(flats)

            def pack_shard(which):
                buffer = flats.at[which]
                pack(buffer, shards[which][...])
                fulls[which][d] = buffer[: fulls[which].shape[1], :].astype(bf16)

            pack_shard(QKV)
            pl.semaphore_wait(barrier, groups - 1 + dp - 1)
            each_peer(lambda k: weight_copy(QKV, k, d).start())
            for which in (OUT, UP, DOWN):
                pack_shard(which)

            def fetch_row(r, carry):
                inp_copy(r).start()
                gout_copy(r).start()
                return carry

            lax.fori_loop(0, rows, fetch_row, 0)
            find_places()
            spread_vectors()
            for ref in (g_qkv, g_out, g_up, g_down, sums):
                ref[...] = jnp.zeros_like(ref)
            weights_ready(QKV, wide_mat)
            each_peer(lambda k: weight_copy(OUT, k, d).start())
            mat = wide_mat[:, : 3 * local]
            wqkv[...] = mat.astype(bf16)
            wqkv_t[...] = mat.T.astype(bf16)

        @pl.when(i == 1)
        def _():
            for which in (UP, DOWN):
                each_peer(lambda k, which=which: weight_copy(which, k, d).start())

        @pl.when(i == RESIDUAL)
        def _():
            weights_ready(OUT, tall_mat)
            for offset in range(1, groups):
                rows_copy(offset, g, lax.rem(g + offset, groups)).start()
            out_rows[g] = all_out[pl.ds(g * per, per)]
            wout_t[...] = tall_mat[...].T.astype(bf16)

        @pl.when(i == FEED)
        def _():
            weights_ready(UP, wide_mat)
            mat = wide_mat[...]
            wup[...] = mat.astype(bf16)
            wup_t[...] = mat.T.astype(bf16)
            weights_ready(DOWN, tall_mat)
            mat = tall_mat[...]
            wdown[...] = mat.astype(bf16)
            wdown_t[...] = mat.T.astype(bf16)

        @pl.when(i == DELAY)
        def _():
            for offset in range(1, groups):
                rows_copy(offset, lax.rem(g + groups - offset, groups), g).wait_recv()
            count = local // per
            for p in range(groups):
                for n in range(per):
                    unpack(wide_mat, n * count, count, local, out_rows[p, n].astype(f32))
                tall_mat[p * local : (p + 1) * local, :] = wide_mat[:, :local].T
            wout_rows[...] = tall_mat[...].T.astype(bf16)

        stages = fulls
        lands = (land_qkv, land_out, land_up, land_down)

        def grad_copy(which, k, slot):
            return remote(
                stages[which].at[lax.rem(d + k, dp)],
                lands[which].at[slot],
                send_grads.at[which, k],
                recv_grads.at[which, k],
                {"dp": lax.rem(d + k, dp)},
            )

        def sums_copy(k, slot):
            return remote(
                all_sums.at[slot],
                all_sums.at[slot],
                send_grads.at[4, k],
                recv_grads.at[4, k],
                {"dp": lax.rem(d + k, dp)},
            )

        def send_grad(which, mat):
            stage = stages[which]
            count = shards[which].shape[0]
            for slot in range(dp):
                buffer = flats.at[slot % FLATS]
                pack(buffer, mat[slot * count : (slot + 1) * count])
                stage[slot] = buffer[: stage.shape[1], :].astype(bf16)
            each_peer(lambda k: grad_copy(which, k, d).start())

        def grad_sum(which, out):
            count = stages[which].shape[1]
            flat = flats.at[which]
            flat[:count, :] = stages[which][d].astype(f32)

            def add(k):
                slot = lax.rem(d - k + dp, dp)
                grad_copy(which, k, slot).wait()
                flat[:count, :] += lands[which][slot].astype(f32)

            each_peer(add)
            unpack(out, 0, *out.shape, flat[...])

        def stage_residual(r):
            blocks_ready(ctx_all, CTX, r)
            attended = mm(wout_t[...], ctx_all[lax.rem(r, CTX_SLOTS)].reshape(channels, seq))
            xr = x_ring.at[lax.rem(r, ring)]
            for k, s in enumerate(lanes):
                x = xr[:, s].astype(f32) + attended[:, s] + col(B_OUT)
                x_one[:, s] = x
                mean = row_sum(x) * (1.0 / local)
                off = x - mean
                put_stat(ONE, k, mean)
                put_stat(ONE + parts, k, row_sum(off * off))
            blocks_sent(ctx_all, CTX, r)

        def stage_attend(r):
            slot = lax.rem(r, ring)
            inp_copy(r).wait()
            rolled = pltpu.roll(inp_rows[r].astype(f32), place[r, 0], 1).astype(bf16)
            x_ring[slot] = rolled
            mixed = mm(wqkv_t[...], rolled)
            for s in lanes:
                mix_ring[slot, :, s] = (mixed[:, s] + b_qkv[...]).astype(bf16)
            first, second = place[r, 2], place[r, 3]
            down = lax.broadcasted_iota(jnp.int32, (half, half), 0)
            along = lax.broadcasted_iota(jnp.int32, (half, half), 1)
            own = lambda at: (at >= first).astype(jnp.int32) + (at >= second).astype(jnp.int32)
            mask[...] = jnp.where(own(down) == own(along), 0.0, -1000000000.0)
            scale = math.log2(math.e) / math.sqrt(HD)
            blocks = [(h, b) for h in range(HG) for b in range(SPLIT)]

            def piece(part, n):
                h, b = blocks[n]
                start = part * local + h * HD
                return mix_ring[slot, start : start + HD, b * half : (b + 1) * half]

            def score(n):
                return mm_tn(piece(1, n), piece(0, n))

            def soften(n, scores):
                if blocks[n][1]:
                    scores = scores + mask[...]
                highest = jnp.max(scores, axis=0, keepdims=True)
                return jnp.exp2((scores - highest) * scale)

            def norm(n, exponent):
                chances = (exponent * (1.0 / row_sum(exponent))).astype(bf16)
                prob_ring[slot, n] = chances
                return chances

            def blend(n, chances):
                h, b = blocks[n]
                ctx_all[lax.rem(r, CTX_SLOTS), g, h * HD : (h + 1) * HD, b * half : (b + 1) * half] = mm(
                    piece(2, n), chances
                ).astype(bf16)

            held = {}
            for step in range(len(blocks) + 3):
                n = step - 0
                if 0 <= n < len(blocks):
                    held[0, n] = score(n)
                n = step - 1
                if 0 <= n < len(blocks):
                    held[1, n] = soften(n, held.pop((0, n)))
                n = step - 2
                if 0 <= n < len(blocks):
                    held[2, n] = norm(n, held.pop((1, n)))
                n = step - 3
                if 0 <= n < len(blocks):
                    blend(n, held.pop((2, n)))
            send_own(ctx_all, CTX, r)

        def stage_norm_back(r):
            slot = lax.rem(r, rog_ring.shape[0])
            kept = lax.rem(r, (NORM_BACK - FEED + 1))
            for k, s in enumerate(lanes):
                first = get_stat(BACK, k, 0, GRAD_LAG)
                second = get_stat(BACK + parts, k, 0, GRAD_LAG)
                for p in range(1, groups):
                    first += get_stat(BACK, k, p, GRAD_LAG)
                    second += get_stat(BACK + parts, k, p, GRAD_LAG)
                first = first * (1.0 / channels)
                second = second * (1.0 / channels)
                scaled = hid_grad[lax.rem(r, (GRAD_LAG + 1)), :, s] * col(GAIN1)
                back = inv_one[kept, k : k + 1, :] * (scaled - first - n_one[kept, :, s] * second)
                rog_ring[slot, :, s] = back
                low = back.astype(bf16)
                att_all[lax.rem(r, ATT_SLOTS), g, :, s] = low
                accumulate(S_BOUT, low.astype(f32))
            send_own(att_all, ATT, r)
            contexts = ctx_all[lax.rem(r, CTX_SLOTS)].reshape(channels, seq)
            g_out[...] += mm_nt(contexts, att_all[lax.rem(r, ATT_SLOTS), g])

        def stage_feed(r):
            kept = lax.rem(r, (NORM_BACK - FEED + 1))
            for k, s in enumerate(lanes):
                means = [get_stat(ONE, k, p) for p in range(groups)]
                center = sum(means[1:], means[0]) * (1.0 / groups)
                spread = get_stat(ONE + parts, k, 0)
                for p in range(1, groups):
                    spread += get_stat(ONE + parts, k, p)
                for mean in means:
                    spread += local * (mean - center) * (mean - center)
                inverse = lax.rsqrt(spread * (1.0 / channels) + eps)
                inv_one[kept, k : k + 1, :] = inverse
                normed = (x_one[:, s] - center) * inverse
                n_one[kept, :, s] = normed
                h = normed * col(GAIN1) + col(SHIFT1)
                hid[:, s] = h
                hid_low[:, s] = h.astype(bf16)
            pre[...] = mm(wup_t[...], hid_low[...])
            for j in range(hidden_units // local):
                units = slice(j * local, (j + 1) * local)
                for s in lanes:
                    u = pre[units, s] + b_up[units, :]
                    cdf = 0.5 + 0.5 * lax.erf(u * math.sqrt(0.5))
                    act[units, s] = (u * cdf).astype(bf16)
                    bell = jnp.exp2(u * u * (-0.5 * math.log2(math.e))) * (1.0 / math.sqrt(2.0 * math.pi))
                    slope[units, s] = cdf + u * bell
            branch = mm(wdown_t[...], act[...])
            gout_copy(r).wait()
            upstream[...] = pltpu.roll(gout_rows[r].astype(f32), place[r, 0], 1)
            for k, s in enumerate(lanes):
                x = hid[:, s] + branch[:, s] + col(B_DOWN)
                x_two[:, s] = x
                mean = row_sum(x) * (1.0 / local)
                off = x - mean
                scaled = upstream[:, s] * col(GAIN2)
                tile = (mean, row_sum(off * off), row_sum(scaled), row_sum(scaled * off))
                for n, value in enumerate(tile):
                    put_stat(TWO + n * parts, k, value)

        def stage_attend_back(r):
            slot = lax.rem(r, ring)
            blocks_ready(att_all, ATT, r)
            ctx_grad[...] = mm(
                wout_rows[...], att_all[lax.rem(r, ATT_SLOTS)].reshape(channels, seq)
            ).astype(bf16)
            factor = 1.0 / math.sqrt(HD)
            blocks = [(h, b) for h in range(HG) for b in range(SPLIT)]

            def at_block(part, n):
                h, b = blocks[n]
                start = part * local + h * HD
                return slice(start, start + HD), slice(b * half, (b + 1) * half)

            def piece(part, n):
                return mix_ring[slot, *at_block(part, n)]

            def spread(n):
                incoming = ctx_grad[at_block(0, n)]
                mix_grad[at_block(2, n)] = mm_nt(incoming, prob_ring[slot, n]).astype(bf16)

            def open_up(n):
                return mm_tn(piece(2, n), ctx_grad[at_block(0, n)])

            def center(n, prob_grad):
                at_n = at_block(0, n)
                inner = row_sum(ctx_grad[at_n].astype(f32) * ctx_all[lax.rem(r, CTX_SLOTS), g, *at_n].astype(f32))
                return (prob_ring[slot, n].astype(f32) * (prob_grad - inner)).astype(bf16)

            def queries(n, score_grad):
                mix_grad[at_block(0, n)] = (mm(piece(1, n), score_grad) * factor).astype(bf16)

            def keys(n, score_grad):
                mix_grad[at_block(1, n)] = (mm_nt(piece(0, n), score_grad) * factor).astype(bf16)

            held = {}
            for step in range(len(blocks) + 2):
                n = step - 0
                if 0 <= n < len(blocks):
                    held[0, n] = open_up(n)
                n = step - 0
                if 0 <= n < len(blocks):
                    spread(n)
                n = step - 1
                if 0 <= n < len(blocks):
                    held[1, n] = center(n, held.pop((0, n)))
                n = step - 2
                if 0 <= n < len(blocks):
                    queries(n, held[1, n])
                n = step - 2
                if 0 <= n < len(blocks):
                    keys(n, held.pop((1, n)))
            g_qkv[...] += mm_nt(mix_grad[...], x_ring[slot])
            blocks_sent(att_all, ATT, r)

            @pl.when(r >= 2)
            def _():
                grad_in_copy(r - 2).wait()

            total = mm(wqkv[...], mix_grad[...]) + rog_ring[lax.rem(r, rog_ring.shape[0])]
            gin_ring[lax.rem(r, 2)] = total
            grad_in_copy(r).start()
            base = 6 * local + hidden_units
            for n, start in ((0, 0), (1, 2 * local)):
                chunk = mix_grad[start : start + local, lanes[0]].astype(f32)
                for s in lanes[1:]:
                    chunk += mix_grad[start : start + local, s].astype(f32)
                sums[base + n * local : base + (n + 1) * local, :] += chunk

        def stage_feed_back(r):
            @pl.when(r >= 2)
            def _():
                result_copy(r - 2).wait()

            for k, s in enumerate(lanes):
                row = lambda p, n: get_stat(TWO + n * parts, k, p)
                means = [row(p, 0) for p in range(groups)]
                center = sum(means[1:], means[0]) * (1.0 / groups)
                spread, first, second = row(0, 1), row(0, 2), row(0, 3)
                for p in range(1, groups):
                    spread += row(p, 1)
                    first += row(p, 2)
                    second += row(p, 3)
                for p, mean in enumerate(means):
                    spread += local * (mean - center) * (mean - center)
                    second += (mean - center) * row(p, 2)
                inverse = lax.rsqrt(spread * (1.0 / channels) + eps)
                first = first * (1.0 / channels)
                second = second * inverse * (1.0 / channels)
                normed = (x_two[:, s] - center) * inverse
                res_ring[lax.rem(r, 2), :, s] = (normed * col(GAIN2) + col(SHIFT2)).astype(bf16)
                up = upstream[:, s]
                back = inverse * (up * col(GAIN2) - first - normed * second)
                rtg[:, s] = back
                low = back.astype(bf16)
                br_low[:, s] = low
                accumulate(S_GAIN2, up * normed)
                accumulate(S_SHIFT2, up)
                accumulate(S_BDOWN, low.astype(f32))
            result_copy(r).start()
            pre[...] = mm(wdown[...], br_low[...])
            g_down[...] += mm_nt(act[...], br_low[...])
            base = 6 * local
            for j in range(hidden_units // local):
                units = slice(j * local, (j + 1) * local)
                for s in lanes:
                    low = (slope[units, s] * pre[units, s]).astype(bf16)
                    pre_low[units, s] = low
                    sums[base + j * local : base + (j + 1) * local, :] += low.astype(f32)
            g_up[...] += mm_nt(pre_low[...], hid_low[...])
            change = mm(wup[...], pre_low[...])
            for k, s in enumerate(lanes):
                total = rtg[:, s] + change[:, s]
                hid_grad[lax.rem(r, (GRAD_LAG + 1)), :, s] = total
                normed = n_one[lax.rem(r, (NORM_BACK - FEED + 1)), :, s]
                scaled = total * col(GAIN1)
                put_stat(BACK, k, row_sum(scaled))
                put_stat(BACK + parts, k, row_sum(scaled * normed))
                accumulate(S_GAIN1, total * normed)
                accumulate(S_SHIFT1, total)

        def at(delay, stage):
            r = i - delay

            @pl.when(jnp.logical_and(r >= 0, r < rows))
            def _():
                stage(r)

        @pl.when(jnp.logical_and(i > RESIDUAL, i < rows + NORM_BACK))
        def _():
            stats_ready()

        at(FEED_BACK, stage_feed_back)
        at(FEED, stage_feed)
        at(RESIDUAL, stage_residual)

        @pl.when(jnp.logical_and(i >= RESIDUAL, i < rows + NORM_BACK - 1))
        def _():
            stats_send()

        at(0, stage_attend)
        at(NORM_BACK, stage_norm_back)

        @pl.when(i == rows - 1 + FEED_BACK)
        def _():
            for which in range(4):
                each_peer(lambda k, which=which: weight_copy(which, k, d).wait_send())
            for offset in range(1, groups):
                rows_copy(offset, g, lax.rem(g + offset, groups)).wait_send()
            send_grad(UP, g_up[...].T)
            send_grad(DOWN, g_down[...])

        @pl.when(i == rows - 1 + NORM_BACK)
        def _():
            send_grad(OUT, g_out[...])
            mine = all_sums.at[d]
            for n in range(6):
                mine[n : n + 1, :local] = row_sum(sums[n * local : (n + 1) * local, :].T)
            base = 6 * local
            mine[6:7, :] = row_sum(sums[base : base + hidden_units, :].T)

        at(PASS_CTX, lambda r: pass_on(ctx_all, CTX, r))
        at(DELAY, stage_attend_back)
        at(PASS_ATT, lambda r: pass_on(att_all, ATT, r))

        @pl.when(i == steps - 1)
        def _():
            send_grad(QKV, g_qkv[...].T)
            mine = all_sums.at[d]
            base = 6 * local + hidden_units
            mine[7:8, : 2 * local] = row_sum(sums[base : base + 2 * local, :].T)
            each_peer(lambda k: sums_copy(k, d).start())
            for which, out in ((UP, o_up), (DOWN, o_down), (OUT, o_out), (QKV, o_qkv)):
                grad_sum(which, out)
            each_peer(lambda k: sums_copy(k, lax.rem(d - k + dp, dp)).wait())
            o_sums[...] = jnp.sum(all_sums[...], axis=0)
        return carry

    lax.fori_loop(0, steps, step, 0)
    for r in (rows - 2, rows - 1):
        result_copy(r).wait()
        grad_in_copy(r).wait()


def run_layer(labels, inputs, grad_out, shards, b_qv, b_up, *vectors):
    groups = lax.axis_size("group")
    dp = lax.axis_size("dp")
    local, tok_count = inputs.shape
    rows, seq = labels.shape
    channels = groups * local
    half = seq // SPLIT
    parts = seq // LANES
    units = b_up.shape[1]
    ring = DELAY + 1
    vmem = pl.BlockSpec(memory_space=pltpu.VMEM)
    anywhere = pl.BlockSpec(memory_space=pl.ANY)
    acc_shapes = ((3 * local, local), (groups * local, local), (units, local), (units, local))
    sums_shape = (6 * local + units + 2 * local, LANES)
    shard_shapes = tuple(w.shape for w in shards)
    slots = tuple((dp, packed_rows(*s), LANES) for s in shard_shapes)
    row_sums = (8, units)
    block = (groups, local, seq)
    return pl.pallas_call(
        functools.partial(layer_kernel, rows, groups, dp),
        out_shape=(
            jax.ShapeDtypeStruct((rows, local, seq), bf16),
            jax.ShapeDtypeStruct((rows, local, seq), f32),
            *(jax.ShapeDtypeStruct(s, f32) for s in shard_shapes),
            jax.ShapeDtypeStruct(row_sums, f32),
            jax.ShapeDtypeStruct((rows, LANES), jnp.int32),
        ),
        in_specs=[vmem, anywhere, anywhere, *([vmem] * (len(shards) + 2 + len(vectors)))],
        out_specs=(anywhere, anywhere, *([vmem] * (len(shards) + 2))),
        scratch_shapes=[
            pltpu.SMEM((rows, LANES), jnp.int32),
            pltpu.VMEM((3 * local, LANES), f32),
            pltpu.VMEM((units, LANES), f32),
            pltpu.VMEM((6 * local, LANES), f32),
            pltpu.VMEM((rows, local, seq), bf16),
            pltpu.VMEM((rows, local, seq), bf16),
            pltpu.VMEM((2, local, seq), bf16),
            pltpu.VMEM((2, local, seq), f32),
            pltpu.VMEM((3 * local, local), bf16),
            pltpu.VMEM((local, 3 * local), bf16),
            pltpu.VMEM((local, channels), bf16),
            pltpu.VMEM((local, channels), bf16),
            pltpu.VMEM((units, local), bf16),
            pltpu.VMEM((local, units), bf16),
            pltpu.VMEM((local, units), bf16),
            pltpu.VMEM((units, local), bf16),
            *(pltpu.VMEM(s, bf16) for s in slots),
            pltpu.VMEM((groups, dp // groups, *slots[1][1:]), bf16),
            pltpu.VMEM((local, units), f32),
            pltpu.VMEM((units, local), f32),
            *(pltpu.VMEM(s, f32) for s in acc_shapes),
            pltpu.VMEM(sums_shape, f32),
            pltpu.VMEM((FLATS, max(s[1] for s in slots), LANES), f32),
            *(pltpu.VMEM(s, bf16) for s in slots),
            pltpu.VMEM((dp, *row_sums), f32),
            pltpu.VMEM((CTX_SLOTS, *block), bf16),
            pltpu.VMEM((ATT_SLOTS, *block), bf16),
            pltpu.VMEM((rows + DELAY, groups, 8 * parts, LANES), f32),
            pltpu.VMEM((ring, local, seq), bf16),
            pltpu.VMEM((ring, 3 * local, seq), bf16),
            pltpu.VMEM((ring, HG * SPLIT, half, half), bf16),
            pltpu.VMEM((half, half), f32),
            pltpu.VMEM((local, seq), f32),
            pltpu.VMEM(((NORM_BACK - FEED + 1), local, seq), f32),
            pltpu.VMEM(((NORM_BACK - FEED + 1), parts, LANES), f32),
            pltpu.VMEM((local, seq), f32),
            pltpu.VMEM((local, seq), bf16),
            pltpu.VMEM((units, seq), f32),
            pltpu.VMEM((units, seq), bf16),
            pltpu.VMEM((units, seq), f32),
            pltpu.VMEM((local, seq), f32),
            pltpu.VMEM((local, seq), f32),
            pltpu.VMEM((local, seq), f32),
            pltpu.VMEM((local, seq), bf16),
            pltpu.VMEM((units, seq), bf16),
            pltpu.VMEM(((GRAD_LAG + 1), local, seq), f32),
            pltpu.VMEM((3, local, seq), f32),
            pltpu.VMEM((local, seq), bf16),
            pltpu.VMEM((3 * local, seq), bf16),
            pltpu.SemaphoreType.DMA((6, SEMS)),
            pltpu.SemaphoreType.DMA((6, SEMS)),
            pltpu.SemaphoreType.DMA((groups - 1, SEMS)),
            pltpu.SemaphoreType.DMA((groups - 1, SEMS)),
            pltpu.SemaphoreType.DMA((4, dp)),
            pltpu.SemaphoreType.DMA((4, dp)),
            pltpu.SemaphoreType.DMA((groups - 1,)),
            pltpu.SemaphoreType.DMA((groups - 1,)),
            pltpu.SemaphoreType.DMA((5, dp)),
            pltpu.SemaphoreType.DMA((5, dp)),
            pltpu.SemaphoreType.DMA((2, rows)),
            pltpu.SemaphoreType.DMA((2, 2)),
            pltpu.SemaphoreType.DMA,
        ],
        compiler_params=pltpu.CompilerParams(
            collective_id=0, has_side_effects=True, vmem_limit_bytes=63 << 20
        ),
        name="layer",
    )(labels, inputs, grad_out, *shards, b_qv, b_up, *(v.reshape(1, local) for v in vectors))


def finish_kernel(many, seq, result, grad_in, qkv, out, up, down, sums, place, *outs):
    i = pl.program_id(0)
    for n in range(many):
        toks = slice(n * seq, (n + 1) * seq)
        turn = place[i * many + n, 1]
        outs[0][:, toks] = pltpu.roll(result[n].astype(f32), turn, 1).astype(bf16)
        outs[1][:, toks] = pltpu.roll(grad_in[n], turn, 1)

    @pl.when(i == 0)
    def _():
        local = result.shape[1]
        for target, source in zip(outs[2:6], (qkv, out, up, down)):
            target[...] = source[...]
        for n in range(6):
            outs[6 + n][...] = sums[n : n + 1, :local]
        outs[12][...] = sums[6:7, :]
        outs[13][...] = sums[7:8, : 2 * local]


def finish(result, grad_in, *small):
    rows, local, seq = result.shape
    units = small[4].shape[1]
    many = math.gcd(rows, FINISH_ROWS)
    raw = pl.BlockSpec((many, local, seq), lambda i: (i, 0, 0))
    block = pl.BlockSpec((local, many * seq), lambda i: (0, i))
    vmem = pl.BlockSpec(memory_space=pltpu.VMEM)
    shapes = (*(s.shape for s in small[:4]), *((1, local),) * 6, (1, units), (1, 2 * local))
    return pl.pallas_call(
        functools.partial(finish_kernel, many, seq),
        grid=(rows // many,),
        out_shape=(
            jax.ShapeDtypeStruct((local, rows * seq), bf16),
            jax.ShapeDtypeStruct((local, rows * seq), f32),
            *(jax.ShapeDtypeStruct(s, f32) for s in shapes),
        ),
        in_specs=[raw, raw, *[vmem] * 5, pl.BlockSpec(memory_space=pltpu.SMEM)],
        out_specs=(block, block, *(vmem,) * len(shapes)),
        compiler_params=pltpu.CompilerParams(vmem_limit_bytes=60 << 20),
        name="finish",
    )(result, grad_in, *small)


def per_device(
    inputs,
    labels,
    w_qkv,
    b_qv,
    w_out,
    b_out,
    gain_one,
    shift_one,
    w_up,
    b_up,
    down_weight,
    down_bias,
    gain_two,
    shift_two,
    grad_out,
):
    shards = (w_qkv[0], w_out, w_up[0], down_weight[0])
    vectors = (b_out, gain_one, shift_one, down_bias, gain_two, shift_two)
    raw = run_layer(labels, inputs, grad_out, shards, b_qv, b_up, *vectors)
    result, input_grad, qkv, out, up, down, *sums = finish(*raw)
    flat = [s.reshape(-1) for s in sums]
    return (
        result,
        input_grad,
        qkv[None],
        sums[7],
        out,
        flat[0],
        flat[1],
        flat[2],
        up[None],
        sums[6],
        down[None],
        sums[3],
        flat[4],
        flat[5],
    )


def solution(mesh):
    placed = (
        P("group", "dp"),
        P("dp", None),
        P("group", "dp", None),
        P("group", None),
        P("dp", "group"),
        P("group"),
        P("group"),
        P("group"),
        P("group", "dp", None),
        P("group", None),
        P("group", "dp", None),
        P("group", None),
        P("group"),
        P("group"),
        P("group", "dp"),
    )
    return jax.shard_map(
        per_device,
        mesh=mesh,
        in_specs=placed,
        out_specs=(
            P("group", "dp"),
            P("group", "dp"),
            P("group", "dp", None),
            P("group", None),
            P("dp", "group"),
            P("group"),
            P("group"),
            P("group"),
            P("group", "dp", None),
            P("group", None),
            P("group", "dp", None),
            P("group", None),
            P("group"),
            P("group"),
        ),
        check_vma=False,
    )
```

```python
import functools
import math

import jax
import jax.numpy as jnp
from jax import lax
from jax.experimental import pallas as pl
from jax.experimental.pallas import tpu as pltpu
from jax.sharding import PartitionSpec as P

HD = 64
HG = 3
LANES = 128
SPLIT = 2
FINISH_ROWS = 8
PASS_CTX, RESIDUAL, FEED, FEED_BACK, NORM_BACK, PASS_ATT, DELAY = 1, 2, 4, 6, 8, 9, 10
CTX_SLOTS, ATT_SLOTS, SEMS = DELAY + 1, 5, 5
SLACK = 2
FETCHED = 6
FLATS = 4
GRAD_LAG = NORM_BACK - FEED_BACK

eps = 1e-12
f32 = jnp.float32
bf16 = jnp.bfloat16
MESH = pl.DeviceIdType.MESH


def mm(left, right):
    return jnp.dot(left, right, preferred_element_type=f32)


def mm_nt(left, right):
    return lax.dot_general(left, right, (((1,), (1,)), ((), ())), preferred_element_type=f32)


def mm_tn(left, right):
    return lax.dot_general(left, right, (((0,), (0,)), ((), ())), preferred_element_type=f32)


def packed_rows(count, width):
    tail = 0 if width % LANES == 0 else count // (2 - count % 2)
    return -(-(width // LANES * count + tail) // 16) * 16


def pack(into, x):
    count, width = x.shape
    whole = width // LANES
    for k in range(whole):
        into[k * count : (k + 1) * count, :] = x[:, k * LANES : (k + 1) * LANES]
    if width % LANES:
        left = width - whole * LANES
        folds = 2 - count % 2
        part = count // folds
        for n in range(folds):
            into[whole * count : whole * count + part, n * left : (n + 1) * left] = x[
                n * part : (n + 1) * part, whole * LANES :
            ]


def unpack(into, start, count, width, x):
    whole = width // LANES
    for k in range(whole):
        into[start : start + count, k * LANES : (k + 1) * LANES] = x[k * count : (k + 1) * count, :]
    if width % LANES:
        left = width - whole * LANES
        folds = 2 - count % 2
        part = count // folds
        for n in range(folds):
            into[start + n * part : start + (n + 1) * part, whole * LANES : width] = x[
                whole * count : whole * count + part, n * left : (n + 1) * left
            ]


def row_sum(x):
    return jnp.sum(x, axis=0, keepdims=True)


def remote(src, dst, send, recv, device):
    return pltpu.make_async_remote_copy(
        src_ref=src, dst_ref=dst, send_sem=send, recv_sem=recv, device_id=device, device_id_type=MESH
    )


def layer_kernel(
    rows,
    groups,
    dp,
    labels,
    inp,
    gout_in,
    w_qkv,
    w_out,
    w_up,
    w_down,
    in_qv,
    in_up,
    in_out,
    in_gain_one,
    in_shift_one,
    in_down,
    in_gain_two,
    in_shift_two,
    result,
    grad_in,
    o_qkv,
    o_out,
    o_up,
    o_down,
    o_sums,
    o_place,
    place,
    b_qkv,
    b_up,
    cols,
    inp_rows,
    gout_rows,
    res_ring,
    gin_ring,
    wqkv_t,
    wqkv,
    wout_t,
    wout_rows,
    wup_t,
    wup,
    wdown_t,
    wdown,
    all_qkv,
    all_out,
    all_up,
    all_down,
    out_rows,
    wide_mat,
    g_qkv,
    g_out,
    g_up,
    g_down,
    sums,
    flats,
    land_qkv,
    land_out,
    land_up,
    land_down,
    all_sums,
    ctx_all,
    att_all,
    stats,
    x_ring,
    mix_ring,
    prob_ring,
    x_one,
    n_one,
    inv_one,
    hid,
    hid_low,
    pre,
    act,
    slope,
    x_two,
    upstream,
    br_low,
    pre_low,
    hid_grad,
    rog_ring,
    mix_grad,
    send_blocks,
    recv_blocks,
    send_stats,
    recv_stats,
    send_weights,
    recv_weights,
    send_rows,
    recv_rows,
    send_grads,
    recv_grads,
    fetch,
    store,
    place_sem,
):
    steps = rows + DELAY
    tall_mat = pre.at[:, : 2 * LANES]
    local = w_out.shape[1]
    seq = inp.shape[1] // rows

    def inp_copy(r):
        toks = pl.ds(pl.multiple_of(r * seq, seq), seq)
        slot = lax.rem(r, FETCHED)
        return pltpu.make_async_copy(inp.at[:, toks], inp_rows.at[slot], fetch.at[0, slot])

    def gout_copy(r):
        toks = pl.ds(pl.multiple_of(r * seq, seq), seq)
        slot = lax.rem(r, FETCHED)
        return pltpu.make_async_copy(gout_in.at[:, toks], gout_rows.at[slot], fetch.at[1, slot])

    def result_copy(r):
        slot = lax.rem(r, 2)
        return pltpu.make_async_copy(res_ring.at[slot], result.at[r], store.at[0, slot])

    def grad_in_copy(r):
        slot = lax.rem(r, 2)
        return pltpu.make_async_copy(gin_ring.at[slot], grad_in.at[r], store.at[1, slot])

    def find_places():
        ids = labels[...]
        counts = [
            jnp.sum(jnp.where(ids == v, 1.0, 0.0), axis=1, keepdims=True) for v in range(4)
        ]
        start = jnp.zeros_like(counts[0])
        first = jnp.zeros_like(start)
        second = jnp.zeros_like(start)
        found = jnp.zeros_like(start)
        begin = jnp.zeros_like(start)
        for v in range(4):
            hit = jnp.where(counts[v] == seq // SPLIT, 1.0 - found, 0.0)
            start = start + hit * begin
            first = first + hit * counts[(v + 1) % 4]
            second = second + hit * (counts[(v + 1) % 4] + counts[(v + 2) % 4])
            found = found + hit
            begin = begin + counts[v]
        turn = jnp.where(start == 0.0, 0.0, seq - start)
        lane = lax.broadcasted_iota(jnp.int32, (rows, LANES), 1)
        table = jnp.zeros((rows, LANES), f32)
        for n, value in enumerate((turn, start, first, second)):
            table = jnp.where(lane == n, value, table)
        o_place[...] = table.astype(jnp.int32)
        copy = pltpu.make_async_copy(o_place, place, place_sem)
        copy.start()
        copy.wait()

    def spread_vectors():
        def column(row):
            return jnp.broadcast_to(row, (LANES, row.shape[1])).T

        qv = column(in_qv[...])
        b_qkv[:local, :] = qv[:local]
        b_qkv[local : 2 * local, :] = jnp.zeros((local, LANES), f32)
        b_qkv[2 * local :, :] = qv[local:]
        b_up[...] = column(in_up[...])
        vectors = (in_out, in_gain_one, in_shift_one, in_down, in_gain_two, in_shift_two)
        for n, ref in enumerate(vectors):
            cols[n * local : (n + 1) * local, :] = column(ref[...])

    def step(i, carry):
        g = lax.axis_index("group")
        d = lax.axis_index("dp")
        across = lax.rem(g + 2, groups)
        beside = g + 1 - 2 * lax.rem(g, 2)
        corner = lax.rem(beside + 2, groups)
        half = seq // SPLIT
        channels = local * groups
        parts = seq // LANES
        hidden_units = wup_t.shape[0]
        ring = x_ring.shape[0]
        lanes = [slice(k * LANES, (k + 1) * LANES) for k in range(parts)]
        col = lambda n: cols[n * local : (n + 1) * local, :]
        B_OUT, GAIN1, SHIFT1, B_DOWN, GAIN2, SHIFT2 = range(6)
        S_BOUT, S_GAIN1, S_SHIFT1, S_BDOWN, S_GAIN2, S_SHIFT2 = range(6)

        def accumulate(slot, chunk):
            sums[slot * local : (slot + 1) * local, :] += chunk

        def block_copy(buf, base, kind, r, slot):
            peer = across if kind == 0 else beside
            at_row = lax.rem(r, buf.shape[0])
            return remote(
                buf.at[at_row, slot],
                buf.at[at_row, slot],
                send_blocks.at[base + kind, lax.rem(r, SEMS)],
                recv_blocks.at[base + kind, lax.rem(r, SEMS)],
                {"group": peer},
            )

        def send_own(buf, base, r):
            block_copy(buf, base, 0, r, g).start()
            block_copy(buf, base, 1, r, g).start()

        def pass_on(buf, base, r):
            block_copy(buf, base, 0, r, across).wait_recv()
            block_copy(buf, base, 2, r, across).start()

        def blocks_ready(buf, base, r):
            block_copy(buf, base, 1, r, beside).wait_recv()
            block_copy(buf, base, 2, r, corner).wait_recv()

        def blocks_sent(buf, base, r):
            block_copy(buf, base, 0, r, g).wait_send()
            block_copy(buf, base, 1, r, g).wait_send()
            block_copy(buf, base, 2, r, across).wait_send()

        def stat_copy(at_step, offset, slot):
            return remote(
                stats.at[lax.rem(at_step, 8), slot],
                stats.at[lax.rem(at_step, 8), slot],
                send_stats.at[offset - 1, lax.rem(at_step, SEMS)],
                recv_stats.at[offset - 1, lax.rem(at_step, SEMS)],
                {"group": lax.rem(g + offset, groups)},
            )

        def stats_send():
            for offset in range(1, groups):
                stat_copy(i, offset, g).start()

        def stats_ready():
            for offset in range(1, groups):
                stat_copy(i - SLACK, offset, lax.rem(g + groups - offset, groups)).wait_recv()
                stat_copy(i - SLACK, offset, g).wait_send()

        def put_stat(first, k, value):
            stats[lax.rem(i, 8), g, first + k : first + k + 1, :] = value

        def get_stat(first, k, p, ago):
            return stats[lax.rem(i - ago, 8), p, first + k : first + k + 1, :]

        ONE, TWO, BACK = 0, 2 * parts, 6 * parts
        CTX, ATT = 0, 3

        shards = (w_qkv, w_out, w_up, w_down)
        fulls = (all_qkv, all_out, all_up, all_down)
        QKV, OUT, UP, DOWN = range(4)

        def weight_copy(which, k, slot):
            full = fulls[which]
            return remote(
                full.at[slot],
                full.at[slot],
                send_weights.at[which, k],
                recv_weights.at[which, k],
                {"dp": lax.rem(d + k, dp)},
            )

        def each_peer(action):
            def body(k, carry):
                action(k)
                return carry

            lax.fori_loop(1, dp, body, 0)

        def weights_ready(which, into):
            each_peer(lambda k: weight_copy(which, k, lax.rem(d - k + dp, dp)).wait_recv())
            count, width = shards[which].shape
            for slot in range(dp):
                unpack(into, slot * count, count, width, fulls[which][slot].astype(f32))

        per = dp // groups

        def rows_copy(offset, source, target):
            return remote(
                all_out.at[pl.ds(target * per, per)],
                out_rows.at[source],
                send_rows.at[offset - 1],
                recv_rows.at[offset - 1],
                {"group": target},
            )

        @pl.when(i == 0)
        def _():
            barrier = pltpu.get_barrier_semaphore()
            for offset in range(1, groups):
                pl.semaphore_signal(
                    barrier, inc=1, device_id={"group": lax.rem(g + offset, groups)}, device_id_type=MESH
                )
            each_peer(
                lambda k: pl.semaphore_signal(
                    barrier, inc=1, device_id={"dp": lax.rem(d + k, dp)}, device_id_type=MESH
                )
            )
            flats[...] = jnp.zeros_like(flats)

            def pack_shard(which):
                buffer = flats.at[which]
                pack(buffer, shards[which][...])
                fulls[which][d] = buffer[: fulls[which].shape[1], :].astype(bf16)

            pack_shard(QKV)
            pl.semaphore_wait(barrier, groups - 1 + dp - 1)
            each_peer(lambda k: weight_copy(QKV, k, d).start())
            for which in (OUT, UP, DOWN):
                pack_shard(which)

            def fetch_row(r, carry):
                inp_copy(r).start()
                gout_copy(r).start()
                return carry

            lax.fori_loop(0, min(FETCHED, rows), fetch_row, 0)
            find_places()
            spread_vectors()
            for ref in (g_qkv, g_out, g_up, g_down, sums):
                ref[...] = jnp.zeros_like(ref)
            weights_ready(QKV, wide_mat)
            each_peer(lambda k: weight_copy(OUT, k, d).start())
            mat = wide_mat[:, : 3 * local]
            wqkv[...] = mat.astype(bf16)
            wqkv_t[...] = mat.T.astype(bf16)

        @pl.when(i == 1)
        def _():
            for which in (UP, DOWN):
                each_peer(lambda k, which=which: weight_copy(which, k, d).start())

        @pl.when(i == RESIDUAL)
        def _():
            weights_ready(OUT, tall_mat)
            for offset in range(1, groups):
                rows_copy(offset, g, lax.rem(g + offset, groups)).start()
            out_rows[g] = all_out[pl.ds(g * per, per)]
            wout_t[...] = tall_mat[:, :local].T.astype(bf16)

        @pl.when(i == FEED)
        def _():
            weights_ready(UP, wide_mat)
            mat = wide_mat[...]
            wup[...] = mat.astype(bf16)
            wup_t[...] = mat.T.astype(bf16)
            weights_ready(DOWN, tall_mat)
            mat = tall_mat[:, :local]
            wdown[...] = mat.astype(bf16)
            wdown_t[...] = mat.T.astype(bf16)

        @pl.when(i == DELAY)
        def _():
            for offset in range(1, groups):
                rows_copy(offset, lax.rem(g + groups - offset, groups), g).wait_recv()
            count = local // per
            for p in range(groups):
                for n in range(per):
                    unpack(wide_mat, n * count, count, local, out_rows[p, n].astype(f32))
                tall_mat[p * local : (p + 1) * local, :local] = wide_mat[:, :local].T
            wout_rows[...] = tall_mat[:, :local].T.astype(bf16)

        stages = fulls
        lands = (land_qkv, land_out, land_up, land_down)

        def grad_copy(which, k, slot):
            return remote(
                stages[which].at[lax.rem(d + k, dp)],
                lands[which].at[slot],
                send_grads.at[which, k],
                recv_grads.at[which, k],
                {"dp": lax.rem(d + k, dp)},
            )

        def sums_copy(k, slot):
            return remote(
                all_sums.at[slot],
                all_sums.at[slot],
                send_grads.at[4, k],
                recv_grads.at[4, k],
                {"dp": lax.rem(d + k, dp)},
            )

        def send_grad(which, mat):
            stage = stages[which]
            count = shards[which].shape[0]
            for slot in range(dp):
                buffer = flats.at[slot % FLATS]
                pack(buffer, mat[slot * count : (slot + 1) * count])
                stage[slot] = buffer[: stage.shape[1], :].astype(bf16)
            each_peer(lambda k: grad_copy(which, k, d).start())

        def grad_sum(which, out):
            count = stages[which].shape[1]
            flat = flats.at[which]
            flat[:count, :] = stages[which][d].astype(f32)

            def add(k):
                slot = lax.rem(d - k + dp, dp)
                grad_copy(which, k, slot).wait()
                flat[:count, :] += lands[which][slot].astype(f32)

            each_peer(add)
            unpack(out, 0, *out.shape, flat[...])

        def stage_residual(r):
            blocks_ready(ctx_all, CTX, r)
            attended = mm(wout_t[...], ctx_all[lax.rem(r, CTX_SLOTS)].reshape(channels, seq))
            xr = x_ring.at[lax.rem(r, ring)]
            for k, s in enumerate(lanes):
                x = xr[:, s].astype(f32) + attended[:, s] + col(B_OUT)
                x_one[lax.rem(r, FEED - RESIDUAL), :, s] = x
                mean = row_sum(x) * (1.0 / local)
                off = x - mean
                put_stat(ONE, k, mean)
                put_stat(ONE + parts, k, row_sum(off * off))
            blocks_sent(ctx_all, CTX, r)

        def stage_attend(r):
            slot = lax.rem(r, ring)
            inp_copy(r).wait()
            rolled = pltpu.roll(
                inp_rows[lax.rem(r, FETCHED)].astype(f32), place[r, 0], 1
            ).astype(bf16)
            x_ring[slot] = rolled

            @pl.when(r + FETCHED < rows)
            def _():
                inp_copy(r + FETCHED).start()

            mixed = mm(wqkv_t[...], rolled)
            for s in lanes:
                mix_ring[slot, :, s] = (mixed[:, s] + b_qkv[...]).astype(bf16)
            first, second = place[r, 2], place[r, 3]
            down = lax.broadcasted_iota(jnp.int32, (half, half), 0)
            along = lax.broadcasted_iota(jnp.int32, (half, half), 1)
            own = lambda at: (at >= first).astype(jnp.int32) + (at >= second).astype(jnp.int32)
            pre[:half, :half] = jnp.where(own(down) == own(along), 0.0, -1000000000.0)
            scale = math.log2(math.e) / math.sqrt(HD)
            blocks = [(h, b) for h in range(HG) for b in range(SPLIT)]

            def piece(part, n):
                h, b = blocks[n]
                start = part * local + h * HD
                return mix_ring[slot, start : start + HD, b * half : (b + 1) * half]

            def score(n):
                return mm_tn(piece(1, n), piece(0, n))

            def soften(n, scores):
                if blocks[n][1]:
                    scores = scores + pre[:half, :half]
                highest = jnp.max(scores, axis=0, keepdims=True)
                return jnp.exp2((scores - highest) * scale)

            def norm(n, exponent):
                chances = (exponent * (1.0 / row_sum(exponent))).astype(bf16)
                prob_ring[slot, n] = chances
                return chances

            def blend(n, chances):
                h, b = blocks[n]
                ctx_all[lax.rem(r, CTX_SLOTS), g, h * HD : (h + 1) * HD, b * half : (b + 1) * half] = mm(
                    piece(2, n), chances
                ).astype(bf16)

            held = {}
            for step in range(len(blocks) + 3):
                n = step - 0
                if 0 <= n < len(blocks):
                    held[0, n] = score(n)
                n = step - 1
                if 0 <= n < len(blocks):
                    held[1, n] = soften(n, held.pop((0, n)))
                n = step - 2
                if 0 <= n < len(blocks):
                    held[2, n] = norm(n, held.pop((1, n)))
                n = step - 3
                if 0 <= n < len(blocks):
                    blend(n, held.pop((2, n)))
            send_own(ctx_all, CTX, r)

        def stage_norm_back(r):
            slot = lax.rem(r, rog_ring.shape[0])
            kept = lax.rem(r, (NORM_BACK - FEED + 1))
            for k, s in enumerate(lanes):
                first = get_stat(BACK, k, 0, GRAD_LAG)
                second = get_stat(BACK + parts, k, 0, GRAD_LAG)
                for p in range(1, groups):
                    first += get_stat(BACK, k, p, GRAD_LAG)
                    second += get_stat(BACK + parts, k, p, GRAD_LAG)
                first = first * (1.0 / channels)
                second = second * (1.0 / channels)
                scaled = hid_grad[lax.rem(r, (GRAD_LAG + 1)), :, s] * col(GAIN1)
                back = inv_one[kept, k : k + 1, :] * (scaled - first - n_one[kept, :, s] * second)
                rog_ring[slot, :, s] = back
                low = back.astype(bf16)
                att_all[lax.rem(r, ATT_SLOTS), g, :, s] = low
                accumulate(S_BOUT, low.astype(f32))
            send_own(att_all, ATT, r)
            contexts = ctx_all[lax.rem(r, CTX_SLOTS)].reshape(channels, seq)
            g_out[...] += mm_nt(contexts, att_all[lax.rem(r, ATT_SLOTS), g])

        def stage_feed(r):
            act_r = act.at[lax.rem(r, FEED_BACK - FEED)]
            slope_r = slope.at[lax.rem(r, FEED_BACK - FEED)]
            hid_low_r = hid_low.at[lax.rem(r, FEED_BACK - FEED)]
            x_two_r = x_two.at[lax.rem(r, FEED_BACK - FEED)]
            upstream_r = upstream.at[lax.rem(r, FEED_BACK - FEED)]
            x_one_r = x_one.at[lax.rem(r, FEED - RESIDUAL)]
            kept = lax.rem(r, (NORM_BACK - FEED + 1))
            for k, s in enumerate(lanes):
                means = [get_stat(ONE, k, p, FEED - RESIDUAL) for p in range(groups)]
                center = sum(means[1:], means[0]) * (1.0 / groups)
                spread = get_stat(ONE + parts, k, 0, FEED - RESIDUAL)
                for p in range(1, groups):
                    spread += get_stat(ONE + parts, k, p, FEED - RESIDUAL)
                for mean in means:
                    spread += local * (mean - center) * (mean - center)
                inverse = lax.rsqrt(spread * (1.0 / channels) + eps)
                inv_one[kept, k : k + 1, :] = inverse
                normed = (x_one_r[:, s] - center) * inverse
                n_one[kept, :, s] = normed
                h = normed * col(GAIN1) + col(SHIFT1)
                hid[:, s] = h
                hid_low_r[:, s] = h.astype(bf16)
            pre[...] = mm(wup_t[...], hid_low_r[...])
            for j in range(hidden_units // local):
                units = slice(j * local, (j + 1) * local)
                for s in lanes:
                    u = pre[units, s] + b_up[units, :]
                    cdf = 0.5 + 0.5 * lax.erf(u * math.sqrt(0.5))
                    act_r[units, s] = (u * cdf).astype(bf16)
                    bell = jnp.exp2(u * u * (-0.5 * math.log2(math.e))) * (1.0 / math.sqrt(2.0 * math.pi))
                    slope_r[units, s] = cdf + u * bell
            branch = mm(wdown_t[...], act_r[...])
            gout_copy(r).wait()
            upstream_r[...] = pltpu.roll(
                gout_rows[lax.rem(r, FETCHED)].astype(f32), place[r, 0], 1
            )

            @pl.when(r + FETCHED < rows)
            def _():
                gout_copy(r + FETCHED).start()

            for k, s in enumerate(lanes):
                x = hid[:, s] + branch[:, s] + col(B_DOWN)
                x_two_r[:, s] = x
                mean = row_sum(x) * (1.0 / local)
                off = x - mean
                scaled = upstream_r[:, s] * col(GAIN2)
                tile = (mean, row_sum(off * off), row_sum(scaled), row_sum(scaled * off))
                for n, value in enumerate(tile):
                    put_stat(TWO + n * parts, k, value)

        def stage_attend_back(r):
            slot = lax.rem(r, ring)
            blocks_ready(att_all, ATT, r)
            br_low[...] = mm(
                wout_rows[...], att_all[lax.rem(r, ATT_SLOTS)].reshape(channels, seq)
            ).astype(bf16)
            factor = 1.0 / math.sqrt(HD)
            blocks = [(h, b) for h in range(HG) for b in range(SPLIT)]

            def at_block(part, n):
                h, b = blocks[n]
                start = part * local + h * HD
                return slice(start, start + HD), slice(b * half, (b + 1) * half)

            def piece(part, n):
                return mix_ring[slot, *at_block(part, n)]

            def spread(n):
                incoming = br_low[at_block(0, n)]
                mix_grad[at_block(2, n)] = mm_nt(incoming, prob_ring[slot, n]).astype(bf16)

            def open_up(n):
                return mm_tn(piece(2, n), br_low[at_block(0, n)])

            def center(n, prob_grad):
                at_n = at_block(0, n)
                inner = row_sum(br_low[at_n].astype(f32) * ctx_all[lax.rem(r, CTX_SLOTS), g, *at_n].astype(f32))
                return (prob_ring[slot, n].astype(f32) * (prob_grad - inner)).astype(bf16)

            def queries(n, score_grad):
                mix_grad[at_block(0, n)] = (mm(piece(1, n), score_grad) * factor).astype(bf16)

            def keys(n, score_grad):
                mix_grad[at_block(1, n)] = (mm_nt(piece(0, n), score_grad) * factor).astype(bf16)

            held = {}
            for step in range(len(blocks) + 2):
                n = step - 0
                if 0 <= n < len(blocks):
                    held[0, n] = open_up(n)
                n = step - 0
                if 0 <= n < len(blocks):
                    spread(n)
                n = step - 1
                if 0 <= n < len(blocks):
                    held[1, n] = center(n, held.pop((0, n)))
                n = step - 2
                if 0 <= n < len(blocks):
                    queries(n, held[1, n])
                n = step - 2
                if 0 <= n < len(blocks):
                    keys(n, held.pop((1, n)))
            g_qkv[...] += mm_nt(mix_grad[...], x_ring[slot])
            blocks_sent(att_all, ATT, r)

            @pl.when(r >= 2)
            def _():
                grad_in_copy(r - 2).wait()

            total = mm(wqkv[...], mix_grad[...]) + rog_ring[lax.rem(r, rog_ring.shape[0])]
            gin_ring[lax.rem(r, 2)] = total
            grad_in_copy(r).start()
            base = 6 * local + hidden_units
            for n, start in ((0, 0), (1, 2 * local)):
                chunk = mix_grad[start : start + local, lanes[0]].astype(f32)
                for s in lanes[1:]:
                    chunk += mix_grad[start : start + local, s].astype(f32)
                sums[base + n * local : base + (n + 1) * local, :] += chunk

        def stage_feed_back(r):
            act_r = act.at[lax.rem(r, FEED_BACK - FEED)]
            slope_r = slope.at[lax.rem(r, FEED_BACK - FEED)]
            hid_low_r = hid_low.at[lax.rem(r, FEED_BACK - FEED)]
            x_two_r = x_two.at[lax.rem(r, FEED_BACK - FEED)]
            upstream_r = upstream.at[lax.rem(r, FEED_BACK - FEED)]
            @pl.when(r >= 2)
            def _():
                result_copy(r - 2).wait()

            for k, s in enumerate(lanes):
                row = lambda p, n: get_stat(TWO + n * parts, k, p, FEED_BACK - FEED)
                means = [row(p, 0) for p in range(groups)]
                center = sum(means[1:], means[0]) * (1.0 / groups)
                spread, first, second = row(0, 1), row(0, 2), row(0, 3)
                for p in range(1, groups):
                    spread += row(p, 1)
                    first += row(p, 2)
                    second += row(p, 3)
                for p, mean in enumerate(means):
                    spread += local * (mean - center) * (mean - center)
                    second += (mean - center) * row(p, 2)
                inverse = lax.rsqrt(spread * (1.0 / channels) + eps)
                first = first * (1.0 / channels)
                second = second * inverse * (1.0 / channels)
                normed = (x_two_r[:, s] - center) * inverse
                res_ring[lax.rem(r, 2), :, s] = (normed * col(GAIN2) + col(SHIFT2)).astype(bf16)
                up = upstream_r[:, s]
                back = inverse * (up * col(GAIN2) - first - normed * second)
                hid[:, s] = back
                low = back.astype(bf16)
                br_low[:, s] = low
                accumulate(S_GAIN2, up * normed)
                accumulate(S_SHIFT2, up)
                accumulate(S_BDOWN, low.astype(f32))
            result_copy(r).start()
            pre[...] = mm(wdown[...], br_low[...])
            g_down[...] += mm_nt(act_r[...], br_low[...])
            base = 6 * local
            for j in range(hidden_units // local):
                units = slice(j * local, (j + 1) * local)
                for s in lanes:
                    low = (slope_r[units, s] * pre[units, s]).astype(bf16)
                    pre_low[units, s] = low
                    sums[base + j * local : base + (j + 1) * local, :] += low.astype(f32)
            g_up[...] += mm_nt(pre_low[...], hid_low_r[...])
            change = mm(wup[...], pre_low[...])
            for k, s in enumerate(lanes):
                total = hid[:, s] + change[:, s]
                hid_grad[lax.rem(r, (GRAD_LAG + 1)), :, s] = total
                normed = n_one[lax.rem(r, (NORM_BACK - FEED + 1)), :, s]
                scaled = total * col(GAIN1)
                put_stat(BACK, k, row_sum(scaled))
                put_stat(BACK + parts, k, row_sum(scaled * normed))
                accumulate(S_GAIN1, total * normed)
                accumulate(S_SHIFT1, total)

        def at(delay, stage):
            r = i - delay

            @pl.when(jnp.logical_and(r >= 0, r < rows))
            def _():
                stage(r)

        @pl.when(jnp.logical_and(i >= RESIDUAL + SLACK, i < rows + NORM_BACK - 1 + SLACK))
        def _():
            stats_ready()

        at(0, stage_attend)
        at(NORM_BACK, stage_norm_back)
        at(FEED_BACK, stage_feed_back)
        at(FEED, stage_feed)
        at(RESIDUAL, stage_residual)

        @pl.when(jnp.logical_and(i >= RESIDUAL, i < rows + NORM_BACK - 1))
        def _():
            stats_send()


        @pl.when(i == rows - 1 + FEED_BACK)
        def _():
            for which in range(4):
                each_peer(lambda k, which=which: weight_copy(which, k, d).wait_send())
            for offset in range(1, groups):
                rows_copy(offset, g, lax.rem(g + offset, groups)).wait_send()
            send_grad(UP, g_up[...].T)
            send_grad(DOWN, g_down[...])

        @pl.when(i == rows - 1 + NORM_BACK)
        def _():
            send_grad(OUT, g_out[...])
            mine = all_sums.at[d]
            for n in range(6):
                mine[n : n + 1, :local] = row_sum(sums[n * local : (n + 1) * local, :].T)
            base = 6 * local
            mine[6:7, :] = row_sum(sums[base : base + hidden_units, :].T)

        at(PASS_CTX, lambda r: pass_on(ctx_all, CTX, r))
        at(DELAY, stage_attend_back)
        at(PASS_ATT, lambda r: pass_on(att_all, ATT, r))

        @pl.when(i == steps - 1)
        def _():
            send_grad(QKV, g_qkv[...].T)
            mine = all_sums.at[d]
            base = 6 * local + hidden_units
            mine[7:8, : 2 * local] = row_sum(sums[base : base + 2 * local, :].T)
            each_peer(lambda k: sums_copy(k, d).start())
            for which, out in ((UP, o_up), (DOWN, o_down), (OUT, o_out), (QKV, o_qkv)):
                grad_sum(which, out)
            each_peer(lambda k: sums_copy(k, lax.rem(d - k + dp, dp)).wait())
            o_sums[...] = jnp.sum(all_sums[...], axis=0)
        return carry

    lax.fori_loop(0, steps, step, 0)
    for r in (rows - 2, rows - 1):
        result_copy(r).wait()
        grad_in_copy(r).wait()


def run_layer(labels, inputs, grad_out, shards, b_qv, b_up, *vectors):
    groups = lax.axis_size("group")
    dp = lax.axis_size("dp")
    local, tok_count = inputs.shape
    rows, seq = labels.shape
    channels = groups * local
    half = seq // SPLIT
    parts = seq // LANES
    units = b_up.shape[1]
    ring = DELAY + 1
    vmem = pl.BlockSpec(memory_space=pltpu.VMEM)
    anywhere = pl.BlockSpec(memory_space=pl.ANY)
    acc_shapes = ((3 * local, local), (groups * local, local), (units, local), (units, local))
    sums_shape = (6 * local + units + 2 * local, LANES)
    shard_shapes = tuple(w.shape for w in shards)
    slots = tuple((dp, packed_rows(*s), LANES) for s in shard_shapes)
    row_sums = (8, units)
    block = (groups, local, seq)
    return pl.pallas_call(
        functools.partial(layer_kernel, rows, groups, dp),
        out_shape=(
            jax.ShapeDtypeStruct((rows, local, seq), bf16),
            jax.ShapeDtypeStruct((rows, local, seq), f32),
            *(jax.ShapeDtypeStruct(s, f32) for s in shard_shapes),
            jax.ShapeDtypeStruct(row_sums, f32),
            jax.ShapeDtypeStruct((rows, LANES), jnp.int32),
        ),
        in_specs=[vmem, anywhere, anywhere, *([vmem] * (len(shards) + 2 + len(vectors)))],
        out_specs=(anywhere, anywhere, *([vmem] * (len(shards) + 2))),
        scratch_shapes=[
            pltpu.SMEM((rows, LANES), jnp.int32),
            pltpu.VMEM((3 * local, LANES), f32),
            pltpu.VMEM((units, LANES), f32),
            pltpu.VMEM((6 * local, LANES), f32),
            pltpu.VMEM((FETCHED, local, seq), bf16),
            pltpu.VMEM((FETCHED, local, seq), bf16),
            pltpu.VMEM((2, local, seq), bf16),
            pltpu.VMEM((2, local, seq), f32),
            pltpu.VMEM((3 * local, local), bf16),
            pltpu.VMEM((local, 3 * local), bf16),
            pltpu.VMEM((local, channels), bf16),
            pltpu.VMEM((local, channels), bf16),
            pltpu.VMEM((units, local), bf16),
            pltpu.VMEM((local, units), bf16),
            pltpu.VMEM((local, units), bf16),
            pltpu.VMEM((units, local), bf16),
            *(pltpu.VMEM(s, bf16) for s in slots),
            pltpu.VMEM((groups, dp // groups, *slots[1][1:]), bf16),
            pltpu.VMEM((local, units), f32),
            *(pltpu.VMEM(s, f32) for s in acc_shapes),
            pltpu.VMEM(sums_shape, f32),
            pltpu.VMEM((FLATS, max(s[1] for s in slots), LANES), f32),
            *(pltpu.VMEM(s, bf16) for s in slots),
            pltpu.VMEM((dp, *row_sums), f32),
            pltpu.VMEM((CTX_SLOTS, *block), bf16),
            pltpu.VMEM((ATT_SLOTS, *block), bf16),
            pltpu.VMEM((8, groups, 8 * parts, LANES), f32),
            pltpu.VMEM((ring, local, seq), bf16),
            pltpu.VMEM((ring, 3 * local, seq), bf16),
            pltpu.VMEM((ring, HG * SPLIT, half, half), bf16),
            pltpu.VMEM((FEED - RESIDUAL, local, seq), f32),
            pltpu.VMEM(((NORM_BACK - FEED + 1), local, seq), f32),
            pltpu.VMEM(((NORM_BACK - FEED + 1), parts, LANES), f32),
            pltpu.VMEM((local, seq), f32),
            pltpu.VMEM((FEED_BACK - FEED, local, seq), bf16),
            pltpu.VMEM((units, seq), f32),
            pltpu.VMEM((FEED_BACK - FEED, units, seq), bf16),
            pltpu.VMEM((FEED_BACK - FEED, units, seq), f32),
            pltpu.VMEM((FEED_BACK - FEED, local, seq), f32),
            pltpu.VMEM((FEED_BACK - FEED, local, seq), f32),
            pltpu.VMEM((local, seq), bf16),
            pltpu.VMEM((units, seq), bf16),
            pltpu.VMEM(((GRAD_LAG + 1), local, seq), f32),
            pltpu.VMEM((3, local, seq), f32),
            pltpu.VMEM((3 * local, seq), bf16),
            pltpu.SemaphoreType.DMA((6, SEMS)),
            pltpu.SemaphoreType.DMA((6, SEMS)),
            pltpu.SemaphoreType.DMA((groups - 1, SEMS)),
            pltpu.SemaphoreType.DMA((groups - 1, SEMS)),
            pltpu.SemaphoreType.DMA((4, dp)),
            pltpu.SemaphoreType.DMA((4, dp)),
            pltpu.SemaphoreType.DMA((groups - 1,)),
            pltpu.SemaphoreType.DMA((groups - 1,)),
            pltpu.SemaphoreType.DMA((5, dp)),
            pltpu.SemaphoreType.DMA((5, dp)),
            pltpu.SemaphoreType.DMA((2, FETCHED)),
            pltpu.SemaphoreType.DMA((2, 2)),
            pltpu.SemaphoreType.DMA,
        ],
        compiler_params=pltpu.CompilerParams(
            collective_id=0, has_side_effects=True, vmem_limit_bytes=65400 << 10
        ),
        name="layer",
    )(labels, inputs, grad_out, *shards, b_qv, b_up, *(v.reshape(1, local) for v in vectors))


def finish_kernel(many, seq, result, grad_in, qkv, out, up, down, sums, place, *outs):
    i = pl.program_id(0)
    for n in range(many):
        toks = slice(n * seq, (n + 1) * seq)
        turn = place[i * many + n, 1]
        outs[0][:, toks] = pltpu.roll(result[n].astype(f32), turn, 1).astype(bf16)
        outs[1][:, toks] = pltpu.roll(grad_in[n], turn, 1)

    @pl.when(i == 0)
    def _():
        local = result.shape[1]
        for target, source in zip(outs[2:6], (qkv, out, up, down)):
            target[...] = source[...]
        for n in range(6):
            outs[6 + n][...] = sums[n : n + 1, :local]
        outs[12][...] = sums[6:7, :]
        outs[13][...] = sums[7:8, : 2 * local]


def finish(result, grad_in, *small):
    rows, local, seq = result.shape
    units = small[4].shape[1]
    many = math.gcd(rows, FINISH_ROWS)
    raw = pl.BlockSpec((many, local, seq), lambda i: (i, 0, 0))
    block = pl.BlockSpec((local, many * seq), lambda i: (0, i))
    vmem = pl.BlockSpec(memory_space=pltpu.VMEM)
    shapes = (*(s.shape for s in small[:4]), *((1, local),) * 6, (1, units), (1, 2 * local))
    return pl.pallas_call(
        functools.partial(finish_kernel, many, seq),
        grid=(rows // many,),
        out_shape=(
            jax.ShapeDtypeStruct((local, rows * seq), bf16),
            jax.ShapeDtypeStruct((local, rows * seq), f32),
            *(jax.ShapeDtypeStruct(s, f32) for s in shapes),
        ),
        in_specs=[raw, raw, *[vmem] * 5, pl.BlockSpec(memory_space=pltpu.SMEM)],
        out_specs=(block, block, *(vmem,) * len(shapes)),
        compiler_params=pltpu.CompilerParams(vmem_limit_bytes=60 << 20),
        name="finish",
    )(result, grad_in, *small)


def per_device(
    inputs,
    labels,
    w_qkv,
    b_qv,
    w_out,
    b_out,
    gain_one,
    shift_one,
    w_up,
    b_up,
    down_weight,
    down_bias,
    gain_two,
    shift_two,
    grad_out,
):
    shards = (w_qkv[0], w_out, w_up[0], down_weight[0])
    vectors = (b_out, gain_one, shift_one, down_bias, gain_two, shift_two)
    raw = run_layer(labels, inputs, grad_out, shards, b_qv, b_up, *vectors)
    result, input_grad, qkv, out, up, down, *sums = finish(*raw)
    flat = [s.reshape(-1) for s in sums]
    return (
        result,
        input_grad,
        qkv[None],
        sums[7],
        out,
        flat[0],
        flat[1],
        flat[2],
        up[None],
        sums[6],
        down[None],
        sums[3],
        flat[4],
        flat[5],
    )


def solution(mesh):
    placed = (
        P("group", "dp"),
        P("dp", None),
        P("group", "dp", None),
        P("group", None),
        P("dp", "group"),
        P("group"),
        P("group"),
        P("group"),
        P("group", "dp", None),
        P("group", None),
        P("group", "dp", None),
        P("group", None),
        P("group"),
        P("group"),
        P("group", "dp"),
    )
    return jax.shard_map(
        per_device,
        mesh=mesh,
        in_specs=placed,
        out_specs=(
            P("group", "dp"),
            P("group", "dp"),
            P("group", "dp", None),
            P("group", None),
            P("dp", "group"),
            P("group"),
            P("group"),
            P("group"),
            P("group", "dp", None),
            P("group", None),
            P("group", "dp", None),
            P("group", None),
            P("group"),
            P("group"),
        ),
        check_vma=False,
    )
```
